256 devices in a mesh: ctx: 128 (over x, y, z), kvh: 2 (over core).
Axes of the slice: x: 4, y: 4, z: 8, core: 2. Of those that a mesh axis runs over, the one named last changes fastest.
Arguments:
- queries: bfloat16 [32768, 4096], P('ctx', 'kvh'), may hold values from -5 to 5
- keys: bfloat16 [32768, 1024], P('ctx', 'kvh'), may hold values from -5 to 5
- values: bfloat16 [32768, 1024], P('ctx', 'kvh'), may hold values from -5 to 5
- segment_ids: int32 [32768], P('ctx'), may hold values from 0 to 255, never falling along the last dimension, each value on 1 to 4096 neighbouring positions
Outputs:
- attended: bfloat16 [32768, 4096], P(('ctx', 'kvh'))
The draws below stay inside these ranges and needn't reach their ends.
Inputs may be any that keep to these rules, and one draw needn't show every extreme that they name: `segment_ids`: every document has at most 4096 tokens.
All inputs are finite; a program needn't handle non-finite values.
Results may differ from the reference program's by a relative error of at most 0.005.
Values may be sent and summed in bfloat16 or wider, within the bound.
A program may use at most 128 MiB of HBM per device.

```python
import math
import jax
import jax.numpy as jnp
import numpy as np
from jax import lax

QUERY_HEADS = 32
KEY_VALUE_HEADS = 8
HEAD_DIMENSION = 128
PACKED_TOKENS = 32768
DOC_MOST = 4096
DOCS = 256


def draw_queries(key, part):
    key = jax.random.fold_in(key, 1)
    initial_sample = jnp.clip(jax.random.normal(key, (PACKED_TOKENS, QUERY_HEADS * HEAD_DIMENSION), jnp.float32), -5.0, 5.0)
    return initial_sample.astype(jnp.bfloat16)


def draw_keys(key, part):
    key = jax.random.fold_in(key, 2)
    initial_sample = jnp.clip(jax.random.normal(key, (PACKED_TOKENS, KEY_VALUE_HEADS * HEAD_DIMENSION), jnp.float32), -5.0, 5.0)
    return initial_sample.astype(jnp.bfloat16)


def block_levels(stream_key, extent, shards, least, top_value):
    def one(dim, shards_of):
        heights = jax.random.uniform(jax.random.fold_in(jax.random.fold_in(stream_key, 6), dim), (shards_of,), jnp.float32, least / len(shards), top_value / len(shards))
        return jnp.repeat(jnp.exp(heights), extent[dim] // shards_of).reshape((-1,) + (1,) * (len(extent) - dim - 1))

    level = one(*shards[0])
    for cut in shards[1:]:
        level = level * one(*cut)
    return level


def profile(amount, total, reach, lean):
    portions = [(1 << 20) // math.isqrt(grade ** lean) + 1 for grade in range(2, amount + 1)]
    spare, holding = total - reach - (amount - 1), [1] * (amount - 1)
    while spare > 0:
        candidates = [i for i in range(amount - 1) if holding[i] < reach]
        pool, remaining = sum([portions[i] for i in candidates]), spare
        for i in candidates:
            more = min(reach - holding[i], max(1, remaining * portions[i] // pool), spare)
            holding[i] = holding[i] + more
            spare = spare - more
    return np.array([reach] + holding)


def uneven_parts(key, number_of, total, reach, skew):
    if number_of == 2:
        one = jax.random.randint(key, (), max(1, total - reach), min(reach, total - 1) + 1)
        return jnp.stack([one, total - one])
    tallies = jnp.asarray(profile(number_of, total, reach, skew), jnp.int32)
    twos = (number_of - 1) // 2
    donor, receiver = tallies[1:1 + 2 * twos:2], tallies[2:2 + 2 * twos:2]
    room = jnp.minimum(donor - 1, reach - receiver)
    passed = jax.random.randint(jax.random.fold_in(key, 1), (twos,), 0, 1 << 20) % (room + 1)
    tallies = tallies.at[1:1 + 2 * twos:2].set(donor - passed).at[2:2 + 2 * twos:2].set(receiver + passed)
    return tallies[jax.random.permutation(jax.random.fold_in(key, 2), number_of)]


def normal_values(key, shape, deviation, reach, cuts=(), kind=jnp.bfloat16):
    values = deviation * jax.random.normal(key, shape, jnp.float32)
    if cuts:
        values = values * block_levels(key, shape, cuts, -0.22, 0.18)
    return jnp.clip(values, -reach, reach).astype(kind)


def setup_inputs(seed: int = 0) -> dict:
    streams_of = jax.random.split(jax.random.key(seed), 5)
    queries = draw_queries(jax.random.fold_in(streams_of[4], 71), 0)
    keys = draw_keys(jax.random.fold_in(streams_of[4], 71), 0)
    values = normal_values(streams_of[2], (PACKED_TOKENS, KEY_VALUE_HEADS * HEAD_DIMENSION), 1.0, 5.0, ((0, 128), (1, 2)))
    segment_ids = jnp.searchsorted(jnp.cumsum(uneven_parts(streams_of[3], DOCS, PACKED_TOKENS, DOC_MOST, 2)), jnp.arange(PACKED_TOKENS), side="right").astype(jnp.int32)
    return dict(queries=queries, keys=keys, values=values, segment_ids=segment_ids)


def reference(queries, keys, values, segment_ids):
    query_group = QUERY_HEADS // KEY_VALUE_HEADS
    scale_factor = HEAD_DIMENSION ** -0.5
    rows_per_block = 256
    key_width = DOC_MOST + rows_per_block
    key_padding = jnp.pad(keys, ((DOC_MOST, 0), (0, 0)))
    value_padding = jnp.pad(values, ((DOC_MOST, 0), (0, 0)))
    seg_pad = jnp.concatenate([jnp.full((DOC_MOST,), -1, jnp.int32), segment_ids.astype(jnp.int32)])

    def one_block(start_offset):
        query_block = lax.dynamic_slice_in_dim(queries, start_offset, rows_per_block, 0).astype(jnp.float32).reshape(rows_per_block, KEY_VALUE_HEADS, query_group, HEAD_DIMENSION)
        key_block = lax.dynamic_slice_in_dim(key_padding, start_offset, key_width, 0).astype(jnp.float32).reshape(key_width, KEY_VALUE_HEADS, HEAD_DIMENSION)
        value_block = lax.dynamic_slice_in_dim(value_padding, start_offset, key_width, 0).astype(jnp.float32).reshape(key_width, KEY_VALUE_HEADS, HEAD_DIMENSION)
        key_seg = lax.dynamic_slice_in_dim(seg_pad, start_offset, key_width, 0)
        query_seg = lax.dynamic_slice_in_dim(segment_ids.astype(jnp.int32), start_offset, rows_per_block, 0)
        query_pos = start_offset + jnp.arange(rows_per_block, dtype=jnp.int32)
        key_pos = start_offset - DOC_MOST + jnp.arange(key_width, dtype=jnp.int32)
        scores = jnp.einsum('tgqd,sgd->tgqs', query_block, key_block) * scale_factor
        allowed = (query_seg[:, None] == key_seg[None, :]) & (key_pos[None, :] <= query_pos[:, None])
        scores = jnp.where(allowed[:, None, None, :], scores, -jnp.inf)
        row_peak = jnp.max(scores, axis=-1, keepdims=True)
        weights = jnp.exp(scores - row_peak)
        denominator = jnp.sum(weights, axis=-1)
        rounded = lax.optimization_barrier(weights.astype(jnp.bfloat16)).astype(jnp.float32)
        mixed = jnp.einsum('tgqs,sgd->tgqd', rounded, value_block) / denominator[..., None]
        return mixed.astype(jnp.bfloat16).reshape(rows_per_block, QUERY_HEADS * HEAD_DIMENSION)

    starts = jnp.arange(PACKED_TOKENS // rows_per_block, dtype=jnp.int32) * rows_per_block
    return lax.map(one_block, starts).reshape(PACKED_TOKENS, QUERY_HEADS * HEAD_DIMENSION)
```

```python
import jax
import jax.numpy as jnp
from jax import lax
from jax.experimental import pallas as pl
from jax.experimental.pallas import tpu as pltpu
from jax.sharding import PartitionSpec as P

NX, NY, NZ = 4, 4, 8
TOK = 256
DIM = 128
GROUP = 4
BACK = 2
ROWS = NY + BACK
SLOTS = ROWS * NZ
SLOT_ROWS = 2 * TOK + 16
LANES = GROUP * TOK
NEG = -1e30
FAR_ID = 512.0
SCALE = 1.4426950408889634 * DIM ** -0.5


def place():
    me = lax.axis_index("ctx")
    return me, me // (NY * NZ), (me // NZ) % NY, me % NZ


def index_of(x, y, z):
    return (x * NY + y) * NZ + z


def remote(src, dst, send, recv, device):
    return pltpu.make_async_remote_copy(src_ref=src, dst_ref=dst, send_sem=send, recv_sem=recv,
                                        device_id=device, device_id_type=pl.DeviceIdType.MESH)


def attention_kernel(q_ref, k_ref, v_ref, seg_ref, out_ref, q_buf, v_buf, seg_buf, vt_buf, qt_buf,
                     kv, qt, qe, acc, peak, first, lead, o_buf, load_sem,
                     y_send, y_recv, q_send, q_recv, z_send, z_recv, x_send, x_recv, o_send, o_recv):
    me, x, y, z = place()
    core = lax.axis_index("kvh")
    half = NZ // 2

    def dev(x_, y_, z_):
        return (index_of(x_, y_, z_), core)

    y_peers = [lax.rem(y + d, NY) for d in range(1, NY)]
    z_next, z_prev = lax.rem(z + 1, NZ), lax.rem(z + NZ - 1, NZ)
    x_next, x_prev = lax.rem(x + 1, NX), lax.rem(x + NX - 1, NX)
    barrier = pltpu.get_barrier_semaphore()
    friends = ([dev(x, p, z) for p in y_peers] + [(index_of(x, p, z), 1 - core) for p in [y] + y_peers]
               + [dev(x, y, z_next), dev(x, y, z_prev), dev(x_next, y, z), dev(x_prev, y, z)])
    for friend in friends:
        pl.semaphore_signal(barrier, inc=1, device_id=friend, device_id_type=pl.DeviceIdType.MESH)
    load_v = pltpu.make_async_copy(v_ref, v_buf, load_sem.at[0])
    load_q = pltpu.make_async_copy(q_ref, q_buf, load_sem.at[1])
    load_v.start()
    load_q.start()

    @pl.when(x == 0)
    def _():
        def blank(at, _):
            kv[at, :2 * TOK, :] = jnp.zeros((2 * TOK, DIM), jnp.bfloat16)
            kv[at, 2 * TOK:, :] = jnp.full((16, DIM), -1.0, jnp.bfloat16)
            return 0

        lax.fori_loop(0, BACK * NZ, blank, 0)

    ids = seg_ref[...].astype(jnp.float32)
    line = lax.broadcasted_iota(jnp.int32, (16, 128), 0)
    ids = jnp.where(line == 0, ids[0:1], jnp.where(line == 1, ids[1:2], FAR_ID))
    seg_buf[...] = ids.astype(jnp.bfloat16)
    load_v.wait()
    for p in range(NY):
        turned = v_buf[:, p * DIM:(p + 1) * DIM].T
        vt_buf[p, :DIM, :] = turned[:, :DIM]
        vt_buf[p, DIM:, :] = turned[:, DIM:]
    pl.semaphore_wait(barrier, len(friends))

    def slot(row, shift):
        return (BACK + row) * NZ + lax.rem(z + shift + NZ, NZ)

    def head_cols(p):
        return pl.ds(pl.multiple_of(p * DIM, DIM), DIM)

    mine = (BACK + y) * NZ + z
    sent = []
    for n, p in enumerate(y_peers):
        for i, (src, lo, rows) in enumerate(((k_ref.at[:, head_cols(p)], 0, TOK), (vt_buf.at[p], TOK, TOK),
                                             (seg_buf, 2 * TOK, 16))):
            copy = remote(src, kv.at[mine, pl.ds(lo, rows)], y_send.at[n, i], y_recv.at[y], dev(x, p, z))
            copy.start()
            sent.append(copy)
    pltpu.make_async_copy(k_ref.at[:, head_cols(y)], kv.at[mine, pl.ds(0, TOK)], y_recv.at[y]).start()
    pltpu.make_async_copy(vt_buf.at[y], kv.at[mine, pl.ds(TOK, TOK)], y_recv.at[y]).start()
    pltpu.make_async_copy(seg_buf, kv.at[mine, pl.ds(2 * TOK, 16)], y_recv.at[y]).start()
    load_q.wait()
    for p in range(NY):
        for g in range(GROUP):
            h = p * GROUP + g
            qt_buf[p, :, g * TOK:(g + 1) * TOK] = q_buf[:, h * DIM:(h + 1) * DIM].T

    def shift_of(way, step):
        return step * (2 * way - 1)

    def z_copy(way, row, step):
        at = kv.at[slot(row, shift_of(way, step - 1))]
        neighbour = jnp.where(way == 0, z_next, z_prev)
        return remote(at, at, z_send.at[way, row, step - 1], z_recv.at[way, row, step - 1], dev(x, y, neighbour))

    def x_copy(row, way, step):
        shift = shift_of(way, step)
        return remote(kv.at[slot(row, shift)], kv.at[slot(row - NY, shift)], x_send.at[row - NY + BACK, way, step],
                      x_recv.at[row - NY + BACK, way, step], dev(x_next, y, z))

    def last_way(row):
        return lax.rem(row + 1, 2)

    def pass_on(way, row, step):
        @pl.when((step < half - 1) | ((step == half - 1) & (way == last_way(row))))
        def _():
            z_copy(way, row, step + 1).start()

        @pl.when((row >= NY - BACK) & (x < NX - 1))
        def _():
            x_copy(row, way, step).start()

    for row in (3, 2, 1, 0):
        at = kv.at[slot(row, 0)]
        pltpu.make_async_copy(at, at, y_recv.at[row]).wait()
        z_copy(0, row, 1).start()
        z_copy(1, row, 1).start()
        if row >= NY - BACK:
            @pl.when(x < NX - 1)
            def _():
                x_copy(row, 0, 0).start()
    asked = []
    for n, p in enumerate(y_peers):
        copy = remote(qt_buf.at[p], qt.at[y], q_send.at[n], q_recv.at[n], dev(x, p, z))
        copy.start()
        asked.append(copy)
    own_q = pltpu.make_async_copy(qt_buf.at[y], qt.at[y], q_send.at[NY - 1])
    own_q.start()

    def first_step(j, _):
        row, way = NY - 1 - j // 2, j % 2
        z_copy(way, row, 1).wait_recv()
        pass_on(way, row, 1)
        return 0

    lax.fori_loop(0, 2 * NY, first_step, 0)
    for copy in asked:
        copy.wait_recv()
    own_q.wait()

    def spread(b, _):
        scaled = qt[b].astype(jnp.float32) * SCALE
        high = scaled.astype(jnp.bfloat16)
        qe[b, :DIM, :] = high
        qe[b, DIM:, :] = (scaled - high.astype(jnp.float32)).astype(jnp.bfloat16)
        return 0

    lax.fori_loop(0, NY, spread, 0)
    key = lax.broadcasted_iota(jnp.int32, (TOK, TOK), 0)
    token = lax.broadcasted_iota(jnp.int32, (TOK, TOK), 1)

    def block_of(at):
        k = kv[at, :TOK, :]
        return jnp.concatenate([k, k], axis=1), [kv[at, TOK:TOK + DIM, :], kv[at, TOK + DIM:2 * TOK, :]]

    def bias_of(at, b):
        there = kv[at, 2 * TOK:, :].astype(jnp.float32)
        less = jnp.where(there < first[b, 0:1, :], 1.0, 0.0)
        count = jnp.sum(jnp.sum(less, axis=0, keepdims=True), axis=1, keepdims=True)
        bound = (lead[b, 0:1, :] + count).astype(jnp.int32)
        return jnp.where(key >= bound, 0.0, NEG)

    def chains(jobs):
        todo = []
        for b, slots, biases, going in jobs:
            loaded = [block_of(at) for at in slots]
            vt = jnp.concatenate([part for _, parts in loaded for part in parts], axis=1)
            vt = jnp.concatenate([vt, jnp.ones((16, vt.shape[1]), jnp.bfloat16)], axis=0)
            for g in range(GROUP):
                todo.append((b, slice(g * TOK, (g + 1) * TOK), [k for k, _ in loaded], biases, vt, going))
        count = len(todo)
        scores, weights = [None] * count, [None] * count
        for i in range(count + 2):
            if i < count:
                b, cols, ks, biases, _, _ = todo[i]
                q = qe[b, :, cols]
                scores[i] = [jnp.dot(k, q, preferred_element_type=jnp.float32) for k in ks]
            if 0 <= i - 1 < count:
                b, cols, _, biases, _, going = todo[i - 1]
                t = [one + bias for one, bias in zip(scores[i - 1], biases)]
                top = t[0]
                for one in t[1:]:
                    top = jnp.maximum(top, one)
                new = jnp.max(top, axis=0, keepdims=True)
                fade = None
                if going:
                    old = peak[b, 0:1, cols]
                    new = jnp.maximum(old, new)
                    fade = jnp.exp2(old - new)
                peak[b, 0:1, cols] = new
                w = jnp.concatenate([jnp.exp2(one - new).astype(jnp.bfloat16) for one in t], axis=0)
                scores[i - 1] = None
                weights[i - 1] = (w, fade)
            if i >= 2:
                b, cols, _, _, vt, going = todo[i - 2]
                w, fade = weights[i - 2]
                o = jnp.dot(vt, w, preferred_element_type=jnp.float32)
                acc[b, :, cols] = acc[b, :, cols] * fade + o if going else o
                weights[i - 2] = None

    def wait_x(row, way, step):
        @pl.when(x > 0)
        def _():
            x_copy(row, way, step).wait_recv()

    for row in (NY - 1, NY - 2):
        wait_x(row, 0, 0)

    def own_work(j, _):
        b = NY - 1 - j
        at = slot(b, 0)
        own = kv[at, 2 * TOK:, :].astype(jnp.float32)
        row = jnp.concatenate([own[0:1], own[1:2]], axis=1)
        rows = jnp.broadcast_to(row, (TOK, TOK))
        begin = row[:, 0:1]
        first[b] = jnp.broadcast_to(begin, (8, 128))
        lead[b] = jnp.broadcast_to(jnp.where(row == begin, 0.0, 4096.0), (8, TOK))
        allowed = (rows == rows.T) & (key <= token)
        slots = [at, slot(b - 1, 0), slot(b - 2, 0)]
        chains([(b, slots, [jnp.where(allowed, 0.0, NEG)] + [bias_of(one, b) for one in slots[1:]], False)])
        return 0

    lax.fori_loop(0, NY, own_work, 0)

    def pair_work(pair, way, step):
        shift = shift_of(way, step)
        there = lax.rem(z + shift + NZ, NZ)
        jobs = []
        for i in (1, 0):
            b = 2 * pair + i
            slots = [slot(b - 1, shift), slot(jnp.where(there < z, b, b - 2), shift)]
            jobs.append((b, slots, [bias_of(at, b) for at in slots], True))
        chains(jobs)

    def later_step(step, _):
        def arrive(j, _):
            row, way = NY - 1 - j // 2, j % 2

            @pl.when((step < half) | (way == last_way(row)))
            def _():
                z_copy(way, row, step).wait_recv()
                pass_on(way, row, step)
            return 0

        lax.fori_loop(0, 2 * NY, arrive, 0)

        def catch_up(j, _):
            @pl.when(j >= 2)
            def _():
                for row in (NY - 1, NY - 2):
                    wait_x(row, j % 2, step - 1)
            pair_work(1 - j // 2, j % 2, step - 1)
            return 0

        lax.fori_loop(0, 4, catch_up, 0)
        return 0

    lax.fori_loop(2, half + 1, later_step, 0)

    rows = TOK // 2
    wide = GROUP * DIM
    cols = out_ref.at[:, pl.ds(pl.multiple_of((core * NY + y) * wide, wide), wide)]

    def part(b, c):
        return o_buf.at[b, pl.ds(pl.multiple_of(c * rows, rows), rows)]

    def over(b):
        return remote(part(b, 1 - core), cols, o_send.at[b, 1], o_recv.at[y, 1], (index_of(x, b, z), 1 - core))

    def along(b):
        return remote(part(b, core), cols, o_send.at[b, 0], o_recv.at[y, 0], (index_of(x, b, z), core))

    def stay(b):
        return pltpu.make_async_copy(part(b, core), cols, o_recv.at[y, 0])

    def send_back(b):
        mixed = acc[b, :DIM, :] / acc[b, DIM:DIM + 1, :]
        for g in range(GROUP):
            o_buf[b, :, g * DIM:(g + 1) * DIM] = mixed[:, g * TOK:(g + 1) * TOK].T.astype(jnp.bfloat16)
        over(b).start()

        @pl.when(b != y)
        def _():
            along(b).start()

        @pl.when(b == y)
        def _():
            stay(b).start()

    def finish(j, _):
        @pl.when(j == 1)
        def _():
            for row in (NY - 1, NY - 2):
                wait_x(row, last_way(row), half)
        pair_work(1 - j, 0, half)
        for i in (1, 0):
            send_back(2 * (1 - j) + i)
        return 0

    lax.fori_loop(0, 2, finish, 0)

    for copy in sent + asked:
        copy.wait_send()

    def z_drain(j, _):
        row, way, step = j // (2 * half), (j // half) % 2, 1 + j % half

        @pl.when((step < half) | (way == last_way(row)))
        def _():
            z_copy(way, row, step).wait_send()
        return 0

    lax.fori_loop(0, 2 * NY * half, z_drain, 0)

    def x_drain(j, _):
        row, way, step = NY - 1 - j // (2 * (half + 1)), (j // (half + 1)) % 2, j % (half + 1)
        sent_one = jnp.where(step == 0, way == 0, (step < half) | (way == last_way(row)))

        @pl.when(sent_one & (x < NX - 1))
        def _():
            x_copy(row, way, step).wait_send()
        return 0

    lax.fori_loop(0, 2 * BACK * (half + 1), x_drain, 0)
    for b in range(NY):
        over(b).wait_send()

        @pl.when(b != y)
        def _():
            along(b).wait_send()
        for e in range(2):
            pltpu.make_async_copy(part(b, core), cols, o_recv.at[b, e]).wait()


def per_device(queries, keys, values, segment_ids):
    any_spec = pl.BlockSpec(memory_space=pl.ANY)
    vmem_spec = pl.BlockSpec(memory_space=pltpu.VMEM)
    dma = pltpu.SemaphoreType.DMA
    bf16, f32 = jnp.bfloat16, jnp.float32
    half = NZ // 2
    return pl.pallas_call(
        attention_kernel,
        out_shape=jax.ShapeDtypeStruct((TOK // 2, 2 * NY * GROUP * DIM), bf16),
        in_specs=[any_spec, any_spec, any_spec, vmem_spec],
        out_specs=any_spec,
        scratch_shapes=[
            pltpu.VMEM(queries.shape, bf16), pltpu.VMEM(values.shape, bf16), pltpu.VMEM((16, 128), bf16),
            pltpu.VMEM((NY, 2 * DIM, TOK // 2), bf16), pltpu.VMEM((NY, DIM, LANES), bf16),
            pltpu.VMEM((SLOTS, SLOT_ROWS, DIM), bf16), pltpu.VMEM((NY, DIM, LANES), bf16),
            pltpu.VMEM((NY, 2 * DIM, LANES), bf16), pltpu.VMEM((NY, DIM + 16, LANES), f32), pltpu.VMEM((NY, 8, LANES), f32),
            pltpu.VMEM((NY, 8, 128), f32), pltpu.VMEM((NY, 8, TOK), f32), pltpu.VMEM((NY, TOK, GROUP * DIM), bf16),
            dma((2,)), dma((NY - 1, 3)), dma((NY,)), dma((NY,)), dma((NY - 1,)),
            dma((2, NY, half)), dma((2, NY, half)), dma((BACK, 2, half + 1)), dma((BACK, 2, half + 1)),
            dma((NY, 2)), dma((NY, 2))],
        compiler_params=pltpu.CompilerParams(collective_id=0, has_side_effects=True,
                                             vmem_limit_bytes=60 * 1024 * 1024),
        name="attention",
    )(queries, keys, values, segment_ids.reshape(2, 128))


def solution(mesh):
    return jax.shard_map(
        per_device,
        mesh=mesh,
        in_specs=(P("ctx", "kvh"), P("ctx", "kvh"), P("ctx", "kvh"), P("ctx")),
        out_specs=P(("ctx", "kvh"), None),
        check_vma=False,
    )
```

```python
import jax
import jax.numpy as jnp
from jax import lax
from jax.experimental import pallas as pl
from jax.experimental.pallas import tpu as pltpu
from jax.sharding import PartitionSpec as P

NX, NY, NZ = 4, 4, 8
TOK = 256
DIM = 128
GROUP = 4
BACK = 2
ROWS = NY + BACK
SLOTS = ROWS * NZ
SLOT_ROWS = 2 * TOK + 16
LANES = GROUP * TOK
NEG = -1e30
FAR_ID = 512.0
SCALE = 1.4426950408889634 * DIM ** -0.5


def place():
    me = lax.axis_index("ctx")
    return me, me // (NY * NZ), (me // NZ) % NY, me % NZ


def index_of(x, y, z):
    return (x * NY + y) * NZ + z


def remote(src, dst, send, recv, device):
    return pltpu.make_async_remote_copy(src_ref=src, dst_ref=dst, send_sem=send, recv_sem=recv,
                                        device_id=device, device_id_type=pl.DeviceIdType.MESH)


def attention_kernel(q_ref, k_ref, v_ref, seg_ref, out_ref, q_buf, v_buf, seg_buf, vt_buf, qt_buf,
                     kv, qe, acc, peak, first, o_buf, load_sem,
                     y_send, y_recv, q_send, q_recv, z_send, z_recv, x_send, x_recv, o_send, o_recv):
    me, x, y, z = place()
    core = lax.axis_index("kvh")
    half = NZ // 2

    def dev(x_, y_, z_):
        return (index_of(x_, y_, z_), core)

    y_peers = [lax.rem(y + d, NY) for d in range(1, NY)]
    z_next, z_prev = lax.rem(z + 1, NZ), lax.rem(z + NZ - 1, NZ)
    x_next, x_prev = lax.rem(x + 1, NX), lax.rem(x + NX - 1, NX)
    barrier = pltpu.get_barrier_semaphore()
    friends = ([dev(x, p, z) for p in y_peers] + [(index_of(x, p, z), 1 - core) for p in [y] + y_peers]
               + [dev(x, y, z_next), dev(x, y, z_prev), dev(x_next, y, z), dev(x_prev, y, z)])
    for friend in friends:
        pl.semaphore_signal(barrier, inc=1, device_id=friend, device_id_type=pl.DeviceIdType.MESH)
    load_v = pltpu.make_async_copy(v_ref, v_buf, load_sem.at[0])
    load_q = pltpu.make_async_copy(q_ref, q_buf, load_sem.at[1])
    load_v.start()
    load_q.start()

    @pl.when(x == 0)
    def _():
        def blank(at, _):
            kv[at, :2 * TOK, :] = jnp.zeros((2 * TOK, DIM), jnp.bfloat16)
            kv[at, 2 * TOK:, :] = jnp.full((16, DIM), -1.0, jnp.bfloat16)
            return 0

        lax.fori_loop(0, BACK * NZ, blank, 0)

    ids = seg_ref[...].astype(jnp.float32)
    line = lax.broadcasted_iota(jnp.int32, (16, 128), 0)
    ids = jnp.where(line == 0, ids[0:1], jnp.where(line == 1, ids[1:2], FAR_ID))
    seg_buf[...] = ids.astype(jnp.bfloat16)
    load_v.wait()
    for p in range(NY):
        turned = v_buf[:, p * DIM:(p + 1) * DIM].T
        vt_buf[p, :DIM, :] = turned[:, :DIM]
        vt_buf[p, DIM:, :] = turned[:, DIM:]
    pl.semaphore_wait(barrier, len(friends))

    def slot(row, shift):
        return (BACK + row) * NZ + lax.rem(z + shift + NZ, NZ)

    def head_cols(p):
        return pl.ds(pl.multiple_of(p * DIM, DIM), DIM)

    mine = (BACK + y) * NZ + z
    sent = []
    for n, p in enumerate(y_peers):
        for i, (src, lo, rows) in enumerate(((k_ref.at[:, head_cols(p)], 0, TOK), (vt_buf.at[p], TOK, TOK),
                                             (seg_buf, 2 * TOK, 16))):
            copy = remote(src, kv.at[mine, pl.ds(lo, rows)], y_send.at[n, i], y_recv.at[y], dev(x, p, z))
            copy.start()
            sent.append(copy)
    pltpu.make_async_copy(k_ref.at[:, head_cols(y)], kv.at[mine, pl.ds(0, TOK)], y_recv.at[y]).start()
    pltpu.make_async_copy(vt_buf.at[y], kv.at[mine, pl.ds(TOK, TOK)], y_recv.at[y]).start()
    pltpu.make_async_copy(seg_buf, kv.at[mine, pl.ds(2 * TOK, 16)], y_recv.at[y]).start()
    load_q.wait()
    for p in range(NY):
        for g in range(GROUP):
            h = p * GROUP + g
            qt_buf[p, :, g * TOK:(g + 1) * TOK] = q_buf[:, h * DIM:(h + 1) * DIM].T

    def shift_of(way, step):
        return step * (2 * way - 1)

    def z_copy(way, row, step):
        at = kv.at[slot(row, shift_of(way, step - 1))]
        neighbour = jnp.where(way == 0, z_next, z_prev)
        return remote(at, at, z_send.at[way, row, step - 1], z_recv.at[way, row, step - 1], dev(x, y, neighbour))

    def x_copy(row, way, step):
        shift = shift_of(way, step)
        return remote(kv.at[slot(row, shift)], kv.at[slot(row - NY, shift)], x_send.at[row - NY + BACK, way, step],
                      x_recv.at[row - NY + BACK, way, step], dev(x_next, y, z))

    def last_way(row):
        return lax.rem(row + 1, 2)

    def pass_on(way, row, step):
        @pl.when((step < half - 1) | ((step == half - 1) & (way == last_way(row))))
        def _():
            z_copy(way, row, step + 1).start()

        @pl.when((row >= NY - BACK) & (x < NX - 1))
        def _():
            x_copy(row, way, step).start()

    for row in (3, 2, 1, 0):
        at = kv.at[slot(row, 0)]
        pltpu.make_async_copy(at, at, y_recv.at[row]).wait()
        z_copy(0, row, 1).start()
        z_copy(1, row, 1).start()
        if row >= NY - BACK:
            @pl.when(x < NX - 1)
            def _():
                x_copy(row, 0, 0).start()
    asked = []
    for n, p in enumerate(y_peers):
        copy = remote(qt_buf.at[p], qe.at[y, pl.ds(0, DIM)], q_send.at[n], q_recv.at[n], dev(x, p, z))
        copy.start()
        asked.append(copy)
    own_q = pltpu.make_async_copy(qt_buf.at[y], qe.at[y, pl.ds(0, DIM)], q_send.at[NY - 1])
    own_q.start()

    def first_step(j, _):
        row, way = NY - 1 - j // 2, j % 2
        z_copy(way, row, 1).wait_recv()
        pass_on(way, row, 1)
        return 0

    lax.fori_loop(0, 2 * NY, first_step, 0)
    for copy in asked:
        copy.wait_recv()
    own_q.wait()

    key = lax.broadcasted_iota(jnp.int32, (TOK, TOK), 0)
    token = lax.broadcasted_iota(jnp.int32, (TOK, TOK), 1)

    lane = lax.broadcasted_iota(jnp.int32, (TOK, DIM), 1)
    line = lax.broadcasted_iota(jnp.int32, (TOK, DIM), 0)
    plain = jnp.where(lane == 1, 1.0, 0.0)

    def early_keys(at, b):
        there = kv[at, 2 * TOK:, :].astype(jnp.float32)
        less = jnp.where(there < first[b, 0:1, :], 1.0, 0.0)
        count = jnp.sum(jnp.sum(less, axis=0, keepdims=True), axis=1, keepdims=True).astype(jnp.int32)
        extra = jnp.where((lane == 0) & (line < count), NEG, plain).astype(jnp.bfloat16)
        return jnp.concatenate([kv[at, :TOK, :], extra], axis=1)

    def own_keys(at):
        return jnp.concatenate([kv[at, :TOK, :], jnp.zeros((TOK, DIM), jnp.bfloat16)], axis=1)

    def turned_values(slots):
        vt = jnp.concatenate([kv[at, lo:lo + DIM, :] for at in slots for lo in (TOK, TOK + DIM)], axis=1)
        return jnp.concatenate([vt, jnp.ones((16, vt.shape[1]), jnp.bfloat16)], axis=0)

    def chains(jobs):
        todo = [(b, slice(g * TOK, (g + 1) * TOK), keys, vt, bias, going)
                for b, keys, vt, bias, going in jobs for g in range(GROUP)]
        count = len(todo)
        scores, weights, done = [None] * count, [None] * count, []
        for i in range(count + 2):
            if i < count:
                b, cols, keys, _, _, _ = todo[i]
                scores[i] = jnp.dot(keys, qe[b, :, cols], preferred_element_type=jnp.float32)
            if 0 <= i - 1 < count:
                b, cols, _, _, bias, going = todo[i - 1]
                s = scores[i - 1]
                if bias is not None:
                    s = jnp.concatenate([s[:TOK] + bias, s[TOK:]], axis=0)
                new = jnp.max(s, axis=0, keepdims=True)
                fade = None
                if going:
                    old = peak[b, 0:1, cols]
                    new = jnp.maximum(old, new)
                    fade = jnp.exp2((old - new) * SCALE)
                weights[i - 1] = (jnp.exp2((s - new) * SCALE).astype(jnp.bfloat16), new, fade)
                scores[i - 1] = None
            if i >= 2:
                b, cols, _, vt, _, going = todo[i - 2]
                w, new, fade = weights[i - 2]
                done.append((b, cols, new, fade, jnp.dot(vt, w, preferred_element_type=jnp.float32)))
                weights[i - 2] = None
        for b, cols, new, fade, o in done:
            peak[b, 0:1, cols] = new
            acc[b, :, cols] = o if fade is None else acc[b, :, cols] * fade + o

    def wait_x(row, way, step):
        @pl.when(x > 0)
        def _():
            x_copy(row, way, step).wait_recv()

    for row in (NY - 1, NY - 2):
        wait_x(row, 0, 0)

    def own_work(j, _):
        jobs = []
        for i in (1, 0):
            b = NY - 2 - 2 * j + i
            at = slot(b, 0)
            own = kv[at, 2 * TOK:, :].astype(jnp.float32)
            row = jnp.concatenate([own[0:1], own[1:2]], axis=1)
            rows = jnp.broadcast_to(row, (TOK, TOK))
            begin = row[:, 0:1]
            first[b] = jnp.broadcast_to(begin, (8, 128))
            rest = jnp.concatenate([jnp.where(row == begin, 0.0, NEG)] * GROUP, axis=1)
            which = lax.broadcasted_iota(jnp.int32, (DIM, LANES), 0)
            qe[b, DIM:, :] = jnp.where(which == 0, 1.0, jnp.where(which == 1, rest, 0.0)).astype(jnp.bfloat16)
            bias = jnp.where((rows == rows.T) & (key <= token), 0.0, NEG)
            early = [slot(b - 1, 0), slot(b - 2, 0)]
            keys = jnp.concatenate([own_keys(at)] + [early_keys(one, b) for one in early], axis=0)
            jobs.append((b, keys, turned_values([at] + early), bias, False))
        chains(jobs)
        return 0

    lax.fori_loop(0, NY // 2, own_work, 0)

    def pair_work(pair, way, step):
        shift = shift_of(way, step)
        there = lax.rem(z + shift + NZ, NZ)
        jobs = []
        for i in (1, 0):
            b = 2 * pair + i
            slots = [slot(b - 1, shift), slot(jnp.where(there < z, b, b - 2), shift)]
            keys = jnp.concatenate([early_keys(at, b) for at in slots], axis=0)
            jobs.append((b, keys, turned_values(slots), None, True))
        chains(jobs)

    def later_step(step, _):
        def arrive(j, _):
            row, way = NY - 1 - j // 2, j % 2

            @pl.when((step < half) | (way == last_way(row)))
            def _():
                z_copy(way, row, step).wait_recv()
                pass_on(way, row, step)
            return 0

        lax.fori_loop(0, 2 * NY, arrive, 0)

        def catch_up(j, _):
            @pl.when(j >= 2)
            def _():
                for row in (NY - 1, NY - 2):
                    wait_x(row, j % 2, step - 1)
            pair_work(1 - j // 2, j % 2, step - 1)
            return 0

        lax.fori_loop(0, 4, catch_up, 0)
        return 0

    lax.fori_loop(2, half + 1, later_step, 0)

    rows = TOK // 2
    wide = GROUP * DIM
    cols = out_ref.at[:, pl.ds(pl.multiple_of((core * NY + y) * wide, wide), wide)]

    def part(b, c):
        return o_buf.at[b, pl.ds(pl.multiple_of(c * rows, rows), rows)]

    def over(b):
        return remote(part(b, 1 - core), cols, o_send.at[b, 1], o_recv.at[y, 1], (index_of(x, b, z), 1 - core))

    def along(b):
        return remote(part(b, core), cols, o_send.at[b, 0], o_recv.at[y, 0], (index_of(x, b, z), core))

    def stay(b):
        return pltpu.make_async_copy(part(b, core), cols, o_recv.at[y, 0])

    def send_back(b):
        mixed = acc[b, :DIM, :] / acc[b, DIM:DIM + 1, :]
        for g in range(GROUP):
            o_buf[b, :, g * DIM:(g + 1) * DIM] = mixed[:, g * TOK:(g + 1) * TOK].T.astype(jnp.bfloat16)
        over(b).start()

        @pl.when(b != y)
        def _():
            along(b).start()

        @pl.when(b == y)
        def _():
            stay(b).start()

    def finish(j, _):
        @pl.when(j == 1)
        def _():
            for row in (NY - 1, NY - 2):
                wait_x(row, last_way(row), half)
        pair_work(1 - j, 0, half)
        for i in (1, 0):
            send_back(2 * (1 - j) + i)
        return 0

    lax.fori_loop(0, 2, finish, 0)

    for copy in sent + asked:
        copy.wait_send()

    def z_drain(j, _):
        row, way, step = j // (2 * half), (j // half) % 2, 1 + j % half

        @pl.when((step < half) | (way == last_way(row)))
        def _():
            z_copy(way, row, step).wait_send()
        return 0

    lax.fori_loop(0, 2 * NY * half, z_drain, 0)

    def x_drain(j, _):
        row, way, step = NY - 1 - j // (2 * (half + 1)), (j // (half + 1)) % 2, j % (half + 1)
        sent_one = jnp.where(step == 0, way == 0, (step < half) | (way == last_way(row)))

        @pl.when(sent_one & (x < NX - 1))
        def _():
            x_copy(row, way, step).wait_send()
        return 0

    lax.fori_loop(0, 2 * BACK * (half + 1), x_drain, 0)
    for b in range(NY):
        over(b).wait_send()

        @pl.when(b != y)
        def _():
            along(b).wait_send()
        for e in range(2):
            pltpu.make_async_copy(part(b, core), cols, o_recv.at[b, e]).wait()


def per_device(queries, keys, values, segment_ids):
    any_spec = pl.BlockSpec(memory_space=pl.ANY)
    vmem_spec = pl.BlockSpec(memory_space=pltpu.VMEM)
    dma = pltpu.SemaphoreType.DMA
    bf16, f32 = jnp.bfloat16, jnp.float32
    half = NZ // 2
    return pl.pallas_call(
        attention_kernel,
        out_shape=jax.ShapeDtypeStruct((TOK // 2, 2 * NY * GROUP * DIM), bf16),
        in_specs=[any_spec, any_spec, any_spec, vmem_spec],
        out_specs=any_spec,
        scratch_shapes=[
            pltpu.VMEM(queries.shape, bf16), pltpu.VMEM(values.shape, bf16), pltpu.VMEM((16, 128), bf16),
            pltpu.VMEM((NY, 2 * DIM, TOK // 2), bf16), pltpu.VMEM((NY, DIM, LANES), bf16),
            pltpu.VMEM((SLOTS, SLOT_ROWS, DIM), bf16),
            pltpu.VMEM((NY, 2 * DIM, LANES), bf16), pltpu.VMEM((NY, DIM + 16, LANES), f32), pltpu.VMEM((NY, 8, LANES), f32),
            pltpu.VMEM((NY, 8, 128), f32), pltpu.VMEM((NY, TOK, GROUP * DIM), bf16),
            dma((2,)), dma((NY - 1, 3)), dma((NY,)), dma((NY,)), dma((NY - 1,)),
            dma((2, NY, half)), dma((2, NY, half)), dma((BACK, 2, half + 1)), dma((BACK, 2, half + 1)),
            dma((NY, 2)), dma((NY, 2))],
        compiler_params=pltpu.CompilerParams(collective_id=0, has_side_effects=True,
                                             vmem_limit_bytes=60 * 1024 * 1024),
        name="attention",
    )(queries, keys, values, segment_ids.reshape(2, 128))


def solution(mesh):
    return jax.shard_map(
        per_device,
        mesh=mesh,
        in_specs=(P("ctx", "kvh"), P("ctx", "kvh"), P("ctx", "kvh"), P("ctx")),
        out_specs=P(("ctx", "kvh"), None),
        check_vma=False,
    )
```

```python
import jax
import jax.numpy as jnp
from jax import lax
from jax.experimental import pallas as pl
from jax.experimental.pallas import tpu as pltpu
from jax.sharding import PartitionSpec as P

NX, NY, NZ = 4, 4, 8
TOK = 256
DIM = 128
GROUP = 4
BACK = 2
ROWS = NY + BACK
SLOTS = ROWS * NZ
SLOT_ROWS = 2 * TOK + 16
LANES = GROUP * TOK
NEG = -1e30
FAR_ID = 512.0
SCALE = 1.4426950408889634 * DIM ** -0.5


def place():
    me = lax.axis_index("ctx")
    return me, me // (NY * NZ), (me // NZ) % NY, me % NZ


def index_of(x, y, z):
    return (x * NY + y) * NZ + z


def remote(src, dst, send, recv, device):
    return pltpu.make_async_remote_copy(src_ref=src, dst_ref=dst, send_sem=send, recv_sem=recv,
                                        device_id=device, device_id_type=pl.DeviceIdType.MESH)


def attention_kernel(q_ref, k_ref, v_ref, seg_ref, out_ref, q_buf, v_buf, seg_in, seg_buf, vt_buf, qt_buf,
                     kv, qe, acc, peak, first, o_buf, load_sem,
                     y_send, y_recv, q_send, q_recv, z_send, z_recv, x_send, x_recv,
                     side_send, side_recv, o_send, o_recv):
    me, x, y, z = place()
    core = lax.axis_index("kvh")
    half = NZ // 2

    def dev(x_, y_, z_):
        return (index_of(x_, y_, z_), core)

    y_peers = [lax.rem(y + d, NY) for d in range(1, NY)]
    z_next, z_prev = lax.rem(z + 1, NZ), lax.rem(z + NZ - 1, NZ)
    x_next, x_prev = lax.rem(x + 1, NX), lax.rem(x + NX - 1, NX)
    barrier = pltpu.get_barrier_semaphore()
    friends = ([dev(x, p, z) for p in y_peers] + [(index_of(x, p, z), 1 - core) for p in [y] + y_peers]
               + [dev(x, y, z_next), dev(x, y, z_prev), dev(x_next, y, z), dev(x_prev, y, z)])
    for friend in friends:
        pl.semaphore_signal(barrier, inc=1, device_id=friend, device_id_type=pl.DeviceIdType.MESH)
    load_v = pltpu.make_async_copy(v_ref, v_buf, load_sem.at[0])
    load_q = pltpu.make_async_copy(q_ref, q_buf, load_sem.at[1])
    load_ids = pltpu.make_async_copy(seg_ref, seg_in, load_sem.at[2])
    load_ids.start()
    load_v.start()
    load_q.start()

    load_ids.wait()
    ids = seg_in[...].astype(jnp.float32)
    line = lax.broadcasted_iota(jnp.int32, (16, 128), 0)
    ids = jnp.where(line == 0, ids[0:1], jnp.where(line == 1, ids[1:2], FAR_ID))
    seg_buf[...] = ids.astype(jnp.bfloat16)
    def slot(row, shift):
        return (BACK + row) * NZ + lax.rem(z + shift + NZ, NZ)

    def head_cols(p):
        return pl.ds(pl.multiple_of(p * DIM, DIM), DIM)

    mine = (BACK + y) * NZ + z
    pltpu.make_async_copy(k_ref.at[:, head_cols(y)], kv.at[mine, pl.ds(0, TOK)], y_recv.at[y]).start()
    pltpu.make_async_copy(seg_buf, kv.at[mine, pl.ds(2 * TOK, 16)], y_recv.at[y]).start()
    load_v.wait()
    for p in range(NY):
        turned = v_buf[:, p * DIM:(p + 1) * DIM].T
        vt_buf[p, :DIM, :] = turned[:, :DIM]
        vt_buf[p, DIM:, :] = turned[:, DIM:]
    pltpu.make_async_copy(vt_buf.at[y], kv.at[mine, pl.ds(TOK, TOK)], y_recv.at[y]).start()
    pl.semaphore_wait(barrier, len(friends))
    sent = []
    for n, p in enumerate(y_peers):
        for i, (src, lo, rows) in enumerate(((k_ref.at[:, head_cols(p)], 0, TOK), (vt_buf.at[p], TOK, TOK),
                                             (seg_buf, 2 * TOK, 16))):
            copy = remote(src, kv.at[mine, pl.ds(lo, rows)], y_send.at[n, i], y_recv.at[y], dev(x, p, z))
            copy.start()
            sent.append(copy)

    def shift_of(way, step):
        return step * (2 * way - 1)

    def z_copy(way, row, step):
        at = kv.at[slot(row, shift_of(way, step - 1))]
        neighbour = jnp.where(way == 0, z_next, z_prev)
        return remote(at, at, z_send.at[way, row, step - 1], z_recv.at[way, row, step - 1], dev(x, y, neighbour))

    def x_copy(row, way, step):
        shift = shift_of(way, step)
        return remote(kv.at[slot(row, shift)], kv.at[slot(row - NY, shift)], x_send.at[row - NY + BACK, way, step],
                      x_recv.at[row - NY + BACK, way, step], dev(x_next, y, z))

    def last_way(row):
        return lax.rem(row + 1, 2)

    def row2_over_x(way, step):
        return (lax.rem(z + shift_of(way, step) + NZ, NZ) >= z) & (step != 1)

    def over_x(way, row, step):
        return (row == NY - 1) | ((row == NY - 2) & row2_over_x(way, step))

    def forward(way, row, step):
        @pl.when(over_x(way, row, step) & (x < NX - 1))
        def _():
            x_copy(row, way, step).start()

    def pass_on(way, row, step):
        @pl.when((step < half - 1) | ((step == half - 1) & (way == last_way(row))))
        def _():
            z_copy(way, row, step + 1).start()
        forward(way, row, step)

    def side_copy(way):
        at = kv.at[slot(-BACK, 0)]
        return remote(at, at, side_send.at[way], side_recv.at[way], dev(x, y, z_prev if way else z_next))

    def side_goes(way):
        return (x > 0) & ((z >= 1) if way else (z == NZ - 1))

    def side_comes(way):
        return (x > 0) & ((z < NZ - 1) if way else (z == 0))

    def row_of(i):
        return lax.rem(y + jnp.where(i == 0, 0, jnp.where(i == 1, 1, jnp.where(i == 2, NY - 1, 2))), NY)

    def first_sends(i, _):
        row = row_of(i)
        at = kv.at[slot(row, 0)]
        pltpu.make_async_copy(at, at, y_recv.at[row]).wait()
        z_copy(0, row, 1).start()
        z_copy(1, row, 1).start()
        forward(0, row, 0)
        return 0

    lax.fori_loop(0, NY, first_sends, 0)
    load_q.wait()
    for p in range(NY):
        for g in range(GROUP):
            h = p * GROUP + g
            qt_buf[p, :, g * TOK:(g + 1) * TOK] = q_buf[:, h * DIM:(h + 1) * DIM].T
    asked = []
    for n, p in enumerate(y_peers):
        copy = remote(qt_buf.at[p], qe.at[y, pl.ds(0, DIM)], q_send.at[n], q_recv.at[n], dev(x, p, z))
        copy.start()
        asked.append(copy)
    own_q = pltpu.make_async_copy(qt_buf.at[y], qe.at[y, pl.ds(0, DIM)], q_send.at[NY - 1])
    own_q.start()

    @pl.when(x == 0)
    def _():
        def blank(at, _):
            kv[at, :2 * TOK, :] = jnp.zeros((2 * TOK, DIM), jnp.bfloat16)
            kv[at, 2 * TOK:, :] = jnp.full((16, DIM), -1.0, jnp.bfloat16)
            return 0

        lax.fori_loop(0, BACK * NZ, blank, 0)

    def arrive(step):
        def one(j, _):
            row, way = row_of(j // 2), j % 2

            @pl.when((step < half) | (way == last_way(row)))
            def _():
                z_copy(way, row, step).wait_recv()
                pass_on(way, row, step)
            return 0

        lax.fori_loop(0, 2 * NY, one, 0)

    arrive(1)

    def wait_x(row, way, step):
        @pl.when(over_x(way, row, step) & (x > 0))
        def _():
            x_copy(row, way, step).wait_recv()

    for row in (NY - 1, NY - 2):
        wait_x(row, 0, 0)
    for way in range(2):
        @pl.when(side_goes(way))
        def _():
            side_copy(way).start()
    for copy in asked:
        copy.wait_recv()
    own_q.wait()

    key = lax.broadcasted_iota(jnp.int32, (TOK, TOK), 0)
    token = lax.broadcasted_iota(jnp.int32, (TOK, TOK), 1)

    lane = lax.broadcasted_iota(jnp.int32, (TOK, DIM), 1)
    line = lax.broadcasted_iota(jnp.int32, (TOK, DIM), 0)
    plain = jnp.where(lane == 1, 1.0, 0.0)

    def early_keys(at, b):
        there = kv[at, 2 * TOK:, :].astype(jnp.float32)
        less = jnp.where(there < first[b, 0:1, :], 1.0, 0.0)
        count = jnp.sum(jnp.sum(less, axis=0, keepdims=True), axis=1, keepdims=True).astype(jnp.int32)
        extra = jnp.where((lane == 0) & (line < count), NEG, plain).astype(jnp.bfloat16)
        return jnp.concatenate([kv[at, :TOK, :], extra], axis=1)

    def own_keys(at):
        return jnp.concatenate([kv[at, :TOK, :], jnp.zeros((TOK, DIM), jnp.bfloat16)], axis=1)

    def turned_values(slots):
        vt = jnp.concatenate([kv[at, lo:lo + DIM, :] for at in slots for lo in (TOK, TOK + DIM)], axis=1)
        return jnp.concatenate([vt, jnp.ones((16, vt.shape[1]), jnp.bfloat16)], axis=0)

    def chains(jobs):
        todo = [(b, slice(g * TOK, (g + 1) * TOK), keys, vt, bias, going)
                for b, keys, vt, bias, going in jobs for g in range(GROUP)]
        count = len(todo)
        scores, weights, done = [None] * count, [None] * count, []
        for i in range(count + 2):
            if i < count:
                b, cols, keys, _, _, _ = todo[i]
                scores[i] = jnp.dot(keys, qe[b, :, cols], preferred_element_type=jnp.float32)
            if 0 <= i - 1 < count:
                b, cols, _, _, bias, going = todo[i - 1]
                s = scores[i - 1]
                if bias is not None:
                    s = jnp.concatenate([s[:TOK] + bias, s[TOK:]], axis=0)
                new = jnp.max(s, axis=0, keepdims=True)
                fade = None
                if going:
                    old = peak[b, 0:1, cols]
                    new = jnp.maximum(old, new)
                    fade = jnp.exp2((old - new) * SCALE)
                weights[i - 1] = (jnp.exp2((s - new) * SCALE).astype(jnp.bfloat16), new, fade)
                scores[i - 1] = None
            if i >= 2:
                b, cols, _, vt, _, going = todo[i - 2]
                w, new, fade = weights[i - 2]
                done.append((b, cols, new, fade, jnp.dot(vt, w, preferred_element_type=jnp.float32)))
                weights[i - 2] = None
        for b, cols, new, fade, o in done:
            peak[b, 0:1, cols] = new
            acc[b, :, cols] = o if fade is None else acc[b, :, cols] * fade + o

    def own_work(j, _):
        jobs = []
        for i in (1, 0):
            b = NY - 2 - 2 * j + i
            at = slot(b, 0)
            own = kv[at, 2 * TOK:, :].astype(jnp.float32)
            row = jnp.concatenate([own[0:1], own[1:2]], axis=1)
            rows = jnp.broadcast_to(row, (TOK, TOK))
            begin = row[:, 0:1]
            first[b] = jnp.broadcast_to(begin, (8, 128))
            rest = jnp.concatenate([jnp.where(row == begin, 0.0, NEG)] * GROUP, axis=1)
            which = lax.broadcasted_iota(jnp.int32, (DIM, LANES), 0)
            qe[b, DIM:, :] = jnp.where(which == 0, 1.0, jnp.where(which == 1, rest, 0.0)).astype(jnp.bfloat16)
            bias = jnp.where((rows == rows.T) & (key <= token), 0.0, NEG)
            early = [slot(b - 1, 0), slot(b - 2, 0)]
            keys = jnp.concatenate([own_keys(at)] + [early_keys(one, b) for one in early], axis=0)
            jobs.append((b, keys, turned_values([at] + early), bias, False))
        chains(jobs)
        return 0

    lax.fori_loop(0, NY // 2, own_work, 0)

    def pair_work(pair, way, step):
        shift = shift_of(way, step)
        there = lax.rem(z + shift + NZ, NZ)
        jobs = []
        for i in (1, 0):
            b = 2 * pair + i
            slots = [slot(b - 1, shift), slot(jnp.where(there < z, b, b - 2), shift)]
            keys = jnp.concatenate([early_keys(at, b) for at in slots], axis=0)
            jobs.append((b, keys, turned_values(slots), None, True))
        chains(jobs)

    def later_step(step, _):
        def catch_up(j, _):
            @pl.when(j == 2)
            def _():
                for way in range(2):
                    for row in (NY - 1, NY - 2):
                        wait_x(row, way, step)

                    @pl.when((step == 1) & side_comes(way))
                    def _():
                        side_copy(way).wait_recv()
            pair_work(1 - j // 2, j % 2, step)
            return 0

        lax.fori_loop(0, 4, catch_up, 0)
        arrive(step + 1)
        return 0

    lax.fori_loop(1, half, later_step, 0)

    rows = TOK // 2
    wide = GROUP * DIM
    cols = out_ref.at[:, pl.ds(pl.multiple_of((core * NY + y) * wide, wide), wide)]

    def part(b, c):
        return o_buf.at[b, pl.ds(pl.multiple_of(c * rows, rows), rows)]

    def over(b):
        return remote(part(b, 1 - core), cols, o_send.at[b, 1], o_recv.at[y, 1], (index_of(x, b, z), 1 - core))

    def along(b):
        return remote(part(b, core), cols, o_send.at[b, 0], o_recv.at[y, 0], (index_of(x, b, z), core))

    def stay(b):
        return pltpu.make_async_copy(part(b, core), cols, o_recv.at[y, 0])

    def send_back(b):
        mixed = acc[b, :DIM, :] / acc[b, DIM:DIM + 1, :]
        for g in range(GROUP):
            o_buf[b, :, g * DIM:(g + 1) * DIM] = mixed[:, g * TOK:(g + 1) * TOK].T.astype(jnp.bfloat16)
        over(b).start()

        @pl.when(b != y)
        def _():
            along(b).start()

        @pl.when(b == y)
        def _():
            stay(b).start()

    def finish(j, _):
        @pl.when(j == 1)
        def _():
            for row in (NY - 1, NY - 2):
                wait_x(row, last_way(row), half)
        pair_work(1 - j, 0, half)
        for i in (1, 0):
            send_back(2 * (1 - j) + i)
        return 0

    lax.fori_loop(0, 2, finish, 0)

    for copy in sent + asked:
        copy.wait_send()

    def z_drain(j, _):
        row, way, step = j // (2 * half), (j // half) % 2, 1 + j % half

        @pl.when((step < half) | (way == last_way(row)))
        def _():
            z_copy(way, row, step).wait_send()
        return 0

    lax.fori_loop(0, 2 * NY * half, z_drain, 0)

    def x_drain(j, _):
        row, way, step = NY - 1 - j // (2 * (half + 1)), (j // (half + 1)) % 2, j % (half + 1)
        there_is = jnp.where(step == 0, way == 0, (step < half) | (way == last_way(row)))

        @pl.when(there_is & over_x(way, row, step) & (x < NX - 1))
        def _():
            x_copy(row, way, step).wait_send()
        return 0

    lax.fori_loop(0, 2 * BACK * (half + 1), x_drain, 0)
    for way in range(2):
        @pl.when(side_goes(way))
        def _():
            side_copy(way).wait_send()
    for b in range(NY):
        over(b).wait_send()

        @pl.when(b != y)
        def _():
            along(b).wait_send()
        for e in range(2):
            pltpu.make_async_copy(part(b, core), cols, o_recv.at[b, e]).wait()


def per_device(queries, keys, values, segment_ids):
    any_spec = pl.BlockSpec(memory_space=pl.ANY)
    hbm_spec = pl.BlockSpec(memory_space=pltpu.HBM)
    dma = pltpu.SemaphoreType.DMA
    bf16, f32 = jnp.bfloat16, jnp.float32
    half = NZ // 2
    return pl.pallas_call(
        attention_kernel,
        out_shape=jax.ShapeDtypeStruct((TOK // 2, 2 * NY * GROUP * DIM), bf16),
        in_specs=[hbm_spec] * 4,
        out_specs=any_spec,
        scratch_shapes=[
            pltpu.VMEM(queries.shape, bf16), pltpu.VMEM(values.shape, bf16), pltpu.VMEM((2, 128), jnp.int32), pltpu.VMEM((16, 128), bf16),
            pltpu.VMEM((NY, 2 * DIM, TOK // 2), bf16), pltpu.VMEM((NY, DIM, LANES), bf16),
            pltpu.VMEM((SLOTS, SLOT_ROWS, DIM), bf16),
            pltpu.VMEM((NY, 2 * DIM, LANES), bf16), pltpu.VMEM((NY, DIM + 16, LANES), f32), pltpu.VMEM((NY, 8, LANES), f32),
            pltpu.VMEM((NY, 8, 128), f32), pltpu.VMEM((NY, TOK, GROUP * DIM), bf16),
            dma((3,)), dma((NY - 1, 3)), dma((NY,)), dma((NY,)), dma((NY - 1,)),
            dma((2, NY, half)), dma((2, NY, half)), dma((BACK, 2, half + 1)), dma((BACK, 2, half + 1)),
            dma((2,)), dma((2,)), dma((NY, 2)), dma((NY, 2))],
        compiler_params=pltpu.CompilerParams(collective_id=0, has_side_effects=True,
                                             vmem_limit_bytes=40 * 1024 * 1024),
        name="attention",
    )(*(pltpu.with_memory_space_constraint(one, pltpu.HBM) for one in
        (queries, keys, values, segment_ids.reshape(2, 128))))


def solution(mesh):
    return jax.shard_map(
        per_device,
        mesh=mesh,
        in_specs=(P("ctx", "kvh"), P("ctx", "kvh"), P("ctx", "kvh"), P("ctx")),
        out_specs=P(("ctx", "kvh"), None),
        check_vma=False,
    )
```

```python
import jax
import jax.numpy as jnp
from jax import lax
from jax.experimental import pallas as pl
from jax.experimental.pallas import tpu as pltpu
from jax.sharding import PartitionSpec as P

NX, NY, NZ = 4, 4, 8
TOK = 256
DIM = 128
GROUP = 4
BACK = 2
ROWS = NY + BACK
SLOTS = ROWS * NZ
SLOT_ROWS = 2 * TOK + 16
LANES = GROUP * TOK
NEG = -1e30
FAR_ID = 512.0
SCALE = 1.4426950408889634 * DIM ** -0.5


def place():
    me = lax.axis_index("ctx")
    return me, me // (NY * NZ), (me // NZ) % NY, me % NZ


def index_of(x, y, z):
    return (x * NY + y) * NZ + z


def remote(src, dst, send, recv, device):
    return pltpu.make_async_remote_copy(src_ref=src, dst_ref=dst, send_sem=send, recv_sem=recv,
                                        device_id=device, device_id_type=pl.DeviceIdType.MESH)


def attention_kernel(q_ref, k_ref, v_ref, seg_ref, out_ref, q_buf, v_buf, seg_in, seg_buf, vt_buf, qt_buf,
                     kv, qe, acc, peak, first, o_buf, load_sem,
                     y_send, y_recv, q_send, q_recv, z_send, z_recv, x_send, x_recv,
                     side_send, side_recv, ready, o_send, o_recv):
    me, x, y, z = place()
    core = lax.axis_index("kvh")
    half = NZ // 2

    def dev(x_, y_, z_):
        return (index_of(x_, y_, z_), core)

    y_peers = [lax.rem(y + d, NY) for d in range(1, NY)]
    z_next, z_prev = lax.rem(z + 1, NZ), lax.rem(z + NZ - 1, NZ)
    x_next, x_prev = lax.rem(x + 1, NX), lax.rem(x + NX - 1, NX)
    barrier = pltpu.get_barrier_semaphore()
    friends = ([dev(x, p, z) for p in y_peers] + [(index_of(x, p, z), 1 - core) for p in [y] + y_peers]
               + [dev(x, y, z_next), dev(x, y, z_prev)])
    for friend in friends:
        pl.semaphore_signal(barrier, inc=1, device_id=friend, device_id_type=pl.DeviceIdType.MESH)

    @pl.when(x < NX - 1)
    def _():
        pl.semaphore_signal(barrier, inc=1, device_id=dev(x_next, y, z), device_id_type=pl.DeviceIdType.MESH)
    load_v = pltpu.make_async_copy(v_ref, v_buf, load_sem.at[0])
    load_q = pltpu.make_async_copy(q_ref, q_buf, load_sem.at[1])
    load_ids = pltpu.make_async_copy(seg_ref, seg_in, load_sem.at[2])
    load_ids.start()
    load_v.start()
    load_q.start()

    load_ids.wait()
    ids = seg_in[...].astype(jnp.float32)
    line = lax.broadcasted_iota(jnp.int32, (16, 128), 0)
    ids = jnp.where(line == 0, ids[0:1], jnp.where(line == 1, ids[1:2], FAR_ID))
    seg_buf[...] = ids.astype(jnp.bfloat16)
    def slot(row, shift):
        return (BACK + row) * NZ + lax.rem(z + shift + NZ, NZ)

    def head_cols(p):
        return pl.ds(pl.multiple_of(p * DIM, DIM), DIM)

    mine = (BACK + y) * NZ + z
    pltpu.make_async_copy(k_ref.at[:, head_cols(y)], kv.at[mine, pl.ds(0, TOK)], y_recv.at[y]).start()
    pltpu.make_async_copy(seg_buf, kv.at[mine, pl.ds(2 * TOK, 16)], y_recv.at[y]).start()
    load_v.wait()
    for p in range(NY):
        turned = v_buf[:, p * DIM:(p + 1) * DIM].T
        vt_buf[p, :DIM, :] = turned[:, :DIM]
        vt_buf[p, DIM:, :] = turned[:, DIM:]
    pltpu.make_async_copy(vt_buf.at[y], kv.at[mine, pl.ds(TOK, TOK)], y_recv.at[y]).start()
    pl.semaphore_wait(barrier, len(friends) + jnp.where(x > 0, 1, 0))

    @pl.when(x > 0)
    def _():
        pl.semaphore_signal(ready, inc=1, device_id=dev(x_prev, y, z), device_id_type=pl.DeviceIdType.MESH)

    sent = []
    for n, p in enumerate(y_peers):
        for i, (src, lo, rows) in enumerate(((k_ref.at[:, head_cols(p)], 0, TOK), (vt_buf.at[p], TOK, TOK),
                                             (seg_buf, 2 * TOK, 16))):
            copy = remote(src, kv.at[mine, pl.ds(lo, rows)], y_send.at[n, i], y_recv.at[y], dev(x, p, z))
            copy.start()
            sent.append(copy)

    def shift_of(way, step):
        return step * (2 * way - 1)

    def z_copy(way, row, step):
        at = kv.at[slot(row, shift_of(way, step - 1))]
        neighbour = jnp.where(way == 0, z_next, z_prev)
        return remote(at, at, z_send.at[way, row, step - 1], z_recv.at[way, row, step - 1], dev(x, y, neighbour))

    def x_copy(row, way, step):
        shift = shift_of(way, step)
        return remote(kv.at[slot(row, shift)], kv.at[slot(row - NY, shift)], x_send.at[row - NY + BACK, way, step],
                      x_recv.at[row - NY + BACK, way, step], dev(x_next, y, z))

    def last_way(row):
        return lax.rem(row + 1, 2)

    def row2_over_x(way, step):
        return (lax.rem(z + shift_of(way, step) + NZ, NZ) >= z) & (step != 1)

    def over_x(way, row, step):
        return (row == NY - 1) | ((row == NY - 2) & row2_over_x(way, step))

    def forward(way, row, step):
        @pl.when(over_x(way, row, step) & (x < NX - 1))
        def _():
            x_copy(row, way, step).start()

    def pass_on(way, row, step):
        @pl.when((step < half - 1) | ((step == half - 1) & (way == last_way(row))))
        def _():
            z_copy(way, row, step + 1).start()
        forward(way, row, step)

    def side_copy(way):
        at = kv.at[slot(-BACK, 0)]
        return remote(at, at, side_send.at[way], side_recv.at[way], dev(x, y, z_prev if way else z_next))

    def side_goes(way):
        return (x > 0) & ((z >= 1) if way else (z == NZ - 1))

    def side_comes(way):
        return (x > 0) & ((z < NZ - 1) if way else (z == 0))

    def row_of(i):
        return lax.rem(y + jnp.where(i == 0, 0, jnp.where(i == 1, 1, jnp.where(i == 2, NY - 1, 2))), NY)

    def first_sends(i, _):
        row = row_of(i)
        at = kv.at[slot(row, 0)]
        pltpu.make_async_copy(at, at, y_recv.at[row]).wait()
        z_copy(0, row, 1).start()
        z_copy(1, row, 1).start()
        return 0

    lax.fori_loop(0, NY, first_sends, 0)

    @pl.when(x < NX - 1)
    def _():
        pl.semaphore_wait(ready, 1)
    forward(0, NY - 1, 0)
    forward(0, NY - 2, 0)
    load_q.wait()
    for p in range(NY):
        for g in range(GROUP):
            h = p * GROUP + g
            qt_buf[p, :, g * TOK:(g + 1) * TOK] = q_buf[:, h * DIM:(h + 1) * DIM].T
    asked = []
    for n, p in enumerate(y_peers):
        copy = remote(qt_buf.at[p], qe.at[y, pl.ds(0, DIM)], q_send.at[n], q_recv.at[n], dev(x, p, z))
        copy.start()
        asked.append(copy)
    own_q = pltpu.make_async_copy(qt_buf.at[y], qe.at[y, pl.ds(0, DIM)], q_send.at[NY - 1])
    own_q.start()

    @pl.when(x == 0)
    def _():
        def blank(at, _):
            kv[at, :2 * TOK, :] = jnp.zeros((2 * TOK, DIM), jnp.bfloat16)
            kv[at, 2 * TOK:, :] = jnp.full((16, DIM), -1.0, jnp.bfloat16)
            return 0

        lax.fori_loop(0, BACK * NZ, blank, 0)

    def arrive(i, step):
        row = row_of(i)
        for way in range(2):
            @pl.when((step < half) | (way == last_way(row)))
            def _():
                z_copy(way, row, step).wait_recv()
                pass_on(way, row, step)

    def first_step(i, _):
        arrive(i, 1)
        return 0

    lax.fori_loop(0, NY, first_step, 0)

    def wait_x(row, way, step):
        @pl.when(over_x(way, row, step) & (x > 0))
        def _():
            x_copy(row, way, step).wait_recv()

    for row in (NY - 1, NY - 2):
        wait_x(row, 0, 0)
    for way in range(2):
        @pl.when(side_goes(way))
        def _():
            side_copy(way).start()
    for copy in asked:
        copy.wait_recv()
    own_q.wait()

    key = lax.broadcasted_iota(jnp.int32, (TOK, TOK), 0)
    token = lax.broadcasted_iota(jnp.int32, (TOK, TOK), 1)

    lane = lax.broadcasted_iota(jnp.int32, (TOK, DIM), 1)
    line = lax.broadcasted_iota(jnp.int32, (TOK, DIM), 0)
    plain = jnp.where(lane == 1, 1.0, 0.0)

    def early_keys(at, b):
        there = kv[at, 2 * TOK:, :].astype(jnp.float32)
        less = jnp.where(there < first[b, 0:1, :], 1.0, 0.0)
        count = jnp.sum(jnp.sum(less, axis=0, keepdims=True), axis=1, keepdims=True).astype(jnp.int32)
        extra = jnp.where((lane == 0) & (line < count), NEG, plain).astype(jnp.bfloat16)
        return jnp.concatenate([kv[at, :TOK, :], extra], axis=1)

    def own_keys(at):
        return jnp.concatenate([kv[at, :TOK, :], jnp.zeros((TOK, DIM), jnp.bfloat16)], axis=1)

    def turned_values(slots):
        vt = jnp.concatenate([kv[at, lo:lo + DIM, :] for at in slots for lo in (TOK, TOK + DIM)], axis=1)
        return jnp.concatenate([vt, jnp.ones((16, vt.shape[1]), jnp.bfloat16)], axis=0)

    def chains(jobs):
        todo = [(b, slice(g * TOK, (g + 1) * TOK), keys, vt, bias, going)
                for b, keys, vt, bias, going in jobs for g in range(GROUP)]
        count = len(todo)
        scores, weights, done = [None] * count, [None] * count, []
        for i in range(count + 2):
            if i < count:
                b, cols, keys, _, _, _ = todo[i]
                scores[i] = jnp.dot(keys, qe[b, :, cols], preferred_element_type=jnp.float32)
            if 0 <= i - 1 < count:
                b, cols, _, _, bias, going = todo[i - 1]
                s = scores[i - 1]
                if bias is not None:
                    s = jnp.concatenate([s[:TOK] + bias, s[TOK:]], axis=0)
                new = jnp.max(s, axis=0, keepdims=True)
                fade = None
                if going:
                    old = peak[b, 0:1, cols]
                    new = jnp.maximum(old, new)
                    fade = jnp.exp2((old - new) * SCALE)
                weights[i - 1] = (jnp.exp2((s - new) * SCALE).astype(jnp.bfloat16), new, fade)
                scores[i - 1] = None
            if i >= 2:
                b, cols, _, vt, _, going = todo[i - 2]
                w, new, fade = weights[i - 2]
                done.append((b, cols, new, fade, jnp.dot(vt, w, preferred_element_type=jnp.float32)))
                weights[i - 2] = None
        for b, cols, new, fade, o in done:
            peak[b, 0:1, cols] = new
            acc[b, :, cols] = o if fade is None else acc[b, :, cols] * fade + o

    def own_work(j, _):
        jobs = []
        for i in (1, 0):
            b = NY - 2 - 2 * j + i
            at = slot(b, 0)
            own = kv[at, 2 * TOK:, :].astype(jnp.float32)
            row = jnp.concatenate([own[0:1], own[1:2]], axis=1)
            rows = jnp.broadcast_to(row, (TOK, TOK))
            begin = row[:, 0:1]
            first[b] = jnp.broadcast_to(begin, (8, 128))
            rest = jnp.concatenate([jnp.where(row == begin, 0.0, NEG)] * GROUP, axis=1)
            which = lax.broadcasted_iota(jnp.int32, (DIM, LANES), 0)
            qe[b, DIM:, :] = jnp.where(which == 0, 1.0, jnp.where(which == 1, rest, 0.0)).astype(jnp.bfloat16)
            bias = jnp.where((rows == rows.T) & (key <= token), 0.0, NEG)
            early = [slot(b - 1, 0), slot(b - 2, 0)]
            keys = jnp.concatenate([own_keys(at)] + [early_keys(one, b) for one in early], axis=0)
            jobs.append((b, keys, turned_values([at] + early), bias, False))
        chains(jobs)
        return 0

    lax.fori_loop(0, NY // 2, own_work, 0)

    def pair_work(pair, way, step):
        shift = shift_of(way, step)
        there = lax.rem(z + shift + NZ, NZ)
        jobs = []
        for i in (1, 0):
            b = 2 * pair + i
            slots = [slot(b - 1, shift), slot(jnp.where(there < z, b, b - 2), shift)]
            keys = jnp.concatenate([early_keys(at, b) for at in slots], axis=0)
            jobs.append((b, keys, turned_values(slots), None, True))
        chains(jobs)

    def later_step(step, _):
        def catch_up(j, _):
            @pl.when(step < half - 1)
            def _():
                arrive(j, step + 1)

            @pl.when(j == 2)
            def _():
                for way in range(2):
                    for row in (NY - 1, NY - 2):
                        wait_x(row, way, step)

                    @pl.when((step == 1) & side_comes(way))
                    def _():
                        side_copy(way).wait_recv()
            pair_work(1 - j // 2, j % 2, step)
            return 0

        lax.fori_loop(0, 4, catch_up, 0)
        return 0

    lax.fori_loop(1, half, later_step, 0)

    def last_step(i, _):
        arrive(i, half)
        return 0

    lax.fori_loop(0, NY, last_step, 0)

    rows = TOK // 2
    wide = GROUP * DIM
    cols = out_ref.at[:, pl.ds(pl.multiple_of((core * NY + y) * wide, wide), wide)]

    def part(b, c):
        return o_buf.at[b, pl.ds(pl.multiple_of(c * rows, rows), rows)]

    def over(b):
        return remote(part(b, 1 - core), cols, o_send.at[b, 1], o_recv.at[y, 1], (index_of(x, b, z), 1 - core))

    def along(b):
        return remote(part(b, core), cols, o_send.at[b, 0], o_recv.at[y, 0], (index_of(x, b, z), core))

    def stay(b):
        return pltpu.make_async_copy(part(b, core), cols, o_recv.at[y, 0])

    def send_back(b):
        mixed = (acc[b, :DIM, :] * (1.0 / acc[b, DIM:DIM + 1, :])).astype(jnp.bfloat16)
        for g in range(GROUP):
            o_buf[b, :, g * DIM:(g + 1) * DIM] = mixed[:, g * TOK:(g + 1) * TOK].T
        over(b).start()

        @pl.when(b != y)
        def _():
            along(b).start()

        @pl.when(b == y)
        def _():
            stay(b).start()

    def finish(j, _):
        @pl.when(j == 1)
        def _():
            for row in (NY - 1, NY - 2):
                wait_x(row, last_way(row), half)
        pair_work(1 - j, 0, half)
        for i in (1, 0):
            send_back(2 * (1 - j) + i)
        return 0

    lax.fori_loop(0, 2, finish, 0)

    for copy in sent + asked:
        copy.wait_send()

    def z_drain(j, _):
        row, way, step = j // (2 * half), (j // half) % 2, 1 + j % half

        @pl.when((step < half) | (way == last_way(row)))
        def _():
            z_copy(way, row, step).wait_send()
        return 0

    lax.fori_loop(0, 2 * NY * half, z_drain, 0)

    def x_drain(j, _):
        row, way, step = NY - 1 - j // (2 * (half + 1)), (j // (half + 1)) % 2, j % (half + 1)
        there_is = jnp.where(step == 0, way == 0, (step < half) | (way == last_way(row)))

        @pl.when(there_is & over_x(way, row, step) & (x < NX - 1))
        def _():
            x_copy(row, way, step).wait_send()
        return 0

    lax.fori_loop(0, 2 * BACK * (half + 1), x_drain, 0)
    for way in range(2):
        @pl.when(side_goes(way))
        def _():
            side_copy(way).wait_send()
    for b in range(NY):
        over(b).wait_send()

        @pl.when(b != y)
        def _():
            along(b).wait_send()
        for e in range(2):
            pltpu.make_async_copy(part(b, core), cols, o_recv.at[b, e]).wait()


def per_device(queries, keys, values, segment_ids):
    any_spec = pl.BlockSpec(memory_space=pl.ANY)
    hbm_spec = pl.BlockSpec(memory_space=pltpu.HBM)
    dma = pltpu.SemaphoreType.DMA
    bf16, f32 = jnp.bfloat16, jnp.float32
    half = NZ // 2
    return pl.pallas_call(
        attention_kernel,
        out_shape=jax.ShapeDtypeStruct((TOK // 2, 2 * NY * GROUP * DIM), bf16),
        in_specs=[hbm_spec] * 4,
        out_specs=any_spec,
        scratch_shapes=[
            pltpu.VMEM(queries.shape, bf16), pltpu.VMEM(values.shape, bf16), pltpu.VMEM((2, 128), jnp.int32), pltpu.VMEM((16, 128), bf16),
            pltpu.VMEM((NY, 2 * DIM, TOK // 2), bf16), pltpu.VMEM((NY, DIM, LANES), bf16),
            pltpu.VMEM((SLOTS, SLOT_ROWS, DIM), bf16),
            pltpu.VMEM((NY, 2 * DIM, LANES), bf16), pltpu.VMEM((NY, DIM + 16, LANES), f32), pltpu.VMEM((NY, 8, LANES), f32),
            pltpu.VMEM((NY, 8, 128), f32), pltpu.VMEM((NY, TOK, GROUP * DIM), bf16),
            dma((3,)), dma((NY - 1, 3)), dma((NY,)), dma((NY,)), dma((NY - 1,)),
            dma((2, NY, half)), dma((2, NY, half)), dma((BACK, 2, half + 1)), dma((BACK, 2, half + 1)),
            dma((2,)), dma((2,)), pltpu.SemaphoreType.REGULAR, dma((NY, 2)), dma((NY, 2))],
        compiler_params=pltpu.CompilerParams(collective_id=0, has_side_effects=True,
                                             vmem_limit_bytes=40 * 1024 * 1024),
        name="attention",
    )(*(pltpu.with_memory_space_constraint(one, pltpu.HBM) for one in
        (queries, keys, values, segment_ids.reshape(2, 128))))


def solution(mesh):
    return jax.shard_map(
        per_device,
        mesh=mesh,
        in_specs=(P("ctx", "kvh"), P("ctx", "kvh"), P("ctx", "kvh"), P("ctx")),
        out_specs=P(("ctx", "kvh"), None),
        check_vma=False,
    )
```

```python
import jax
import jax.numpy as jnp
from jax import lax
from jax.experimental import pallas as pl
from jax.experimental.pallas import tpu as pltpu
from jax.sharding import PartitionSpec as P

NX, NY, NZ = 4, 4, 8
TOK = 256
DIM = 128
GROUP = 4
BACK = 2
ROWS = NY + BACK
SLOTS = ROWS * NZ
SLOT_ROWS = 2 * TOK + 16
LANES = GROUP * TOK
NEG = -1e30
FAR_ID = 512.0
SCALE = 1.4426950408889634 * DIM ** -0.5


def place():
    me = lax.axis_index("ctx")
    return me, me // (NY * NZ), (me // NZ) % NY, me % NZ


def index_of(x, y, z):
    return (x * NY + y) * NZ + z


def remote(src, dst, send, recv, device):
    return pltpu.make_async_remote_copy(src_ref=src, dst_ref=dst, send_sem=send, recv_sem=recv,
                                        device_id=device, device_id_type=pl.DeviceIdType.MESH)


def attention_kernel(q_ref, k_ref, v_ref, seg_ref, out_ref, q_buf, v_buf, seg_in, seg_buf, vt_buf, qt_buf,
                     kv, qe, acc, peak, first, o_buf, load_sem,
                     y_send, y_recv, q_send, q_recv, z_send, z_recv, x_send, x_recv,
                     side_send, side_recv, ready, o_send, o_recv):
    me, x, y, z = place()
    core = lax.axis_index("kvh")
    half = NZ // 2

    def dev(x_, y_, z_):
        return (index_of(x_, y_, z_), core)

    y_peers = [lax.rem(y + d, NY) for d in range(1, NY)]
    z_next, z_prev = lax.rem(z + 1, NZ), lax.rem(z + NZ - 1, NZ)
    x_next, x_prev = lax.rem(x + 1, NX), lax.rem(x + NX - 1, NX)
    barrier = pltpu.get_barrier_semaphore()
    friends = ([dev(x, p, z) for p in y_peers] + [(index_of(x, p, z), 1 - core) for p in [y] + y_peers]
               + [dev(x, y, z_next), dev(x, y, z_prev)])
    for friend in friends:
        pl.semaphore_signal(barrier, inc=1, device_id=friend, device_id_type=pl.DeviceIdType.MESH)

    @pl.when(x < NX - 1)
    def _():
        pl.semaphore_signal(barrier, inc=1, device_id=dev(x_next, y, z), device_id_type=pl.DeviceIdType.MESH)
    load_v = pltpu.make_async_copy(v_ref, v_buf, load_sem.at[0])
    load_q = pltpu.make_async_copy(q_ref, q_buf, load_sem.at[1])
    load_ids = pltpu.make_async_copy(seg_ref, seg_in, load_sem.at[2])
    load_ids.start()
    load_v.start()
    load_q.start()

    load_ids.wait()
    ids = seg_in[...].astype(jnp.float32)
    line = lax.broadcasted_iota(jnp.int32, (16, 128), 0)
    ids = jnp.where(line == 0, ids[0:1], jnp.where(line == 1, ids[1:2], FAR_ID))
    seg_buf[...] = ids.astype(jnp.bfloat16)
    def slot(row, shift):
        return (BACK + row) * NZ + lax.rem(z + shift + NZ, NZ)

    def head_cols(p):
        return pl.ds(pl.multiple_of(p * DIM, DIM), DIM)

    mine = (BACK + y) * NZ + z
    pltpu.make_async_copy(k_ref.at[:, head_cols(y)], kv.at[mine, pl.ds(0, TOK)], y_recv.at[y]).start()
    pltpu.make_async_copy(seg_buf, kv.at[mine, pl.ds(2 * TOK, 16)], y_recv.at[y]).start()
    pl.semaphore_wait(barrier, len(friends) + jnp.where(x > 0, 1, 0))

    @pl.when(x > 0)
    def _():
        pl.semaphore_signal(ready, inc=1, device_id=dev(x_prev, y, z), device_id_type=pl.DeviceIdType.MESH)

    sent = []

    def to_peers(i, src_of, lo, rows):
        for n, p in enumerate(y_peers):
            copy = remote(src_of(p), kv.at[mine, pl.ds(lo, rows)], y_send.at[n, i], y_recv.at[y], dev(x, p, z))
            copy.start()
            sent.append(copy)

    to_peers(0, lambda p: k_ref.at[:, head_cols(p)], 0, TOK)
    to_peers(2, lambda p: seg_buf, 2 * TOK, 16)
    load_v.wait()
    for p in range(NY):
        turned = v_buf[:, p * DIM:(p + 1) * DIM].T
        vt_buf[p, :DIM, :] = turned[:, :DIM]
        vt_buf[p, DIM:, :] = turned[:, DIM:]
    pltpu.make_async_copy(vt_buf.at[y], kv.at[mine, pl.ds(TOK, TOK)], y_recv.at[y]).start()
    to_peers(1, lambda p: vt_buf.at[p], TOK, TOK)

    def shift_of(way, step):
        return step * (2 * way - 1)

    def z_copy(way, row, step):
        at = kv.at[slot(row, shift_of(way, step - 1))]
        neighbour = jnp.where(way == 0, z_next, z_prev)
        return remote(at, at, z_send.at[way, row, step - 1], z_recv.at[way, row, step - 1], dev(x, y, neighbour))

    def x_copy(row, way, step):
        shift = shift_of(way, step)
        return remote(kv.at[slot(row, shift)], kv.at[slot(row - NY, shift)], x_send.at[row - NY + BACK, way, step],
                      x_recv.at[row - NY + BACK, way, step], dev(x_next, y, z))

    def last_way(row):
        return lax.rem(row + 1, 2)

    def row2_over_x(way, step):
        return (lax.rem(z + shift_of(way, step) + NZ, NZ) >= z) & (step != 1)

    def over_x(way, row, step):
        return (row == NY - 1) | ((row == NY - 2) & row2_over_x(way, step))

    def forward(way, row, step):
        @pl.when(over_x(way, row, step) & (x < NX - 1))
        def _():
            x_copy(row, way, step).start()

    def pass_on(way, row, step):
        @pl.when((step < half - 1) | ((step == half - 1) & (way == last_way(row))))
        def _():
            z_copy(way, row, step + 1).start()
        forward(way, row, step)

    def side_copy(way):
        at = kv.at[slot(-BACK, 0)]
        return remote(at, at, side_send.at[way], side_recv.at[way], dev(x, y, z_prev if way else z_next))

    def side_goes(way):
        return (x > 0) & ((z >= 1) if way else (z == NZ - 1))

    def side_comes(way):
        return (x > 0) & ((z < NZ - 1) if way else (z == 0))

    def row_of(i):
        return lax.rem(y + jnp.where(i == 0, 0, jnp.where(i == 1, 1, jnp.where(i == 2, NY - 1, 2))), NY)

    def first_sends(i, _):
        row = row_of(i)
        at = kv.at[slot(row, 0)]
        pltpu.make_async_copy(at, at, y_recv.at[row]).wait()
        z_copy(0, row, 1).start()
        z_copy(1, row, 1).start()
        return 0

    lax.fori_loop(0, NY, first_sends, 0)

    @pl.when(x < NX - 1)
    def _():
        pl.semaphore_wait(ready, 1)
    forward(0, NY - 1, 0)
    forward(0, NY - 2, 0)
    load_q.wait()
    for p in range(NY):
        for g in range(GROUP):
            h = p * GROUP + g
            qt_buf[p, :, g * TOK:(g + 1) * TOK] = q_buf[:, h * DIM:(h + 1) * DIM].T
    asked = []
    for n, p in enumerate(y_peers):
        copy = remote(qt_buf.at[p], qe.at[y, pl.ds(0, DIM)], q_send.at[n], q_recv.at[n], dev(x, p, z))
        copy.start()
        asked.append(copy)
    own_q = pltpu.make_async_copy(qt_buf.at[y], qe.at[y, pl.ds(0, DIM)], q_send.at[NY - 1])
    own_q.start()

    @pl.when(x == 0)
    def _():
        def blank(at, _):
            kv[at, :2 * TOK, :] = jnp.zeros((2 * TOK, DIM), jnp.bfloat16)
            kv[at, 2 * TOK:, :] = jnp.full((16, DIM), -1.0, jnp.bfloat16)
            return 0

        lax.fori_loop(0, BACK * NZ, blank, 0)

    def arrive(i, step):
        row = row_of(i)
        for way in range(2):
            @pl.when((step < half) | (way == last_way(row)))
            def _():
                z_copy(way, row, step).wait_recv()
                pass_on(way, row, step)

    def first_step(i, _):
        arrive(i, 1)
        return 0

    lax.fori_loop(0, NY, first_step, 0)

    def wait_x(row, way, step):
        @pl.when(over_x(way, row, step) & (x > 0))
        def _():
            x_copy(row, way, step).wait_recv()

    for row in (NY - 1, NY - 2):
        wait_x(row, 0, 0)
    for way in range(2):
        @pl.when(side_goes(way))
        def _():
            side_copy(way).start()
    for copy in asked:
        copy.wait_recv()
    own_q.wait()

    key = lax.broadcasted_iota(jnp.int32, (TOK, TOK), 0)
    token = lax.broadcasted_iota(jnp.int32, (TOK, TOK), 1)

    lane = lax.broadcasted_iota(jnp.int32, (TOK, DIM), 1)
    line = lax.broadcasted_iota(jnp.int32, (TOK, DIM), 0)
    plain = jnp.where(lane == 1, 1.0, 0.0)

    def early_keys(at, b):
        there = kv[at, 2 * TOK:, :].astype(jnp.float32)
        less = jnp.where(there < first[b, 0:1, :], 1.0, 0.0)
        count = jnp.sum(jnp.sum(less, axis=0, keepdims=True), axis=1, keepdims=True).astype(jnp.int32)
        extra = jnp.where((lane == 0) & (line < count), NEG, plain).astype(jnp.bfloat16)
        return jnp.concatenate([kv[at, :TOK, :], extra], axis=1)

    def own_keys(at):
        return jnp.concatenate([kv[at, :TOK, :], jnp.zeros((TOK, DIM), jnp.bfloat16)], axis=1)

    def turned_values(slots):
        vt = jnp.concatenate([kv[at, lo:lo + DIM, :] for at in slots for lo in (TOK, TOK + DIM)], axis=1)
        return jnp.concatenate([vt, jnp.ones((16, vt.shape[1]), jnp.bfloat16)], axis=0)

    def chains(jobs):
        todo = [(b, slice(g * TOK, (g + 1) * TOK), keys, vt, bias, going)
                for b, keys, vt, bias, going in jobs for g in range(GROUP)]
        count = len(todo)
        scores, weights, done = [None] * count, [None] * count, []
        for i in range(count + 2):
            if i < count:
                b, cols, keys, _, _, _ = todo[i]
                scores[i] = jnp.dot(keys, qe[b, :, cols], preferred_element_type=jnp.float32)
            if 0 <= i - 1 < count:
                b, cols, _, _, bias, going = todo[i - 1]
                s = scores[i - 1]
                if bias is not None:
                    s = jnp.concatenate([s[:TOK] + bias, s[TOK:]], axis=0)
                new = jnp.max(s, axis=0, keepdims=True)
                fade = None
                if going:
                    old = peak[b, 0:1, cols]
                    new = jnp.maximum(old, new)
                    fade = jnp.exp2((old - new) * SCALE)
                weights[i - 1] = (jnp.exp2((s - new) * SCALE).astype(jnp.bfloat16), new, fade)
                scores[i - 1] = None
            if i >= 2:
                b, cols, _, vt, _, going = todo[i - 2]
                w, new, fade = weights[i - 2]
                done.append((b, cols, new, fade, jnp.dot(vt, w, preferred_element_type=jnp.float32)))
                weights[i - 2] = None
        for b, cols, new, fade, o in done:
            peak[b, 0:1, cols] = new
            acc[b, :, cols] = o if fade is None else acc[b, :, cols] * fade + o

    def own_work(j, _):
        jobs = []
        for i in (1, 0):
            b = NY - 2 - 2 * j + i
            at = slot(b, 0)
            own = kv[at, 2 * TOK:, :].astype(jnp.float32)
            row = jnp.concatenate([own[0:1], own[1:2]], axis=1)
            rows = jnp.broadcast_to(row, (TOK, TOK))
            begin = row[:, 0:1]
            first[b] = jnp.broadcast_to(begin, (8, 128))
            rest = jnp.concatenate([jnp.where(row == begin, 0.0, NEG)] * GROUP, axis=1)
            which = lax.broadcasted_iota(jnp.int32, (DIM, LANES), 0)
            qe[b, DIM:, :] = jnp.where(which == 0, 1.0, jnp.where(which == 1, rest, 0.0)).astype(jnp.bfloat16)
            bias = jnp.where((rows == rows.T) & (key <= token), 0.0, NEG)
            early = [slot(b - 1, 0), slot(b - 2, 0)]
            keys = jnp.concatenate([own_keys(at)] + [early_keys(one, b) for one in early], axis=0)
            jobs.append((b, keys, turned_values([at] + early), bias, False))
        chains(jobs)
        return 0

    lax.fori_loop(0, NY // 2, own_work, 0)

    def pair_work(pair, way, step):
        shift = shift_of(way, step)
        there = lax.rem(z + shift + NZ, NZ)
        jobs = []
        for i in (1, 0):
            b = 2 * pair + i
            slots = [slot(b - 1, shift), slot(jnp.where(there < z, b, b - 2), shift)]
            keys = jnp.concatenate([early_keys(at, b) for at in slots], axis=0)
            jobs.append((b, keys, turned_values(slots), None, True))
        chains(jobs)

    def wait_for_x(step):
        for way in range(2):
            for row in (NY - 1, NY - 2):
                wait_x(row, way, step)

            @pl.when((step == 1) & side_comes(way))
            def _():
                side_copy(way).wait_recv()

    def later_step(step, _):
        def catch_up(j, _):
            @pl.when(step < half - 1)
            def _():
                arrive(j, step + 1)

            @pl.when((step > 1) & (j == 2))
            def _():
                wait_for_x(step - 1)

            @pl.when((step > 1) | (j < 2))
            def _():
                pair_work(1 - j // 2, j % 2, step - j // 2)
            return 0

        lax.fori_loop(0, 4, catch_up, 0)
        return 0

    lax.fori_loop(1, half, later_step, 0)

    def last_step(i, _):
        arrive(i, half)
        return 0

    lax.fori_loop(0, NY, last_step, 0)

    rows = TOK // 2
    wide = GROUP * DIM
    cols = out_ref.at[:, pl.ds(pl.multiple_of((core * NY + y) * wide, wide), wide)]

    def part(b, c):
        return o_buf.at[b, pl.ds(pl.multiple_of(c * rows, rows), rows)]

    def over(b):
        return remote(part(b, 1 - core), cols, o_send.at[b, 1], o_recv.at[y, 1], (index_of(x, b, z), 1 - core))

    def along(b):
        return remote(part(b, core), cols, o_send.at[b, 0], o_recv.at[y, 0], (index_of(x, b, z), core))

    def stay(b):
        return pltpu.make_async_copy(part(b, core), cols, o_recv.at[y, 0])

    def send_back(b):
        mixed = (acc[b, :DIM, :] * (1.0 / acc[b, DIM:DIM + 1, :])).astype(jnp.bfloat16)
        for g in range(GROUP):
            o_buf[b, :, g * DIM:(g + 1) * DIM] = mixed[:, g * TOK:(g + 1) * TOK].T
        over(b).start()

        @pl.when(b != y)
        def _():
            along(b).start()

        @pl.when(b == y)
        def _():
            stay(b).start()

    def finish(j, _):
        @pl.when(j == 1)
        def _():
            wait_for_x(half - 1)

        @pl.when(j == 3)
        def _():
            for row in (NY - 1, NY - 2):
                wait_x(row, last_way(row), half)
        last = (j == 0) | (j == 3)
        pair = jnp.where(j == 0, 1, 0)
        pair_work(pair, jnp.where(j == 2, 1, 0), jnp.where(last, half, half - 1))

        @pl.when(last)
        def _():
            for i in (1, 0):
                send_back(2 * pair + i)
        return 0

    lax.fori_loop(0, 4, finish, 0)

    for copy in sent + asked:
        copy.wait_send()

    def z_drain(j, _):
        row, way, step = j // (2 * half), (j // half) % 2, 1 + j % half

        @pl.when((step < half) | (way == last_way(row)))
        def _():
            z_copy(way, row, step).wait_send()
        return 0

    lax.fori_loop(0, 2 * NY * half, z_drain, 0)

    def x_drain(j, _):
        row, way, step = NY - 1 - j // (2 * (half + 1)), (j // (half + 1)) % 2, j % (half + 1)
        there_is = jnp.where(step == 0, way == 0, (step < half) | (way == last_way(row)))

        @pl.when(there_is & over_x(way, row, step) & (x < NX - 1))
        def _():
            x_copy(row, way, step).wait_send()
        return 0

    lax.fori_loop(0, 2 * BACK * (half + 1), x_drain, 0)
    for way in range(2):
        @pl.when(side_goes(way))
        def _():
            side_copy(way).wait_send()
    for b in range(NY):
        over(b).wait_send()

        @pl.when(b != y)
        def _():
            along(b).wait_send()
        for e in range(2):
            pltpu.make_async_copy(part(b, core), cols, o_recv.at[b, e]).wait()


def per_device(queries, keys, values, segment_ids):
    any_spec = pl.BlockSpec(memory_space=pl.ANY)
    hbm_spec = pl.BlockSpec(memory_space=pltpu.HBM)
    dma = pltpu.SemaphoreType.DMA
    bf16, f32 = jnp.bfloat16, jnp.float32
    half = NZ // 2
    return pl.pallas_call(
        attention_kernel,
        out_shape=jax.ShapeDtypeStruct((TOK // 2, 2 * NY * GROUP * DIM), bf16),
        in_specs=[hbm_spec] * 4,
        out_specs=any_spec,
        scratch_shapes=[
            pltpu.VMEM(queries.shape, bf16), pltpu.VMEM(values.shape, bf16), pltpu.VMEM((2, 128), jnp.int32), pltpu.VMEM((16, 128), bf16),
            pltpu.VMEM((NY, 2 * DIM, TOK // 2), bf16), pltpu.VMEM((NY, DIM, LANES), bf16),
            pltpu.VMEM((SLOTS, SLOT_ROWS, DIM), bf16),
            pltpu.VMEM((NY, 2 * DIM, LANES), bf16), pltpu.VMEM((NY, DIM + 16, LANES), f32), pltpu.VMEM((NY, 8, LANES), f32),
            pltpu.VMEM((NY, 8, 128), f32), pltpu.VMEM((NY, TOK, GROUP * DIM), bf16),
            dma((3,)), dma((NY - 1, 3)), dma((NY,)), dma((NY,)), dma((NY - 1,)),
            dma((2, NY, half)), dma((2, NY, half)), dma((BACK, 2, half + 1)), dma((BACK, 2, half + 1)),
            dma((2,)), dma((2,)), pltpu.SemaphoreType.REGULAR, dma((NY, 2)), dma((NY, 2))],
        compiler_params=pltpu.CompilerParams(collective_id=0, has_side_effects=True,
                                             vmem_limit_bytes=40 * 1024 * 1024),
        name="attention",
    )(*(pltpu.with_memory_space_constraint(one, pltpu.HBM) for one in
        (queries, keys, values, segment_ids.reshape(2, 128))))


def solution(mesh):
    return jax.shard_map(
        per_device,
        mesh=mesh,
        in_specs=(P("ctx", "kvh"), P("ctx", "kvh"), P("ctx", "kvh"), P("ctx")),
        out_specs=P(("ctx", "kvh"), None),
        check_vma=False,
    )
```

```python
import jax
import jax.numpy as jnp
from jax import lax
from jax.experimental import pallas as pl
from jax.experimental.pallas import tpu as pltpu
from jax.sharding import PartitionSpec as P

NX, NY, NZ = 4, 4, 8
TOK = 256
DIM = 128
GROUP = 4
BACK = 2
ROWS = NY + BACK
SLOTS = ROWS * NZ
SLOT_ROWS = 2 * TOK + 16
LANES = GROUP * TOK
WIDE = 2 * TOK
NEG = -1e30
FAR_ID = 512.0
SCALE = 1.4426950408889634 * DIM ** -0.5


def place():
    me = lax.axis_index("ctx")
    return me, me // (NY * NZ), (me // NZ) % NY, me % NZ


def index_of(x, y, z):
    return (x * NY + y) * NZ + z


def remote(src, dst, send, recv, device):
    return pltpu.make_async_remote_copy(src_ref=src, dst_ref=dst, send_sem=send, recv_sem=recv,
                                        device_id=device, device_id_type=pl.DeviceIdType.MESH)


def attention_kernel(q_ref, k_ref, v_ref, seg_ref, out_ref, q_buf, v_buf, seg_in, seg_buf, vt_buf, qt_buf,
                     kv, qe, acc, peak, first, o_buf, load_sem,
                     y_send, y_recv, q_send, q_recv, z_send, z_recv, x_send, x_recv,
                     side_send, side_recv, ready, o_send, o_recv):
    me, x, y, z = place()
    core = lax.axis_index("kvh")
    half = NZ // 2

    def dev(x_, y_, z_):
        return (index_of(x_, y_, z_), core)

    y_peers = [lax.rem(y + d, NY) for d in range(1, NY)]
    z_next, z_prev = lax.rem(z + 1, NZ), lax.rem(z + NZ - 1, NZ)
    x_next, x_prev = lax.rem(x + 1, NX), lax.rem(x + NX - 1, NX)
    barrier = pltpu.get_barrier_semaphore()
    friends = ([dev(x, p, z) for p in y_peers] + [(index_of(x, p, z), 1 - core) for p in [y] + y_peers]
               + [dev(x, y, z_next), dev(x, y, z_prev)])
    for friend in friends:
        pl.semaphore_signal(barrier, inc=1, device_id=friend, device_id_type=pl.DeviceIdType.MESH)

    @pl.when(x < NX - 1)
    def _():
        pl.semaphore_signal(barrier, inc=1, device_id=dev(x_next, y, z), device_id_type=pl.DeviceIdType.MESH)
    load_v = pltpu.make_async_copy(v_ref, v_buf, load_sem.at[0])
    load_q = pltpu.make_async_copy(q_ref, q_buf, load_sem.at[1])
    load_ids = pltpu.make_async_copy(seg_ref, seg_in, load_sem.at[2])
    load_ids.start()
    load_v.start()
    load_q.start()

    load_ids.wait()
    ids = seg_in[...].astype(jnp.float32)
    line = lax.broadcasted_iota(jnp.int32, (16, 128), 0)
    ids = jnp.where(line == 0, ids[0:1], jnp.where(line == 1, ids[1:2], FAR_ID))
    seg_buf[...] = ids.astype(jnp.bfloat16)
    def slot(row, shift):
        return (BACK + row) * NZ + lax.rem(z + shift + NZ, NZ)

    def head_cols(p):
        return pl.ds(pl.multiple_of(p * DIM, DIM), DIM)

    mine = (BACK + y) * NZ + z
    pltpu.make_async_copy(k_ref.at[:, head_cols(y)], kv.at[mine, pl.ds(0, TOK)], y_recv.at[y]).start()
    pltpu.make_async_copy(seg_buf, kv.at[mine, pl.ds(2 * TOK, 16)], y_recv.at[y]).start()
    pl.semaphore_wait(barrier, len(friends) + jnp.where(x > 0, 1, 0))

    @pl.when(x > 0)
    def _():
        pl.semaphore_signal(ready, inc=1, device_id=dev(x_prev, y, z), device_id_type=pl.DeviceIdType.MESH)

    sent = []

    def to_peers(i, src_of, lo, rows):
        for n, p in enumerate(y_peers):
            copy = remote(src_of(p), kv.at[mine, pl.ds(lo, rows)], y_send.at[n, i], y_recv.at[y], dev(x, p, z))
            copy.start()
            sent.append(copy)

    to_peers(0, lambda p: k_ref.at[:, head_cols(p)], 0, TOK)
    to_peers(2, lambda p: seg_buf, 2 * TOK, 16)
    load_v.wait()
    for p in range(NY):
        turned = v_buf[:, p * DIM:(p + 1) * DIM].T
        vt_buf[p, :DIM, :] = turned[:, :DIM]
        vt_buf[p, DIM:, :] = turned[:, DIM:]
    pltpu.make_async_copy(vt_buf.at[y], kv.at[mine, pl.ds(TOK, TOK)], y_recv.at[y]).start()
    to_peers(1, lambda p: vt_buf.at[p], TOK, TOK)

    def shift_of(way, step):
        return step * (2 * way - 1)

    def z_copy(way, row, step):
        at = kv.at[slot(row, shift_of(way, step - 1))]
        neighbour = jnp.where(way == 0, z_next, z_prev)
        return remote(at, at, z_send.at[way, row, step - 1], z_recv.at[way, row, step - 1], dev(x, y, neighbour))

    def x_copy(row, way, step):
        shift = shift_of(way, step)
        return remote(kv.at[slot(row, shift)], kv.at[slot(row - NY, shift)], x_send.at[row - NY + BACK, way, step],
                      x_recv.at[row - NY + BACK, way, step], dev(x_next, y, z))

    def last_way(row):
        return lax.rem(row + 1, 2)

    def row2_over_x(way, step):
        return (lax.rem(z + shift_of(way, step) + NZ, NZ) >= z) & (step != 1)

    def over_x(way, row, step):
        return (row == NY - 1) | ((row == NY - 2) & row2_over_x(way, step))

    def forward(way, row, step):
        @pl.when(over_x(way, row, step) & (x < NX - 1))
        def _():
            x_copy(row, way, step).start()

    def pass_on(way, row, step):
        @pl.when((step < half - 1) | ((step == half - 1) & (way == last_way(row))))
        def _():
            z_copy(way, row, step + 1).start()
        forward(way, row, step)

    def side_copy(way):
        at = kv.at[slot(-BACK, 0)]
        return remote(at, at, side_send.at[way], side_recv.at[way], dev(x, y, z_prev if way else z_next))

    def side_goes(way):
        return (x > 0) & ((z >= 1) if way else (z == NZ - 1))

    def side_comes(way):
        return (x > 0) & ((z < NZ - 1) if way else (z == 0))

    def row_of(i):
        return lax.rem(y + jnp.where(i == 0, 0, jnp.where(i == 1, 1, jnp.where(i == 2, NY - 1, 2))), NY)

    def first_sends(i, _):
        row = row_of(i)
        at = kv.at[slot(row, 0)]
        pltpu.make_async_copy(at, at, y_recv.at[row]).wait()
        z_copy(0, row, 1).start()
        z_copy(1, row, 1).start()
        return 0

    lax.fori_loop(0, NY, first_sends, 0)

    @pl.when(x < NX - 1)
    def _():
        pl.semaphore_wait(ready, 1)
    forward(0, NY - 1, 0)
    forward(0, NY - 2, 0)
    load_q.wait()
    for p in range(NY):
        for g in range(GROUP):
            h = p * GROUP + g
            qt_buf[p, :, g * TOK:(g + 1) * TOK] = q_buf[:, h * DIM:(h + 1) * DIM].T
    asked = []
    for n, p in enumerate(y_peers):
        copy = remote(qt_buf.at[p], qe.at[y, pl.ds(0, DIM)], q_send.at[n], q_recv.at[n], dev(x, p, z))
        copy.start()
        asked.append(copy)
    own_q = pltpu.make_async_copy(qt_buf.at[y], qe.at[y, pl.ds(0, DIM)], q_send.at[NY - 1])
    own_q.start()

    @pl.when(x == 0)
    def _():
        def blank(at, _):
            kv[at, :2 * TOK, :] = jnp.zeros((2 * TOK, DIM), jnp.bfloat16)
            kv[at, 2 * TOK:, :] = jnp.full((16, DIM), -1.0, jnp.bfloat16)
            return 0

        lax.fori_loop(0, BACK * NZ, blank, 0)

    def arrive(i, step):
        row = row_of(i)
        for way in range(2):
            @pl.when((step < half) | (way == last_way(row)))
            def _():
                z_copy(way, row, step).wait_recv()
                pass_on(way, row, step)

    def first_step(i, _):
        arrive(i, 1)
        return 0

    lax.fori_loop(0, NY, first_step, 0)

    def wait_x(row, way, step):
        @pl.when(over_x(way, row, step) & (x > 0))
        def _():
            x_copy(row, way, step).wait_recv()

    for row in (NY - 1, NY - 2):
        wait_x(row, 0, 0)
    for way in range(2):
        @pl.when(side_goes(way))
        def _():
            side_copy(way).start()
    for copy in asked:
        copy.wait_recv()
    own_q.wait()

    key = lax.broadcasted_iota(jnp.int32, (TOK, TOK), 0)
    token = lax.broadcasted_iota(jnp.int32, (TOK, TOK), 1)

    lane = lax.broadcasted_iota(jnp.int32, (TOK, DIM), 1)
    line = lax.broadcasted_iota(jnp.int32, (TOK, DIM), 0)
    plain = jnp.where(lane == 1, 1.0, 0.0)

    def early_keys(at, b):
        there = kv[at, 2 * TOK:, :].astype(jnp.float32)
        less = jnp.where(there < first[b, 0:1, :], 1.0, 0.0)
        count = jnp.sum(jnp.sum(less, axis=0, keepdims=True), axis=1, keepdims=True).astype(jnp.int32)
        extra = jnp.where((lane == 0) & (line < count), NEG, plain).astype(jnp.bfloat16)
        return jnp.concatenate([kv[at, :TOK, :], extra], axis=1)

    def own_keys(at):
        return jnp.concatenate([kv[at, :TOK, :], jnp.zeros((TOK, DIM), jnp.bfloat16)], axis=1)

    def turned_values(slots):
        vt = jnp.concatenate([kv[at, lo:lo + DIM, :] for at in slots for lo in (TOK, TOK + DIM)], axis=1)
        return jnp.concatenate([vt, jnp.ones((16, vt.shape[1]), jnp.bfloat16)], axis=0)

    def chains(jobs):
        todo = [(b, slice(g * WIDE, (g + 1) * WIDE), keys, vt, bias, going)
                for b, keys, vt, bias, going in jobs for g in range(LANES // WIDE)]

        def scores_of(b, cols, keys, vt, bias, going):
            return jnp.dot(keys, qe[b, :, cols], preferred_element_type=jnp.float32)

        ahead = scores_of(*todo[0])
        for i, (b, cols, keys, vt, bias, going) in enumerate(todo):
            s = ahead
            if i + 1 < len(todo):
                ahead = scores_of(*todo[i + 1])
            if bias is not None:
                s = jnp.concatenate([s[:TOK] + bias, s[TOK:]], axis=0)
            new = jnp.max(s, axis=0, keepdims=True)
            if going:
                old = peak[b, 0:1, cols]
                new = jnp.maximum(old, new)
                fade = jnp.exp2((old - new) * SCALE)
            w = jnp.exp2(s * SCALE - new * SCALE).astype(jnp.bfloat16)
            o = jnp.dot(vt, w, preferred_element_type=jnp.float32)
            peak[b, 0:1, cols] = new
            acc[b, :, cols] = acc[b, :, cols] * fade + o if going else o

    def own_work(j, _):
        jobs = []
        for i in (1, 0):
            b = NY - 2 - 2 * j + i
            at = slot(b, 0)
            own = kv[at, 2 * TOK:, :].astype(jnp.float32)
            row = jnp.concatenate([own[0:1], own[1:2]], axis=1)
            rows = jnp.broadcast_to(row, (TOK, TOK))
            begin = row[:, 0:1]
            first[b] = jnp.broadcast_to(begin, (8, 128))
            rest = jnp.concatenate([jnp.where(row == begin, 0.0, NEG)] * GROUP, axis=1)
            which = lax.broadcasted_iota(jnp.int32, (DIM, LANES), 0)
            qe[b, DIM:, :] = jnp.where(which == 0, 1.0, jnp.where(which == 1, rest, 0.0)).astype(jnp.bfloat16)
            bias = jnp.concatenate([jnp.where((rows == rows.T) & (key <= token), 0.0, NEG)] * (WIDE // TOK), axis=1)
            early = [slot(b - 1, 0), slot(b - 2, 0)]
            keys = jnp.concatenate([own_keys(at)] + [early_keys(one, b) for one in early], axis=0)
            jobs.append((b, keys, turned_values([at] + early), bias, False))
        chains(jobs)
        return 0

    lax.fori_loop(0, NY // 2, own_work, 0)

    def pair_work(pair, ways, step):
        jobs = []
        for i in (1, 0):
            b = 2 * pair + i
            slots = []
            for way in ways:
                shift = shift_of(way, step)
                there = lax.rem(z + shift + NZ, NZ)
                slots += [slot(b - 1, shift), slot(jnp.where(there < z, b, b - 2), shift)]
            keys = jnp.concatenate([early_keys(at, b) for at in slots], axis=0)
            jobs.append((b, keys, turned_values(slots), None, True))
        chains(jobs)

    def wait_for_x(step):
        for way in range(2):
            for row in (NY - 1, NY - 2):
                wait_x(row, way, step)

            @pl.when((step == 1) & side_comes(way))
            def _():
                side_copy(way).wait_recv()

    def later_step(step, _):
        def catch_up(j, _):
            @pl.when(step < half - 1)
            def _():
                arrive(2 * j, step + 1)
                arrive(2 * j + 1, step + 1)

            @pl.when((step > 1) & (j == 1))
            def _():
                wait_for_x(step - 1)

            @pl.when((step > 1) | (j == 0))
            def _():
                pair_work(1 - j, (0, 1), step - j)
            return 0

        lax.fori_loop(0, 2, catch_up, 0)
        return 0

    lax.fori_loop(1, half, later_step, 0)

    def last_step(i, _):
        arrive(i, half)
        return 0

    lax.fori_loop(0, NY, last_step, 0)

    rows = TOK // 2
    wide = GROUP * DIM
    cols = out_ref.at[:, pl.ds(pl.multiple_of((core * NY + y) * wide, wide), wide)]

    def part(b, c):
        return o_buf.at[b, pl.ds(pl.multiple_of(c * rows, rows), rows)]

    def over(b):
        return remote(part(b, 1 - core), cols, o_send.at[b, 1], o_recv.at[y, 1], (index_of(x, b, z), 1 - core))

    def along(b):
        return remote(part(b, core), cols, o_send.at[b, 0], o_recv.at[y, 0], (index_of(x, b, z), core))

    def stay(b):
        return pltpu.make_async_copy(part(b, core), cols, o_recv.at[y, 0])

    def send_back(b):
        mixed = (acc[b, :DIM, :] * (1.0 / acc[b, DIM:DIM + 1, :])).astype(jnp.bfloat16)
        for g in range(GROUP):
            o_buf[b, :, g * DIM:(g + 1) * DIM] = mixed[:, g * TOK:(g + 1) * TOK].T
        over(b).start()

        @pl.when(b != y)
        def _():
            along(b).start()

        @pl.when(b == y)
        def _():
            stay(b).start()

    def finish(j, _):
        @pl.when(j == 1)
        def _():
            wait_for_x(half - 1)
            pair_work(0, (0, 1), half - 1)
            for row in (NY - 1, NY - 2):
                wait_x(row, last_way(row), half)
        pair_work(1 - j, (0,), half)
        for i in (1, 0):
            send_back(2 * (1 - j) + i)
        return 0

    lax.fori_loop(0, 2, finish, 0)

    for copy in sent + asked:
        copy.wait_send()

    def z_drain(j, _):
        row, way, step = j // (2 * half), (j // half) % 2, 1 + j % half

        @pl.when((step < half) | (way == last_way(row)))
        def _():
            z_copy(way, row, step).wait_send()
        return 0

    lax.fori_loop(0, 2 * NY * half, z_drain, 0)

    def x_drain(j, _):
        row, way, step = NY - 1 - j // (2 * (half + 1)), (j // (half + 1)) % 2, j % (half + 1)
        there_is = jnp.where(step == 0, way == 0, (step < half) | (way == last_way(row)))

        @pl.when(there_is & over_x(way, row, step) & (x < NX - 1))
        def _():
            x_copy(row, way, step).wait_send()
        return 0

    lax.fori_loop(0, 2 * BACK * (half + 1), x_drain, 0)
    for way in range(2):
        @pl.when(side_goes(way))
        def _():
            side_copy(way).wait_send()
    for b in range(NY):
        over(b).wait_send()

        @pl.when(b != y)
        def _():
            along(b).wait_send()
        for e in range(2):
            pltpu.make_async_copy(part(b, core), cols, o_recv.at[b, e]).wait()


def per_device(queries, keys, values, segment_ids):
    any_spec = pl.BlockSpec(memory_space=pl.ANY)
    hbm_spec = pl.BlockSpec(memory_space=pltpu.HBM)
    dma = pltpu.SemaphoreType.DMA
    bf16, f32 = jnp.bfloat16, jnp.float32
    half = NZ // 2
    return pl.pallas_call(
        attention_kernel,
        out_shape=jax.ShapeDtypeStruct((TOK // 2, 2 * NY * GROUP * DIM), bf16),
        in_specs=[hbm_spec] * 4,
        out_specs=any_spec,
        scratch_shapes=[
            pltpu.VMEM(queries.shape, bf16), pltpu.VMEM(values.shape, bf16), pltpu.VMEM((2, 128), jnp.int32), pltpu.VMEM((16, 128), bf16),
            pltpu.VMEM((NY, 2 * DIM, TOK // 2), bf16), pltpu.VMEM((NY, DIM, LANES), bf16),
            pltpu.VMEM((SLOTS, SLOT_ROWS, DIM), bf16),
            pltpu.VMEM((NY, 2 * DIM, LANES), bf16), pltpu.VMEM((NY, DIM + 16, LANES), f32), pltpu.VMEM((NY, 8, LANES), f32),
            pltpu.VMEM((NY, 8, 128), f32), pltpu.VMEM((NY, TOK, GROUP * DIM), bf16),
            dma((3,)), dma((NY - 1, 3)), dma((NY,)), dma((NY,)), dma((NY - 1,)),
            dma((2, NY, half)), dma((2, NY, half)), dma((BACK, 2, half + 1)), dma((BACK, 2, half + 1)),
            dma((2,)), dma((2,)), pltpu.SemaphoreType.REGULAR, dma((NY, 2)), dma((NY, 2))],
        compiler_params=pltpu.CompilerParams(collective_id=0, has_side_effects=True,
                                             vmem_limit_bytes=40 * 1024 * 1024),
        name="attention",
    )(*(pltpu.with_memory_space_constraint(one, pltpu.HBM) for one in
        (queries, keys, values, segment_ids.reshape(2, 128))))


def solution(mesh):
    return jax.shard_map(
        per_device,
        mesh=mesh,
        in_specs=(P("ctx", "kvh"), P("ctx", "kvh"), P("ctx", "kvh"), P("ctx")),
        out_specs=P(("ctx", "kvh"), None),
        check_vma=False,
    )
```

```python
import jax
import jax.numpy as jnp
from jax import lax
from jax.experimental import pallas as pl
from jax.experimental.pallas import tpu as pltpu
from jax.sharding import PartitionSpec as P

NX, NY, NZ = 4, 4, 8
TOK = 256
DIM = 128
GROUP = 4
BACK = 2
ROWS = NY + BACK
SLOTS = ROWS * NZ
SLOT_ROWS = 2 * TOK + 16
LANES = GROUP * TOK
WIDE = 2 * TOK
NEG = -1e30
FAR_ID = 512.0
SCALE = 1.4426950408889634 * DIM ** -0.5


def place():
    me = lax.axis_index("ctx")
    return me, me // (NY * NZ), (me // NZ) % NY, me % NZ


def index_of(x, y, z):
    return (x * NY + y) * NZ + z


def remote(src, dst, send, recv, device):
    return pltpu.make_async_remote_copy(src_ref=src, dst_ref=dst, send_sem=send, recv_sem=recv,
                                        device_id=device, device_id_type=pl.DeviceIdType.MESH)


def attention_kernel(q_ref, k_ref, v_ref, seg_ref, out_ref, q_buf, v_buf, seg_in, seg_buf, vt_buf, qt_buf,
                     kv, qe, acc, peak, first, o_buf, load_sem,
                     y_send, y_recv, q_send, q_recv, z_send, z_recv, x_send, x_recv,
                     side_send, side_recv, ready, o_send, o_recv,
                     k_box, v_box, q_box, o_box, r_send, r_recv, f_send):
    me, x, y, z = place()
    core = lax.axis_index("kvh")
    half = NZ // 2

    def dev(x_, y_, z_):
        return (index_of(x_, y_, z_), core)

    y_peers = [lax.rem(y + d, NY) for d in range(1, NY)]
    z_next, z_prev = lax.rem(z + 1, NZ), lax.rem(z + NZ - 1, NZ)
    x_next, x_prev = lax.rem(x + 1, NX), lax.rem(x + NX - 1, NX)
    barrier = pltpu.get_barrier_semaphore()
    friends = ([dev(x, p, z) for p in y_peers] + [(index_of(x, p, z), 1 - core) for p in [y] + y_peers]
               + [dev(x, y, z_next), dev(x, y, z_prev)])
    for friend in friends:
        pl.semaphore_signal(barrier, inc=1, device_id=friend, device_id_type=pl.DeviceIdType.MESH)

    @pl.when(x < NX - 1)
    def _():
        pl.semaphore_signal(barrier, inc=1, device_id=dev(x_next, y, z), device_id_type=pl.DeviceIdType.MESH)
    load_v = pltpu.make_async_copy(v_ref, v_buf, load_sem.at[0])
    load_q = pltpu.make_async_copy(q_ref, q_buf, load_sem.at[1])
    load_ids = pltpu.make_async_copy(seg_ref, seg_in, load_sem.at[2])
    load_ids.start()
    load_v.start()
    load_q.start()

    load_ids.wait()
    ids = seg_in[...].astype(jnp.float32)
    line = lax.broadcasted_iota(jnp.int32, (16, 128), 0)
    ids = jnp.where(line == 0, ids[0:1], jnp.where(line == 1, ids[1:2], FAR_ID))
    seg_buf[...] = ids.astype(jnp.bfloat16)
    def slot(row, shift):
        return (BACK + row) * NZ + lax.rem(z + shift + NZ, NZ)

    def head_cols(p):
        return pl.ds(pl.multiple_of(p * DIM, DIM), DIM)

    mine = (BACK + y) * NZ + z
    pltpu.make_async_copy(k_ref.at[:, head_cols(y)], kv.at[mine, pl.ds(0, TOK)], y_recv.at[y]).start()
    pltpu.make_async_copy(seg_buf, kv.at[mine, pl.ds(2 * TOK, 16)], y_recv.at[y]).start()
    pl.semaphore_wait(barrier, len(friends) + jnp.where(x > 0, 1, 0))

    @pl.when(x > 0)
    def _():
        pl.semaphore_signal(ready, inc=1, device_id=dev(x_prev, y, z), device_id_type=pl.DeviceIdType.MESH)

    up, across, down = y_peers
    sent = []

    def through(part, src, box):
        return remote(src, box, r_send.at[part], r_recv.at[part], dev(x, down if part % 2 else up, z))

    def direct(i, src, lo, rows, n):
        copy = remote(src, kv.at[mine, pl.ds(lo, rows)], y_send.at[n, i], y_recv.at[y], dev(x, y_peers[n], z))
        copy.start()
        sent.append(copy)

    def send(copy):
        copy.start()
        sent.append(copy)

    send(through(0, k_ref.at[:, head_cols(across)], k_box))
    for n in (0, 2):
        direct(0, k_ref.at[:, head_cols(y_peers[n])], 0, TOK, n)
    load_v.wait()
    for p in range(NY):
        turned = v_buf[:, p * DIM:(p + 1) * DIM].T
        vt_buf[p, :DIM, :] = turned[:, :DIM]
        vt_buf[p, DIM:, :] = turned[:, DIM:]
    pltpu.make_async_copy(vt_buf.at[y], kv.at[mine, pl.ds(TOK, TOK)], y_recv.at[y]).start()
    send(through(1, vt_buf.at[across], v_box))
    for n in (0, 2):
        direct(1, vt_buf.at[y_peers[n]], TOK, TOK, n)
    for n in range(NY - 1):
        direct(2, seg_buf, 2 * TOK, 16, n)

    def shift_of(way, step):
        return step * (2 * way - 1)

    def z_copy(way, row, step):
        at = kv.at[slot(row, shift_of(way, step - 1))]
        neighbour = jnp.where(way == 0, z_next, z_prev)
        return remote(at, at, z_send.at[way, row, step - 1], z_recv.at[way, row, step - 1], dev(x, y, neighbour))

    def x_copy(row, way, step):
        shift = shift_of(way, step)
        return remote(kv.at[slot(row, shift)], kv.at[slot(row - NY, shift)], x_send.at[row - NY + BACK, way, step],
                      x_recv.at[row - NY + BACK, way, step], dev(x_next, y, z))

    def last_way(row):
        return lax.rem(row + 1, 2)

    def row2_over_x(way, step):
        return (lax.rem(z + shift_of(way, step) + NZ, NZ) >= z) & (step != 1)

    def over_x(way, row, step):
        return (row == NY - 1) | ((row == NY - 2) & row2_over_x(way, step))

    def forward(way, row, step):
        @pl.when(over_x(way, row, step) & (x < NX - 1))
        def _():
            x_copy(row, way, step).start()

    def pass_on(way, row, step):
        @pl.when((step < half - 1) | ((step == half - 1) & (way == last_way(row))))
        def _():
            z_copy(way, row, step + 1).start()
        forward(way, row, step)

    def side_copy(way):
        at = kv.at[slot(-BACK, 0)]
        return remote(at, at, side_send.at[way], side_recv.at[way], dev(x, y, z_prev if way else z_next))

    def side_goes(way):
        return (x > 0) & ((z >= 1) if way else (z == NZ - 1))

    def side_comes(way):
        return (x > 0) & ((z < NZ - 1) if way else (z == 0))

    def row_of(i):
        return lax.rem(y + jnp.where(i == 0, 0, jnp.where(i == 1, 1, jnp.where(i == 2, NY - 1, 2))), NY)

    def first_sends(i, _):
        row = row_of(i)
        at = kv.at[slot(row, 0)]
        pltpu.make_async_copy(at, at, y_recv.at[row]).wait()
        z_copy(0, row, 1).start()
        z_copy(1, row, 1).start()
        return 0

    lax.fori_loop(0, 1, first_sends, 0)
    load_q.wait()
    for p in range(NY):
        for g in range(GROUP):
            h = p * GROUP + g
            qt_buf[p, :, g * TOK:(g + 1) * TOK] = q_buf[:, h * DIM:(h + 1) * DIM].T

    def pass_through(part, box, dst, recv, device):
        pltpu.make_async_copy(box, box, r_recv.at[part]).wait()
        send(remote(box, dst, f_send.at[part], recv, device))

    up_dev, down_dev = dev(x, up, z), dev(x, down, z)
    pass_through(0, k_box, kv.at[slot(down, 0), pl.ds(0, TOK)], y_recv.at[down], up_dev)
    pass_through(1, v_box, kv.at[slot(up, 0), pl.ds(TOK, TOK)], y_recv.at[up], down_dev)
    lax.fori_loop(1, NY, first_sends, 0)

    @pl.when(x < NX - 1)
    def _():
        pl.semaphore_wait(ready, 1)
    forward(0, NY - 1, 0)
    forward(0, NY - 2, 0)
    part_rows = DIM // 2
    send(through(2, qt_buf.at[across, pl.ds(0, part_rows)], q_box.at[0]))
    send(through(3, qt_buf.at[across, pl.ds(part_rows, part_rows)], q_box.at[1]))
    asked = []
    for n in (0, 2):
        copy = remote(qt_buf.at[y_peers[n]], qe.at[y, pl.ds(0, DIM)], q_send.at[n], q_recv.at[n], dev(x, y_peers[n], z))
        copy.start()
        asked.append(copy)
    own_q = pltpu.make_async_copy(qt_buf.at[y], qe.at[y, pl.ds(0, DIM)], q_send.at[NY - 1])
    own_q.start()

    @pl.when(x == 0)
    def _():
        def blank(at, _):
            kv[at, :2 * TOK, :] = jnp.zeros((2 * TOK, DIM), jnp.bfloat16)
            kv[at, 2 * TOK:, :] = jnp.full((16, DIM), -1.0, jnp.bfloat16)
            return 0

        lax.fori_loop(0, BACK * NZ, blank, 0)

    def arrive(i, step):
        row = row_of(i)
        for way in range(2):
            @pl.when((step < half) | (way == last_way(row)))
            def _():
                z_copy(way, row, step).wait_recv()
                pass_on(way, row, step)

    def first_step(i, _):
        arrive(i, 1)
        return 0

    lax.fori_loop(0, 2, first_step, 0)
    pass_through(2, q_box.at[0], qe.at[down, pl.ds(0, part_rows)], q_recv.at[1], up_dev)
    pass_through(3, q_box.at[1], qe.at[up, pl.ds(part_rows, part_rows)], q_recv.at[1], down_dev)
    lax.fori_loop(2, NY, first_step, 0)

    def wait_x(row, way, step):
        @pl.when(over_x(way, row, step) & (x > 0))
        def _():
            x_copy(row, way, step).wait_recv()

    for row in (NY - 1, NY - 2):
        wait_x(row, 0, 0)
    for way in range(2):
        @pl.when(side_goes(way))
        def _():
            side_copy(way).start()
    for copy in asked:
        copy.wait_recv()
    far_q = qe.at[across, pl.ds(0, DIM)]
    pltpu.make_async_copy(far_q, far_q, q_recv.at[1]).wait()
    own_q.wait()

    key = lax.broadcasted_iota(jnp.int32, (TOK, TOK), 0)
    token = lax.broadcasted_iota(jnp.int32, (TOK, TOK), 1)

    lane = lax.broadcasted_iota(jnp.int32, (TOK, DIM), 1)
    line = lax.broadcasted_iota(jnp.int32, (TOK, DIM), 0)
    plain = jnp.where(lane == 1, 1.0, 0.0)

    def early_keys(at, b):
        there = kv[at, 2 * TOK:, :].astype(jnp.float32)
        less = jnp.where(there < first[b, 0:1, :], 1.0, 0.0)
        count = jnp.sum(jnp.sum(less, axis=0, keepdims=True), axis=1, keepdims=True).astype(jnp.int32)
        extra = jnp.where((lane == 0) & (line < count), NEG, plain).astype(jnp.bfloat16)
        return jnp.concatenate([kv[at, :TOK, :], extra], axis=1)

    def own_keys(at):
        return jnp.concatenate([kv[at, :TOK, :], jnp.zeros((TOK, DIM), jnp.bfloat16)], axis=1)

    def turned_values(slots):
        vt = jnp.concatenate([kv[at, lo:lo + DIM, :] for at in slots for lo in (TOK, TOK + DIM)], axis=1)
        return jnp.concatenate([vt, jnp.ones((16, vt.shape[1]), jnp.bfloat16)], axis=0)

    def chains(jobs):
        todo = [(b, slice(g * WIDE, (g + 1) * WIDE), keys, vt, bias, going)
                for b, keys, vt, bias, going in jobs for g in range(LANES // WIDE)]

        def scores_of(b, cols, keys, vt, bias, going):
            return jnp.dot(keys, qe[b, :, cols], preferred_element_type=jnp.float32)

        ahead = scores_of(*todo[0])
        for i, (b, cols, keys, vt, bias, going) in enumerate(todo):
            s = ahead
            if i + 1 < len(todo):
                ahead = scores_of(*todo[i + 1])
            if bias is not None:
                s = jnp.concatenate([s[:TOK] + bias, s[TOK:]], axis=0)
            new = jnp.max(s, axis=0, keepdims=True)
            if going:
                old = peak[b, 0:1, cols]
                new = jnp.maximum(old, new)
                fade = jnp.exp2((old - new) * SCALE)
            w = jnp.exp2(s * SCALE - new * SCALE).astype(jnp.bfloat16)
            o = jnp.dot(vt, w, preferred_element_type=jnp.float32)
            peak[b, 0:1, cols] = new
            acc[b, :, cols] = acc[b, :, cols] * fade + o if going else o

    def own_work(j, _):
        jobs = []
        for i in (1, 0):
            b = NY - 2 - 2 * j + i
            at = slot(b, 0)
            own = kv[at, 2 * TOK:, :].astype(jnp.float32)
            row = jnp.concatenate([own[0:1], own[1:2]], axis=1)
            rows = jnp.broadcast_to(row, (TOK, TOK))
            begin = row[:, 0:1]
            first[b] = jnp.broadcast_to(begin, (8, 128))
            rest = jnp.concatenate([jnp.where(row == begin, 0.0, NEG)] * GROUP, axis=1)
            which = lax.broadcasted_iota(jnp.int32, (DIM, LANES), 0)
            qe[b, DIM:, :] = jnp.where(which == 0, 1.0, jnp.where(which == 1, rest, 0.0)).astype(jnp.bfloat16)
            bias = jnp.concatenate([jnp.where((rows == rows.T) & (key <= token), 0.0, NEG)] * (WIDE // TOK), axis=1)
            early = [slot(b - 1, 0), slot(b - 2, 0)]
            keys = jnp.concatenate([own_keys(at)] + [early_keys(one, b) for one in early], axis=0)
            jobs.append((b, keys, turned_values([at] + early), bias, False))
        chains(jobs)
        arrive(2 * j, 2)
        arrive(2 * j + 1, 2)
        return 0

    lax.fori_loop(0, NY // 2, own_work, 0)

    def pair_work(pair, ways, step):
        jobs = []
        for i in (1, 0):
            b = 2 * pair + i
            slots = []
            for way in ways:
                shift = shift_of(way, step)
                there = lax.rem(z + shift + NZ, NZ)
                slots += [slot(b - 1, shift), slot(jnp.where(there < z, b, b - 2), shift)]
            keys = jnp.concatenate([early_keys(at, b) for at in slots], axis=0)
            jobs.append((b, keys, turned_values(slots), None, True))
        chains(jobs)

    def wait_for_x(step):
        for way in range(2):
            for row in (NY - 1, NY - 2):
                wait_x(row, way, step)

            @pl.when((step == 1) & side_comes(way))
            def _():
                side_copy(way).wait_recv()

    def later_step(step, _):
        def catch_up(j, _):
            @pl.when(j == 1)
            def _():
                wait_for_x(step)
            pair_work(1 - j, (0, 1), step)

            @pl.when(step < half - 1)
            def _():
                arrive(2 * j, step + 2)
                arrive(2 * j + 1, step + 2)
            return 0

        lax.fori_loop(0, 2 - step // (half - 1), catch_up, 0)
        return 0

    lax.fori_loop(1, half, later_step, 0)

    rows = TOK // 2
    wide = GROUP * DIM
    cols = out_ref.at[:, pl.ds(pl.multiple_of((core * NY + y) * wide, wide), wide)]

    def part(b, c):
        return o_buf.at[b, pl.ds(pl.multiple_of(c * rows, rows), rows)]

    def over(b):
        return remote(part(b, 1 - core), cols, o_send.at[b, 1], o_recv.at[y, 1], (index_of(x, b, z), 1 - core))

    def along(b):
        return remote(part(b, core), cols, o_send.at[b, 0], o_recv.at[y, 0], (index_of(x, b, z), core))

    def stay(b):
        return pltpu.make_async_copy(part(b, core), cols, o_recv.at[y, 0])

    def send_back(b):
        mixed = (acc[b, :DIM, :] * (1.0 / acc[b, DIM:DIM + 1, :])).astype(jnp.bfloat16)
        for g in range(GROUP):
            o_buf[b, :, g * DIM:(g + 1) * DIM] = mixed[:, g * TOK:(g + 1) * TOK].T

        @pl.when(b == across)
        def _():
            through(4, part(b, core), o_box.at[0]).start()
            through(5, part(b, 1 - core), o_box.at[1]).start()

        @pl.when(b != across)
        def _():
            over(b).start()

        @pl.when((b != across) & (b != y))
        def _():
            along(b).start()

        @pl.when(b == y)
        def _():
            stay(b).start()

    def cols_of(source):
        return out_ref.at[:, pl.ds(pl.multiple_of((core * NY + source) * wide, wide), wide)]

    def output_through(part):
        pltpu.make_async_copy(o_box.at[part - 4], o_box.at[part - 4], r_recv.at[part]).wait()
        output_on(part).start()

    def output_on(part):
        if part == 4:
            return remote(o_box.at[0], cols_of(down), f_send.at[4], o_recv.at[down, 0], up_dev)
        return remote(o_box.at[1], cols_of(up), f_send.at[5], o_recv.at[up, 1], (index_of(x, down, z), 1 - core))

    early = (y == 1) | (y == 2)

    def finish(j, _):
        @pl.when(j == 1)
        def _():
            wait_for_x(half - 1)
            pair_work(0, (0, 1), half - 1)

            @pl.when(early)
            def _():
                output_through(4)

            @pl.when(jnp.logical_not(early))
            def _():
                output_through(5)
            for row in (NY - 1, NY - 2):
                wait_x(row, last_way(row), half)
        pair_work(1 - j, (0,), half)
        for i in (1, 0):
            send_back(2 * (1 - j) + i)
        return 0

    lax.fori_loop(0, 2, finish, 0)

    @pl.when(early)
    def _():
        output_through(5)

    @pl.when(jnp.logical_not(early))
    def _():
        output_through(4)

    for copy in sent + asked:
        copy.wait_send()

    def z_drain(j, _):
        row, way, step = j // (2 * half), (j // half) % 2, 1 + j % half

        @pl.when((step < half) | (way == last_way(row)))
        def _():
            z_copy(way, row, step).wait_send()
        return 0

    lax.fori_loop(0, 2 * NY * half, z_drain, 0)

    def x_drain(j, _):
        row, way, step = NY - 1 - j // (2 * (half + 1)), (j // (half + 1)) % 2, j % (half + 1)
        there_is = jnp.where(step == 0, way == 0, (step < half) | (way == last_way(row)))

        @pl.when(there_is & over_x(way, row, step) & (x < NX - 1))
        def _():
            x_copy(row, way, step).wait_send()
        return 0

    lax.fori_loop(0, 2 * BACK * (half + 1), x_drain, 0)
    for way in range(2):
        @pl.when(side_goes(way))
        def _():
            side_copy(way).wait_send()
    through(4, part(across, core), o_box.at[0]).wait_send()
    through(5, part(across, 1 - core), o_box.at[1]).wait_send()
    output_on(4).wait_send()
    output_on(5).wait_send()
    for b in range(NY):
        @pl.when(b != across)
        def _():
            over(b).wait_send()

        @pl.when((b != y) & (b != across))
        def _():
            along(b).wait_send()
        for e in range(2):
            pltpu.make_async_copy(part(b, core), cols, o_recv.at[b, e]).wait()


def per_device(queries, keys, values, segment_ids):
    any_spec = pl.BlockSpec(memory_space=pl.ANY)
    hbm_spec = pl.BlockSpec(memory_space=pltpu.HBM)
    dma = pltpu.SemaphoreType.DMA
    bf16, f32 = jnp.bfloat16, jnp.float32
    half = NZ // 2
    return pl.pallas_call(
        attention_kernel,
        out_shape=jax.ShapeDtypeStruct((TOK // 2, 2 * NY * GROUP * DIM), bf16),
        in_specs=[hbm_spec] * 4,
        out_specs=any_spec,
        scratch_shapes=[
            pltpu.VMEM(queries.shape, bf16), pltpu.VMEM(values.shape, bf16), pltpu.VMEM((2, 128), jnp.int32), pltpu.VMEM((16, 128), bf16),
            pltpu.VMEM((NY, 2 * DIM, TOK // 2), bf16), pltpu.VMEM((NY, DIM, LANES), bf16),
            pltpu.VMEM((SLOTS, SLOT_ROWS, DIM), bf16),
            pltpu.VMEM((NY, 2 * DIM, LANES), bf16), pltpu.VMEM((NY, DIM + 16, LANES), f32), pltpu.VMEM((NY, 8, LANES), f32),
            pltpu.VMEM((NY, 8, 128), f32), pltpu.VMEM((NY, TOK, GROUP * DIM), bf16),
            dma((3,)), dma((NY - 1, 3)), dma((NY,)), dma((NY,)), dma((NY - 1,)),
            dma((2, NY, half)), dma((2, NY, half)), dma((BACK, 2, half + 1)), dma((BACK, 2, half + 1)),
            dma((2,)), dma((2,)), pltpu.SemaphoreType.REGULAR, dma((NY, 2)), dma((NY, 2)),
            pltpu.VMEM((TOK, DIM), bf16), pltpu.VMEM((TOK, DIM), bf16), pltpu.VMEM((2, DIM // 2, LANES), bf16),
            pltpu.VMEM((2, TOK // 2, GROUP * DIM), bf16), dma((6,)), dma((6,)), dma((6,))],
        compiler_params=pltpu.CompilerParams(collective_id=0, has_side_effects=True,
                                             vmem_limit_bytes=40 * 1024 * 1024),
        name="attention",
    )(*(pltpu.with_memory_space_constraint(one, pltpu.HBM) for one in
        (queries, keys, values, segment_ids.reshape(2, 128))))


def solution(mesh):
    return jax.shard_map(
        per_device,
        mesh=mesh,
        in_specs=(P("ctx", "kvh"), P("ctx", "kvh"), P("ctx", "kvh"), P("ctx")),
        out_specs=P(("ctx", "kvh"), None),
        check_vma=False,
    )
```

```python
import jax
import jax.numpy as jnp
from jax import lax
from jax.experimental import pallas as pl
from jax.experimental.pallas import tpu as pltpu
from jax.sharding import PartitionSpec as P

NX, NY, NZ = 4, 4, 8
TOK = 256
DIM = 128
GROUP = 4
BACK = 2
ROWS = NY + BACK
SLOTS = ROWS * NZ
SLOT_ROWS = 2 * TOK + 16
LANES = GROUP * TOK
WIDE = TOK
PIECES = 2
NEG = -1e30
FAR_ID = 512.0
SCALE = 1.4426950408889634 * DIM ** -0.5


def place():
    me = lax.axis_index("ctx")
    return me, me // (NY * NZ), (me // NZ) % NY, me % NZ


def index_of(x, y, z):
    return (x * NY + y) * NZ + z


def remote(src, dst, send, recv, device):
    return pltpu.make_async_remote_copy(src_ref=src, dst_ref=dst, send_sem=send, recv_sem=recv,
                                        device_id=device, device_id_type=pl.DeviceIdType.MESH)


def attention_kernel(q_ref, k_ref, v_ref, seg_ref, out_ref, q_buf, v_buf, seg_in, seg_buf, vt_buf, qt_buf,
                     kv, qe, acc, peak, first, o_buf, load_sem,
                     y_send, y_recv, q_send, q_recv, z_send, z_recv, x_send, x_recv,
                     side_send, side_recv, ready, o_send, o_recv,
                     k_box, v_box, q_box, o_box, r_send, r_recv, f_send):
    me, x, y, z = place()
    core = lax.axis_index("kvh")
    half = NZ // 2

    def dev(x_, y_, z_):
        return (index_of(x_, y_, z_), core)

    y_peers = [lax.rem(y + d, NY) for d in range(1, NY)]
    z_next, z_prev = lax.rem(z + 1, NZ), lax.rem(z + NZ - 1, NZ)
    x_next, x_prev = lax.rem(x + 1, NX), lax.rem(x + NX - 1, NX)
    barrier = pltpu.get_barrier_semaphore()
    friends = ([dev(x, p, z) for p in y_peers] + [(index_of(x, p, z), 1 - core) for p in [y] + y_peers]
               + [dev(x, y, z_next), dev(x, y, z_prev)])
    for friend in friends:
        pl.semaphore_signal(barrier, inc=1, device_id=friend, device_id_type=pl.DeviceIdType.MESH)

    @pl.when(x < NX - 1)
    def _():
        pl.semaphore_signal(barrier, inc=1, device_id=dev(x_next, y, z), device_id_type=pl.DeviceIdType.MESH)
    load_v = pltpu.make_async_copy(v_ref, v_buf, load_sem.at[0])
    load_q = pltpu.make_async_copy(q_ref, q_buf, load_sem.at[1])
    load_ids = pltpu.make_async_copy(seg_ref, seg_in, load_sem.at[2])
    load_ids.start()
    load_v.start()
    load_q.start()

    load_ids.wait()
    ids = seg_in[...].astype(jnp.float32)
    line = lax.broadcasted_iota(jnp.int32, (16, 128), 0)
    ids = jnp.where(line == 0, ids[0:1], jnp.where(line == 1, ids[1:2], FAR_ID))
    seg_buf[...] = ids.astype(jnp.bfloat16)
    def slot(row, shift):
        return (BACK + row) * NZ + lax.rem(z + shift + NZ, NZ)

    def head_cols(p):
        return pl.ds(pl.multiple_of(p * DIM, DIM), DIM)

    mine = (BACK + y) * NZ + z
    pltpu.make_async_copy(k_ref.at[:, head_cols(y)], kv.at[mine, pl.ds(0, TOK)], y_recv.at[y]).start()
    pltpu.make_async_copy(seg_buf, kv.at[mine, pl.ds(2 * TOK, 16)], y_recv.at[y]).start()
    pl.semaphore_wait(barrier, len(friends) + jnp.where(x > 0, 1, 0))

    @pl.when(x > 0)
    def _():
        pl.semaphore_signal(ready, inc=1, device_id=dev(x_prev, y, z), device_id_type=pl.DeviceIdType.MESH)

    up, across, down = y_peers
    sent = []

    def through(part, src, box):
        return remote(src, box, r_send.at[part], r_recv.at[part], dev(x, down if part % 2 else up, z))

    def direct(i, src, lo, rows, n):
        copy = remote(src, kv.at[mine, pl.ds(lo, rows)], y_send.at[n, i], y_recv.at[y], dev(x, y_peers[n], z))
        copy.start()
        sent.append(copy)

    def send(copy):
        copy.start()
        sent.append(copy)

    send(through(0, k_ref.at[:, head_cols(across)], k_box))
    for n in (0, 2):
        direct(0, k_ref.at[:, head_cols(y_peers[n])], 0, TOK, n)
    load_v.wait()
    for p in range(NY):
        turned = v_buf[:, p * DIM:(p + 1) * DIM].T
        vt_buf[p, :DIM, :] = turned[:, :DIM]
        vt_buf[p, DIM:, :] = turned[:, DIM:]
    pltpu.make_async_copy(vt_buf.at[y], kv.at[mine, pl.ds(TOK, TOK)], y_recv.at[y]).start()
    send(through(1, vt_buf.at[across], v_box))
    for n in (0, 2):
        direct(1, vt_buf.at[y_peers[n]], TOK, TOK, n)
    for n in range(NY - 1):
        direct(2, seg_buf, 2 * TOK, 16, n)

    def shift_of(way, step):
        return step * (2 * way - 1)

    def z_copy(way, row, step):
        at = kv.at[slot(row, shift_of(way, step - 1))]
        neighbour = jnp.where(way == 0, z_next, z_prev)
        return remote(at, at, z_send.at[way, row, step - 1], z_recv.at[way, row, step - 1], dev(x, y, neighbour))

    def x_copy(row, way, step):
        shift = shift_of(way, step)
        return remote(kv.at[slot(row, shift)], kv.at[slot(row - NY, shift)], x_send.at[row - NY + BACK, way, step],
                      x_recv.at[row - NY + BACK, way, step], dev(x_next, y, z))

    def last_way(row):
        return lax.rem(row + 1, 2)

    def row2_over_x(way, step):
        return (lax.rem(z + shift_of(way, step) + NZ, NZ) >= z) & (step != 1)

    def over_x(way, row, step):
        return (row == NY - 1) | ((row == NY - 2) & row2_over_x(way, step))

    def forward(way, row, step):
        @pl.when(over_x(way, row, step) & (x < NX - 1))
        def _():
            x_copy(row, way, step).start()

    def pass_on(way, row, step):
        @pl.when((step < half - 1) | ((step == half - 1) & (way == last_way(row))))
        def _():
            z_copy(way, row, step + 1).start()
        forward(way, row, step)

    def side_copy(way):
        at = kv.at[slot(-BACK, 0)]
        return remote(at, at, side_send.at[way], side_recv.at[way], dev(x, y, z_prev if way else z_next))

    def side_goes(way):
        return (x > 0) & ((z >= 1) if way else (z == NZ - 1))

    def side_comes(way):
        return (x > 0) & ((z < NZ - 1) if way else (z == 0))

    def row_of(i):
        return lax.rem(y + jnp.where(i == 0, 0, jnp.where(i == 1, 1, jnp.where(i == 2, NY - 1, 2))), NY)

    def first_sends(i, _):
        row = row_of(i)
        at = kv.at[slot(row, 0)]
        pltpu.make_async_copy(at, at, y_recv.at[row]).wait()
        z_copy(0, row, 1).start()
        z_copy(1, row, 1).start()
        return 0

    lax.fori_loop(0, 1, first_sends, 0)
    load_q.wait()
    for p in range(NY):
        for g in range(GROUP):
            h = p * GROUP + g
            qt_buf[p, :, g * TOK:(g + 1) * TOK] = q_buf[:, h * DIM:(h + 1) * DIM].T

    def pass_through(part, box, dst, recv, device):
        pltpu.make_async_copy(box, box, r_recv.at[part]).wait()
        send(remote(box, dst, f_send.at[part], recv, device))

    up_dev, down_dev = dev(x, up, z), dev(x, down, z)
    pass_through(0, k_box, kv.at[slot(down, 0), pl.ds(0, TOK)], y_recv.at[down], up_dev)
    pass_through(1, v_box, kv.at[slot(up, 0), pl.ds(TOK, TOK)], y_recv.at[up], down_dev)
    lax.fori_loop(1, NY, first_sends, 0)

    @pl.when(x < NX - 1)
    def _():
        pl.semaphore_wait(ready, 1)
    forward(0, NY - 1, 0)
    forward(0, NY - 2, 0)
    part_rows = DIM // 2
    send(through(2, qt_buf.at[across, pl.ds(0, part_rows)], q_box.at[0]))
    send(through(3, qt_buf.at[across, pl.ds(part_rows, part_rows)], q_box.at[1]))
    asked = []
    for n in (0, 2):
        copy = remote(qt_buf.at[y_peers[n]], qe.at[y, pl.ds(0, DIM)], q_send.at[n], q_recv.at[n], dev(x, y_peers[n], z))
        copy.start()
        asked.append(copy)
    own_q = pltpu.make_async_copy(qt_buf.at[y], qe.at[y, pl.ds(0, DIM)], q_send.at[NY - 1])
    own_q.start()

    @pl.when(x == 0)
    def _():
        def blank(at, _):
            kv[at, :2 * TOK, :] = jnp.zeros((2 * TOK, DIM), jnp.bfloat16)
            kv[at, 2 * TOK:, :] = jnp.full((16, DIM), -1.0, jnp.bfloat16)
            return 0

        lax.fori_loop(0, BACK * NZ, blank, 0)

    def arrive(i, step):
        row = row_of(i)
        for way in range(2):
            @pl.when((step < half) | (way == last_way(row)))
            def _():
                z_copy(way, row, step).wait_recv()
                pass_on(way, row, step)

    def first_step(i, _):
        arrive(i, 1)
        return 0

    lax.fori_loop(0, 2, first_step, 0)
    pass_through(2, q_box.at[0], qe.at[down, pl.ds(0, part_rows)], q_recv.at[1], up_dev)
    pass_through(3, q_box.at[1], qe.at[up, pl.ds(part_rows, part_rows)], q_recv.at[1], down_dev)
    lax.fori_loop(2, NY, first_step, 0)

    def wait_x(row, way, step):
        @pl.when(over_x(way, row, step) & (x > 0))
        def _():
            x_copy(row, way, step).wait_recv()

    for row in (NY - 1, NY - 2):
        wait_x(row, 0, 0)
    for way in range(2):
        @pl.when(side_goes(way))
        def _():
            side_copy(way).start()
    for copy in asked:
        copy.wait_recv()
    far_q = qe.at[across, pl.ds(0, DIM)]
    pltpu.make_async_copy(far_q, far_q, q_recv.at[1]).wait()
    own_q.wait()

    key = lax.broadcasted_iota(jnp.int32, (TOK, TOK), 0)
    token = lax.broadcasted_iota(jnp.int32, (TOK, TOK), 1)

    lane = lax.broadcasted_iota(jnp.int32, (TOK, DIM), 1)
    line = lax.broadcasted_iota(jnp.int32, (TOK, DIM), 0)
    plain = jnp.where(lane == 1, 1.0, 0.0)

    def early_keys(at, b):
        there = kv[at, 2 * TOK:, :].astype(jnp.float32)
        less = jnp.where(there < first[b, 0:1, :], 1.0, 0.0)
        count = jnp.sum(jnp.sum(less, axis=0, keepdims=True), axis=1, keepdims=True).astype(jnp.int32)
        extra = jnp.where((lane == 0) & (line < count), NEG, plain).astype(jnp.bfloat16)
        return jnp.concatenate([kv[at, :TOK, :], extra], axis=1)

    def own_keys(at):
        return jnp.concatenate([kv[at, :TOK, :], jnp.zeros((TOK, DIM), jnp.bfloat16)], axis=1)

    def turned_values(slots):
        vt = jnp.concatenate([kv[at, lo:lo + DIM, :] for at in slots for lo in (TOK, TOK + DIM)], axis=1)
        return jnp.concatenate([vt, jnp.ones((16, vt.shape[1]), jnp.bfloat16)], axis=0)

    def chains(jobs):
        todo = [(b, slice(g * WIDE, (g + 1) * WIDE), keys, vt, bias, going)
                for b, keys, vt, bias, going in jobs for g in range(LANES // WIDE)]
        count = len(todo)

        def scores_of(i, n):
            b, cols, keys, _, bias, _ = todo[i]
            size = keys.shape[0] // PIECES
            s = jnp.dot(keys[n * size:(n + 1) * size], qe[b, :, cols], preferred_element_type=jnp.float32)
            if bias is not None and n == 0:
                s = jnp.concatenate([s[:TOK] + bias, s[TOK:]], axis=0)
            return s, jnp.max(s, axis=0, keepdims=True)

        def weigh(i, n, s, shift):
            return jnp.exp2(s * SCALE - shift).astype(jnp.bfloat16)

        def values_of(i, n, w, o):
            vt = todo[i][3]
            size = vt.shape[1] // PIECES
            more = jnp.dot(vt[:, n * size:(n + 1) * size], w, preferred_element_type=jnp.float32)
            return more if o is None else o + more

        ahead = [scores_of(0, n) for n in range(PIECES)]
        late = None
        for i, (b, cols, keys, vt, bias, going) in enumerate(todo):
            held, ahead = ahead, []
            new = held[0][1]
            for _, top in held[1:]:
                new = jnp.maximum(new, top)
            fade = None
            if going:
                old = peak[b, 0:1, cols]
                new = jnp.maximum(old, new)
                fade = jnp.exp2((old - new) * SCALE)
            peak[b, 0:1, cols] = new
            shift = new * SCALE
            o = None
            for n in range(PIECES):
                if i + 1 < count:
                    ahead.append(scores_of(i + 1, n))
                w = weigh(i, n, held[n][0], shift)
                if late is not None:
                    late()
                    late = None
                if n + 1 < PIECES:
                    o = values_of(i, n, w, o)

            def late(i=i, w=w, o=o, b=b, cols=cols, fade=fade):
                total = values_of(i, PIECES - 1, w, o)
                acc[b, :, cols] = total if fade is None else acc[b, :, cols] * fade + total
        late()

    def own_work(j, _):
        jobs = []
        for i in (1, 0):
            b = NY - 2 - 2 * j + i
            at = slot(b, 0)
            own = kv[at, 2 * TOK:, :].astype(jnp.float32)
            row = jnp.concatenate([own[0:1], own[1:2]], axis=1)
            rows = jnp.broadcast_to(row, (TOK, TOK))
            begin = row[:, 0:1]
            first[b] = jnp.broadcast_to(begin, (8, 128))
            rest = jnp.concatenate([jnp.where(row == begin, 0.0, NEG)] * GROUP, axis=1)
            which = lax.broadcasted_iota(jnp.int32, (DIM, LANES), 0)
            qe[b, DIM:, :] = jnp.where(which == 0, 1.0, jnp.where(which == 1, rest, 0.0)).astype(jnp.bfloat16)
            bias = jnp.concatenate([jnp.where((rows == rows.T) & (key <= token), 0.0, NEG)] * (WIDE // TOK), axis=1)
            early = [slot(b - 1, 0), slot(b - 2, 0)]
            keys = jnp.concatenate([own_keys(at)] + [early_keys(one, b) for one in early], axis=0)
            jobs.append((b, keys, turned_values([at] + early), bias, False))
        chains(jobs)
        arrive(2 * j, 2)
        arrive(2 * j + 1, 2)
        return 0

    lax.fori_loop(0, NY // 2, own_work, 0)

    def pair_work(pair, ways, step):
        jobs = []
        for i in (1, 0):
            b = 2 * pair + i
            slots = []
            for way in ways:
                shift = shift_of(way, step)
                there = lax.rem(z + shift + NZ, NZ)
                slots += [slot(b - 1, shift), slot(jnp.where(there < z, b, b - 2), shift)]
            keys = jnp.concatenate([early_keys(at, b) for at in slots], axis=0)
            jobs.append((b, keys, turned_values(slots), None, True))
        chains(jobs)

    def wait_for_x(step):
        for way in range(2):
            for row in (NY - 1, NY - 2):
                wait_x(row, way, step)

            @pl.when((step == 1) & side_comes(way))
            def _():
                side_copy(way).wait_recv()

    def later_step(step, _):
        def catch_up(j, _):
            @pl.when(j == 1)
            def _():
                wait_for_x(step)
            pair_work(1 - j, (0, 1), step)

            @pl.when(step < half - 1)
            def _():
                arrive(2 * j, step + 2)
                arrive(2 * j + 1, step + 2)
            return 0

        lax.fori_loop(0, 2 - step // (half - 1), catch_up, 0)
        return 0

    lax.fori_loop(1, half, later_step, 0)

    rows = TOK // 2
    wide = GROUP * DIM
    cols = out_ref.at[:, pl.ds(pl.multiple_of((core * NY + y) * wide, wide), wide)]

    def part(b, c):
        return o_buf.at[b, pl.ds(pl.multiple_of(c * rows, rows), rows)]

    def over(b):
        return remote(part(b, 1 - core), cols, o_send.at[b, 1], o_recv.at[y, 1], (index_of(x, b, z), 1 - core))

    def along(b):
        return remote(part(b, core), cols, o_send.at[b, 0], o_recv.at[y, 0], (index_of(x, b, z), core))

    def stay(b):
        return pltpu.make_async_copy(part(b, core), cols, o_recv.at[y, 0])

    def send_back(b):
        mixed = (acc[b, :DIM, :] * (1.0 / acc[b, DIM:DIM + 1, :])).astype(jnp.bfloat16)
        for g in range(GROUP):
            o_buf[b, :, g * DIM:(g + 1) * DIM] = mixed[:, g * TOK:(g + 1) * TOK].T

        @pl.when(b == across)
        def _():
            through(4, part(b, core), o_box.at[0]).start()
            through(5, part(b, 1 - core), o_box.at[1]).start()

        @pl.when(b != across)
        def _():
            over(b).start()

        @pl.when((b != across) & (b != y))
        def _():
            along(b).start()

        @pl.when(b == y)
        def _():
            stay(b).start()

    def cols_of(source):
        return out_ref.at[:, pl.ds(pl.multiple_of((core * NY + source) * wide, wide), wide)]

    def output_through(part):
        pltpu.make_async_copy(o_box.at[part - 4], o_box.at[part - 4], r_recv.at[part]).wait()
        output_on(part).start()

    def output_on(part):
        if part == 4:
            return remote(o_box.at[0], cols_of(down), f_send.at[4], o_recv.at[down, 0], up_dev)
        return remote(o_box.at[1], cols_of(up), f_send.at[5], o_recv.at[up, 1], (index_of(x, down, z), 1 - core))

    early = (y == 1) | (y == 2)

    def finish(j, _):
        @pl.when(j == 1)
        def _():
            wait_for_x(half - 1)
            pair_work(0, (0, 1), half - 1)

            @pl.when(early)
            def _():
                output_through(4)

            @pl.when(jnp.logical_not(early))
            def _():
                output_through(5)
            for row in (NY - 1, NY - 2):
                wait_x(row, last_way(row), half)
        pair_work(1 - j, (0,), half)
        for i in (1, 0):
            send_back(2 * (1 - j) + i)
        return 0

    lax.fori_loop(0, 2, finish, 0)

    @pl.when(early)
    def _():
        output_through(5)

    @pl.when(jnp.logical_not(early))
    def _():
        output_through(4)

    for copy in sent + asked:
        copy.wait_send()

    def z_drain(j, _):
        row, way, step = j // (2 * half), (j // half) % 2, 1 + j % half

        @pl.when((step < half) | (way == last_way(row)))
        def _():
            z_copy(way, row, step).wait_send()
        return 0

    lax.fori_loop(0, 2 * NY * half, z_drain, 0)

    def x_drain(j, _):
        row, way, step = NY - 1 - j // (2 * (half + 1)), (j // (half + 1)) % 2, j % (half + 1)
        there_is = jnp.where(step == 0, way == 0, (step < half) | (way == last_way(row)))

        @pl.when(there_is & over_x(way, row, step) & (x < NX - 1))
        def _():
            x_copy(row, way, step).wait_send()
        return 0

    lax.fori_loop(0, 2 * BACK * (half + 1), x_drain, 0)
    for way in range(2):
        @pl.when(side_goes(way))
        def _():
            side_copy(way).wait_send()
    through(4, part(across, core), o_box.at[0]).wait_send()
    through(5, part(across, 1 - core), o_box.at[1]).wait_send()
    output_on(4).wait_send()
    output_on(5).wait_send()
    for b in range(NY):
        @pl.when(b != across)
        def _():
            over(b).wait_send()

        @pl.when((b != y) & (b != across))
        def _():
            along(b).wait_send()
        for e in range(2):
            pltpu.make_async_copy(part(b, core), cols, o_recv.at[b, e]).wait()


def per_device(queries, keys, values, segment_ids):
    any_spec = pl.BlockSpec(memory_space=pl.ANY)
    hbm_spec = pl.BlockSpec(memory_space=pltpu.HBM)
    dma = pltpu.SemaphoreType.DMA
    bf16, f32 = jnp.bfloat16, jnp.float32
    half = NZ // 2
    return pl.pallas_call(
        attention_kernel,
        out_shape=jax.ShapeDtypeStruct((TOK // 2, 2 * NY * GROUP * DIM), bf16),
        in_specs=[hbm_spec] * 4,
        out_specs=any_spec,
        scratch_shapes=[
            pltpu.VMEM(queries.shape, bf16), pltpu.VMEM(values.shape, bf16), pltpu.VMEM((2, 128), jnp.int32), pltpu.VMEM((16, 128), bf16),
            pltpu.VMEM((NY, 2 * DIM, TOK // 2), bf16), pltpu.VMEM((NY, DIM, LANES), bf16),
            pltpu.VMEM((SLOTS, SLOT_ROWS, DIM), bf16),
            pltpu.VMEM((NY, 2 * DIM, LANES), bf16), pltpu.VMEM((NY, DIM + 16, LANES), f32), pltpu.VMEM((NY, 8, LANES), f32),
            pltpu.VMEM((NY, 8, 128), f32), pltpu.VMEM((NY, TOK, GROUP * DIM), bf16),
            dma((3,)), dma((NY - 1, 3)), dma((NY,)), dma((NY,)), dma((NY - 1,)),
            dma((2, NY, half)), dma((2, NY, half)), dma((BACK, 2, half + 1)), dma((BACK, 2, half + 1)),
            dma((2,)), dma((2,)), pltpu.SemaphoreType.REGULAR, dma((NY, 2)), dma((NY, 2)),
            pltpu.VMEM((TOK, DIM), bf16), pltpu.VMEM((TOK, DIM), bf16), pltpu.VMEM((2, DIM // 2, LANES), bf16),
            pltpu.VMEM((2, TOK // 2, GROUP * DIM), bf16), dma((6,)), dma((6,)), dma((6,))],
        compiler_params=pltpu.CompilerParams(collective_id=0, has_side_effects=True,
                                             vmem_limit_bytes=40 * 1024 * 1024),
        name="attention",
    )(*(pltpu.with_memory_space_constraint(one, pltpu.HBM) for one in
        (queries, keys, values, segment_ids.reshape(2, 128))))


def solution(mesh):
    return jax.shard_map(
        per_device,
        mesh=mesh,
        in_specs=(P("ctx", "kvh"), P("ctx", "kvh"), P("ctx", "kvh"), P("ctx")),
        out_specs=P(("ctx", "kvh"), None),
        check_vma=False,
    )
```

```python
import jax
import jax.numpy as jnp
from jax import lax
from jax.experimental import pallas as pl
from jax.experimental.pallas import tpu as pltpu
from jax.sharding import PartitionSpec as P

NX, NY, NZ = 4, 4, 8
TOK = 256
DIM = 128
GROUP = 4
BACK = 2
ROWS = NY + BACK
SLOTS = ROWS * NZ
SLOT_ROWS = 2 * TOK + 16
LANES = GROUP * TOK
WIDE = LANES
PIECES = 2
NEG = -1e30
FAR_ID = 512.0
SCALE = 1.4426950408889634 * DIM ** -0.5


def place():
    me = lax.axis_index("ctx")
    return me, me // (NY * NZ), (me // NZ) % NY, me % NZ


def index_of(x, y, z):
    return (x * NY + y) * NZ + z


def remote(src, dst, send, recv, device):
    return pltpu.make_async_remote_copy(src_ref=src, dst_ref=dst, send_sem=send, recv_sem=recv,
                                        device_id=device, device_id_type=pl.DeviceIdType.MESH)


def attention_kernel(q_ref, k_ref, v_ref, seg_ref, out_ref, q_buf, v_buf, seg_in, seg_buf, vt_buf, qt_buf,
                     kv, qe, acc, peak, first, o_buf, load_sem,
                     y_send, y_recv, q_send, q_recv, z_send, z_recv, x_send, x_recv,
                     side_send, side_recv, ready, o_send, o_recv,
                     k_box, v_box, q_box, o_box, r_send, r_recv, f_send):
    me, x, y, z = place()
    core = lax.axis_index("kvh")
    half = NZ // 2

    def dev(x_, y_, z_):
        return (index_of(x_, y_, z_), core)

    y_peers = [lax.rem(y + d, NY) for d in range(1, NY)]
    z_next, z_prev = lax.rem(z + 1, NZ), lax.rem(z + NZ - 1, NZ)
    x_next, x_prev = lax.rem(x + 1, NX), lax.rem(x + NX - 1, NX)
    barrier = pltpu.get_barrier_semaphore()
    friends = ([dev(x, p, z) for p in y_peers] + [(index_of(x, p, z), 1 - core) for p in [y] + y_peers]
               + [dev(x, y, z_next), dev(x, y, z_prev)])
    for friend in friends:
        pl.semaphore_signal(barrier, inc=1, device_id=friend, device_id_type=pl.DeviceIdType.MESH)

    @pl.when(x < NX - 1)
    def _():
        pl.semaphore_signal(barrier, inc=1, device_id=dev(x_next, y, z), device_id_type=pl.DeviceIdType.MESH)
    load_v = pltpu.make_async_copy(v_ref, v_buf, load_sem.at[0])
    load_q = pltpu.make_async_copy(q_ref, q_buf, load_sem.at[1])
    load_ids = pltpu.make_async_copy(seg_ref, seg_in, load_sem.at[2])
    load_ids.start()
    load_v.start()
    load_q.start()

    load_ids.wait()
    ids = seg_in[...].astype(jnp.float32)
    line = lax.broadcasted_iota(jnp.int32, (16, 128), 0)
    ids = jnp.where(line == 0, ids[0:1], jnp.where(line == 1, ids[1:2], FAR_ID))
    seg_buf[...] = ids.astype(jnp.bfloat16)
    def slot(row, shift):
        return (BACK + row) * NZ + lax.rem(z + shift + NZ, NZ)

    def head_cols(p):
        return pl.ds(pl.multiple_of(p * DIM, DIM), DIM)

    mine = (BACK + y) * NZ + z
    pltpu.make_async_copy(k_ref.at[:, head_cols(y)], kv.at[mine, pl.ds(0, TOK)], y_recv.at[y]).start()
    pltpu.make_async_copy(seg_buf, kv.at[mine, pl.ds(2 * TOK, 16)], y_recv.at[y]).start()
    load_v.wait()
    for p in range(NY):
        turned = v_buf[:, p * DIM:(p + 1) * DIM].T
        vt_buf[p, :DIM, :] = turned[:, :DIM]
        vt_buf[p, DIM:, :] = turned[:, DIM:]
    pltpu.make_async_copy(vt_buf.at[y], kv.at[mine, pl.ds(TOK, TOK)], y_recv.at[y]).start()
    pl.semaphore_wait(barrier, len(friends) + jnp.where(x > 0, 1, 0))

    @pl.when(x > 0)
    def _():
        pl.semaphore_signal(ready, inc=1, device_id=dev(x_prev, y, z), device_id_type=pl.DeviceIdType.MESH)

    up, across, down = y_peers
    sent = []

    def through(part, src, box):
        return remote(src, box, r_send.at[part], r_recv.at[part], dev(x, down if part % 2 else up, z))

    def direct(i, src, lo, rows, n):
        copy = remote(src, kv.at[mine, pl.ds(lo, rows)], y_send.at[n, i], y_recv.at[y], dev(x, y_peers[n], z))
        copy.start()
        sent.append(copy)

    def send(copy):
        copy.start()
        sent.append(copy)

    send(through(0, k_ref.at[:, head_cols(across)], k_box))
    send(through(1, vt_buf.at[across], v_box))
    for n in (0, 2):
        direct(0, k_ref.at[:, head_cols(y_peers[n])], 0, TOK, n)
        direct(1, vt_buf.at[y_peers[n]], TOK, TOK, n)
        direct(2, seg_buf, 2 * TOK, 16, n)
    direct(2, seg_buf, 2 * TOK, 16, 1)

    def shift_of(way, step):
        return step * (2 * way - 1)

    def z_copy(way, row, step):
        at = kv.at[slot(row, shift_of(way, step - 1))]
        neighbour = jnp.where(way == 0, z_next, z_prev)
        return remote(at, at, z_send.at[way, row, step - 1], z_recv.at[way, row, step - 1], dev(x, y, neighbour))

    def x_copy(row, way, step):
        shift = shift_of(way, step)
        return remote(kv.at[slot(row, shift)], kv.at[slot(row - NY, shift)], x_send.at[row - NY + BACK, way, step],
                      x_recv.at[row - NY + BACK, way, step], dev(x_next, y, z))

    def last_way(row):
        return lax.rem(row + 1, 2)

    def row2_over_x(way, step):
        return (lax.rem(z + shift_of(way, step) + NZ, NZ) >= z) & (step != 1)

    def over_x(way, row, step):
        return (row == NY - 1) | ((row == NY - 2) & row2_over_x(way, step))

    def forward(way, row, step):
        @pl.when(over_x(way, row, step) & (x < NX - 1))
        def _():
            x_copy(row, way, step).start()

    def pass_on(way, row, step):
        @pl.when((step < half - 1) | ((step == half - 1) & (way == last_way(row))))
        def _():
            z_copy(way, row, step + 1).start()
        forward(way, row, step)

    def side_copy(way):
        at = kv.at[slot(-BACK, 0)]
        return remote(at, at, side_send.at[way], side_recv.at[way], dev(x, y, z_prev if way else z_next))

    def side_goes(way):
        return (x > 0) & ((z >= 1) if way else (z == NZ - 1))

    def side_comes(way):
        return (x > 0) & ((z < NZ - 1) if way else (z == 0))

    def row_of(i):
        return lax.rem(y + jnp.where(i == 0, 0, jnp.where(i == 1, 1, jnp.where(i == 2, NY - 1, 2))), NY)

    def first_sends(i, _):
        row = row_of(i)
        at = kv.at[slot(row, 0)]
        pltpu.make_async_copy(at, at, y_recv.at[row]).wait()
        z_copy(0, row, 1).start()
        z_copy(1, row, 1).start()
        return 0

    lax.fori_loop(0, 1, first_sends, 0)

    def pass_through(part, box, dst, recv, device):
        pltpu.make_async_copy(box, box, r_recv.at[part]).wait()
        send(remote(box, dst, f_send.at[part], recv, device))

    up_dev, down_dev = dev(x, up, z), dev(x, down, z)
    pass_through(0, k_box, kv.at[slot(down, 0), pl.ds(0, TOK)], y_recv.at[down], up_dev)
    pass_through(1, v_box, kv.at[slot(up, 0), pl.ds(TOK, TOK)], y_recv.at[up], down_dev)
    lax.fori_loop(1, NY, first_sends, 0)

    @pl.when(x < NX - 1)
    def _():
        pl.semaphore_wait(ready, 1)
    forward(0, NY - 1, 0)
    forward(0, NY - 2, 0)
    load_q.wait()
    for p in range(NY):
        for g in range(GROUP):
            h = p * GROUP + g
            qt_buf[p, :, g * TOK:(g + 1) * TOK] = q_buf[:, h * DIM:(h + 1) * DIM].T
    part_rows = DIM // 2
    send(through(2, qt_buf.at[across, pl.ds(0, part_rows)], q_box.at[0]))
    send(through(3, qt_buf.at[across, pl.ds(part_rows, part_rows)], q_box.at[1]))
    asked = []
    for n in (0, 2):
        copy = remote(qt_buf.at[y_peers[n]], qe.at[y, pl.ds(0, DIM)], q_send.at[n], q_recv.at[n], dev(x, y_peers[n], z))
        copy.start()
        asked.append(copy)
    own_q = pltpu.make_async_copy(qt_buf.at[y], qe.at[y, pl.ds(0, DIM)], q_send.at[NY - 1])
    own_q.start()

    @pl.when(x == 0)
    def _():
        def blank(at, _):
            kv[at, :2 * TOK, :] = jnp.zeros((2 * TOK, DIM), jnp.bfloat16)
            kv[at, 2 * TOK:, :] = jnp.full((16, DIM), -1.0, jnp.bfloat16)
            return 0

        lax.fori_loop(0, BACK * NZ, blank, 0)

    def arrive(i, step):
        row = row_of(i)
        for way in range(2):
            @pl.when((step < half) | (way == last_way(row)))
            def _():
                z_copy(way, row, step).wait_recv()
                pass_on(way, row, step)

    def first_step(i, _):
        arrive(i, 1)
        return 0

    lax.fori_loop(0, 2, first_step, 0)
    pass_through(2, q_box.at[0], qe.at[down, pl.ds(0, part_rows)], q_recv.at[1], up_dev)
    pass_through(3, q_box.at[1], qe.at[up, pl.ds(part_rows, part_rows)], q_recv.at[1], down_dev)
    lax.fori_loop(2, NY, first_step, 0)

    def wait_x(row, way, step):
        @pl.when(over_x(way, row, step) & (x > 0))
        def _():
            x_copy(row, way, step).wait_recv()

    for row in (NY - 1, NY - 2):
        wait_x(row, 0, 0)
    for way in range(2):
        @pl.when(side_goes(way))
        def _():
            side_copy(way).start()
    for copy in asked:
        copy.wait_recv()
    far_q = qe.at[across, pl.ds(0, DIM)]
    pltpu.make_async_copy(far_q, far_q, q_recv.at[1]).wait()
    own_q.wait()

    key = lax.broadcasted_iota(jnp.int32, (TOK, TOK), 0)
    token = lax.broadcasted_iota(jnp.int32, (TOK, TOK), 1)

    lane = lax.broadcasted_iota(jnp.int32, (TOK, DIM), 1)
    line = lax.broadcasted_iota(jnp.int32, (TOK, DIM), 0)
    plain = jnp.where(lane == 1, 1.0, 0.0)

    def early_keys(at, b):
        there = kv[at, 2 * TOK:, :].astype(jnp.float32)
        less = jnp.where(there < first[b, 0:1, :], 1.0, 0.0)
        count = jnp.sum(jnp.sum(less, axis=0, keepdims=True), axis=1, keepdims=True).astype(jnp.int32)
        extra = jnp.where((lane == 0) & (line < count), NEG, plain).astype(jnp.bfloat16)
        return jnp.concatenate([kv[at, :TOK, :], extra], axis=1)

    def own_keys(at):
        return jnp.concatenate([kv[at, :TOK, :], jnp.zeros((TOK, DIM), jnp.bfloat16)], axis=1)

    def turned_values(slots):
        vt = jnp.concatenate([kv[at, lo:lo + DIM, :] for at in slots for lo in (TOK, TOK + DIM)], axis=1)
        return jnp.concatenate([vt, jnp.ones((16, vt.shape[1]), jnp.bfloat16)], axis=0)

    def chains(jobs):
        todo = [(b, slice(g * WIDE, (g + 1) * WIDE), keys, vt, bias, going)
                for b, keys, vt, bias, going in jobs for g in range(LANES // WIDE)]
        count = len(todo)

        def scores_of(i, n):
            b, cols, keys, _, bias, _ = todo[i]
            size = keys.shape[0] // PIECES
            s = jnp.dot(keys[n * size:(n + 1) * size], qe[b, :, cols], preferred_element_type=jnp.float32)
            if bias is not None and n == 0:
                s = jnp.concatenate([s[:TOK] + bias, s[TOK:]], axis=0)
            return s, jnp.max(s, axis=0, keepdims=True)

        def weigh(i, n, s, shift):
            return jnp.exp2(s * SCALE - shift).astype(jnp.bfloat16)

        def values_of(i, n, w, o):
            vt = todo[i][3]
            size = vt.shape[1] // PIECES
            more = jnp.dot(vt[:, n * size:(n + 1) * size], w, preferred_element_type=jnp.float32)
            return more if o is None else o + more

        ahead = [scores_of(0, n) for n in range(PIECES)]
        late = None
        for i, (b, cols, keys, vt, bias, going) in enumerate(todo):
            held, ahead = ahead, []
            new = held[0][1]
            for _, top in held[1:]:
                new = jnp.maximum(new, top)
            fade = None
            if going:
                old = peak[b, 0:1, cols]
                new = jnp.maximum(old, new)
                fade = jnp.exp2((old - new) * SCALE)
            peak[b, 0:1, cols] = new
            shift = new * SCALE
            o = None
            for n in range(PIECES):
                if i + 1 < count:
                    ahead.append(scores_of(i + 1, n))
                w = weigh(i, n, held[n][0], shift)
                if late is not None:
                    late()
                    late = None
                if n + 1 < PIECES:
                    o = values_of(i, n, w, o)

            def late(i=i, w=w, o=o, b=b, cols=cols, fade=fade):
                total = values_of(i, PIECES - 1, w, o)
                acc[b, :, cols] = total if fade is None else acc[b, :, cols] * fade + total
        late()

    def own_work(j, _):
        jobs = []
        for i in (1, 0):
            b = NY - 2 - 2 * j + i
            at = slot(b, 0)
            own = kv[at, 2 * TOK:, :].astype(jnp.float32)
            row = jnp.concatenate([own[0:1], own[1:2]], axis=1)
            rows = jnp.broadcast_to(row, (TOK, TOK))
            begin = row[:, 0:1]
            first[b] = jnp.broadcast_to(begin, (8, 128))
            rest = jnp.concatenate([jnp.where(row == begin, 0.0, NEG)] * GROUP, axis=1)
            which = lax.broadcasted_iota(jnp.int32, (DIM, LANES), 0)
            qe[b, DIM:, :] = jnp.where(which == 0, 1.0, jnp.where(which == 1, rest, 0.0)).astype(jnp.bfloat16)
            bias = jnp.concatenate([jnp.where((rows == rows.T) & (key <= token), 0.0, NEG)] * (WIDE // TOK), axis=1)
            early = [slot(b - 1, 0), slot(b - 2, 0)]
            keys = jnp.concatenate([own_keys(at)] + [early_keys(one, b) for one in early], axis=0)
            jobs.append((b, keys, turned_values([at] + early), bias, False))
        chains(jobs)
        arrive(2 * j, 2)
        arrive(2 * j + 1, 2)
        return 0

    lax.fori_loop(0, NY // 2, own_work, 0)

    def pair_work(pair, ways, step):
        jobs = []
        for i in (1, 0):
            b = 2 * pair + i
            slots = []
            for way in ways:
                shift = shift_of(way, step)
                there = lax.rem(z + shift + NZ, NZ)
                slots += [slot(b - 1, shift), slot(jnp.where(there < z, b, b - 2), shift)]
            keys = jnp.concatenate([early_keys(at, b) for at in slots], axis=0)
            jobs.append((b, keys, turned_values(slots), None, True))
        chains(jobs)

    def wait_for_x(step):
        for way in range(2):
            for row in (NY - 1, NY - 2):
                wait_x(row, way, step)

            @pl.when((step == 1) & side_comes(way))
            def _():
                side_copy(way).wait_recv()

    def later_step(step, _):
        def catch_up(j, _):
            @pl.when(j == 1)
            def _():
                wait_for_x(step)
            pair_work(1 - j, (0, 1), step)

            @pl.when(step < half - 1)
            def _():
                arrive(2 * j, step + 2)
                arrive(2 * j + 1, step + 2)
            return 0

        lax.fori_loop(0, 2 - step // (half - 1), catch_up, 0)
        return 0

    lax.fori_loop(1, half, later_step, 0)

    rows = TOK // 2
    wide = GROUP * DIM
    cols = out_ref.at[:, pl.ds(pl.multiple_of((core * NY + y) * wide, wide), wide)]

    def part(b, c):
        return o_buf.at[b, pl.ds(pl.multiple_of(c * rows, rows), rows)]

    def over(b):
        return remote(part(b, 1 - core), cols, o_send.at[b, 1], o_recv.at[y, 1], (index_of(x, b, z), 1 - core))

    def along(b):
        return remote(part(b, core), cols, o_send.at[b, 0], o_recv.at[y, 0], (index_of(x, b, z), core))

    def stay(b):
        return pltpu.make_async_copy(part(b, core), cols, o_recv.at[y, 0])

    def send_back(b):
        mixed = (acc[b, :DIM, :] * (1.0 / acc[b, DIM:DIM + 1, :])).astype(jnp.bfloat16)
        for g in range(GROUP):
            o_buf[b, :, g * DIM:(g + 1) * DIM] = mixed[:, g * TOK:(g + 1) * TOK].T

        @pl.when(b == across)
        def _():
            through(4, part(b, core), o_box.at[0]).start()
            through(5, part(b, 1 - core), o_box.at[1]).start()

        @pl.when(b != across)
        def _():
            over(b).start()

        @pl.when((b != across) & (b != y))
        def _():
            along(b).start()

        @pl.when(b == y)
        def _():
            stay(b).start()

    def cols_of(source):
        return out_ref.at[:, pl.ds(pl.multiple_of((core * NY + source) * wide, wide), wide)]

    def output_through(part):
        pltpu.make_async_copy(o_box.at[part - 4], o_box.at[part - 4], r_recv.at[part]).wait()
        output_on(part).start()

    def output_on(part):
        if part == 4:
            return remote(o_box.at[0], cols_of(down), f_send.at[4], o_recv.at[down, 0], up_dev)
        return remote(o_box.at[1], cols_of(up), f_send.at[5], o_recv.at[up, 1], (index_of(x, down, z), 1 - core))

    early = (y == 1) | (y == 2)

    def finish(j, _):
        @pl.when(j == 1)
        def _():
            wait_for_x(half - 1)
            pair_work(0, (0, 1), half - 1)

            @pl.when(early)
            def _():
                output_through(4)

            @pl.when(jnp.logical_not(early))
            def _():
                output_through(5)
            for row in (NY - 1, NY - 2):
                wait_x(row, last_way(row), half)
        pair_work(1 - j, (0,), half)
        for i in (1, 0):
            send_back(2 * (1 - j) + i)
        return 0

    lax.fori_loop(0, 2, finish, 0)

    @pl.when(early)
    def _():
        output_through(5)

    @pl.when(jnp.logical_not(early))
    def _():
        output_through(4)

    for copy in sent + asked:
        copy.wait_send()

    def z_drain(j, _):
        row, way, step = j // (2 * half), (j // half) % 2, 1 + j % half

        @pl.when((step < half) | (way == last_way(row)))
        def _():
            z_copy(way, row, step).wait_send()
        return 0

    lax.fori_loop(0, 2 * NY * half, z_drain, 0)

    def x_drain(j, _):
        row, way, step = NY - 1 - j // (2 * (half + 1)), (j // (half + 1)) % 2, j % (half + 1)
        there_is = jnp.where(step == 0, way == 0, (step < half) | (way == last_way(row)))

        @pl.when(there_is & over_x(way, row, step) & (x < NX - 1))
        def _():
            x_copy(row, way, step).wait_send()
        return 0

    lax.fori_loop(0, 2 * BACK * (half + 1), x_drain, 0)
    for way in range(2):
        @pl.when(side_goes(way))
        def _():
            side_copy(way).wait_send()
    through(4, part(across, core), o_box.at[0]).wait_send()
    through(5, part(across, 1 - core), o_box.at[1]).wait_send()
    output_on(4).wait_send()
    output_on(5).wait_send()
    for b in range(NY):
        @pl.when(b != across)
        def _():
            over(b).wait_send()

        @pl.when((b != y) & (b != across))
        def _():
            along(b).wait_send()
        for e in range(2):
            pltpu.make_async_copy(part(b, core), cols, o_recv.at[b, e]).wait()


def per_device(queries, keys, values, segment_ids):
    any_spec = pl.BlockSpec(memory_space=pl.ANY)
    hbm_spec = pl.BlockSpec(memory_space=pltpu.HBM)
    dma = pltpu.SemaphoreType.DMA
    bf16, f32 = jnp.bfloat16, jnp.float32
    half = NZ // 2
    return pl.pallas_call(
        attention_kernel,
        out_shape=jax.ShapeDtypeStruct((TOK // 2, 2 * NY * GROUP * DIM), bf16),
        in_specs=[hbm_spec] * 4,
        out_specs=any_spec,
        scratch_shapes=[
            pltpu.VMEM(queries.shape, bf16), pltpu.VMEM(values.shape, bf16), pltpu.VMEM((2, 128), jnp.int32), pltpu.VMEM((16, 128), bf16),
            pltpu.VMEM((NY, 2 * DIM, TOK // 2), bf16), pltpu.VMEM((NY, DIM, LANES), bf16),
            pltpu.VMEM((SLOTS, SLOT_ROWS, DIM), bf16),
            pltpu.VMEM((NY, 2 * DIM, LANES), bf16), pltpu.VMEM((NY, DIM + 16, LANES), f32), pltpu.VMEM((NY, 8, LANES), f32),
            pltpu.VMEM((NY, 8, 128), f32), pltpu.VMEM((NY, TOK, GROUP * DIM), bf16),
            dma((3,)), dma((NY - 1, 3)), dma((NY,)), dma((NY,)), dma((NY - 1,)),
            dma((2, NY, half)), dma((2, NY, half)), dma((BACK, 2, half + 1)), dma((BACK, 2, half + 1)),
            dma((2,)), dma((2,)), pltpu.SemaphoreType.REGULAR, dma((NY, 2)), dma((NY, 2)),
            pltpu.VMEM((TOK, DIM), bf16), pltpu.VMEM((TOK, DIM), bf16), pltpu.VMEM((2, DIM // 2, LANES), bf16),
            pltpu.VMEM((2, TOK // 2, GROUP * DIM), bf16), dma((6,)), dma((6,)), dma((6,))],
        compiler_params=pltpu.CompilerParams(collective_id=0, has_side_effects=True,
                                             vmem_limit_bytes=40 * 1024 * 1024),
        name="attention",
    )(*(pltpu.with_memory_space_constraint(one, pltpu.HBM) for one in
        (queries, keys, values, segment_ids.reshape(2, 128))))


def solution(mesh):
    return jax.shard_map(
        per_device,
        mesh=mesh,
        in_specs=(P("ctx", "kvh"), P("ctx", "kvh"), P("ctx", "kvh"), P("ctx")),
        out_specs=P(("ctx", "kvh"), None),
        check_vma=False,
    )
```

```python
import jax
import jax.numpy as jnp
from jax import lax
from jax.experimental import pallas as pl
from jax.experimental.pallas import tpu as pltpu
from jax.sharding import PartitionSpec as P

NX, NY, NZ = 4, 4, 8
TOK = 256
DIM = 128
GROUP = 4
BACK = 2
ROWS = NY + BACK
SLOTS = ROWS * NZ
SLOT_ROWS = 2 * TOK + 16
LANES = GROUP * TOK
WIDE = LANES
PIECES = 2
NEG = -1e30
FAR_ID = 512.0
SCALE = 1.4426950408889634 * DIM ** -0.5
LN2 = 0.6931471805599453


def place():
    me = lax.axis_index("ctx")
    return me, me // (NY * NZ), (me // NZ) % NY, me % NZ


def index_of(x, y, z):
    return (x * NY + y) * NZ + z


def remote(src, dst, send, recv, device):
    return pltpu.make_async_remote_copy(src_ref=src, dst_ref=dst, send_sem=send, recv_sem=recv,
                                        device_id=device, device_id_type=pl.DeviceIdType.MESH)


def attention_kernel(q_ref, k_ref, v_ref, seg_ref, out_ref, q_buf, v_buf, seg_in, seg_buf, vt_buf, qt_buf,
                     kv, qe, acc, peak, first, o_buf, load_sem,
                     y_send, y_recv, q_send, q_recv, z_send, z_recv, x_send, x_recv,
                     side_send, side_recv, ready, o_send, o_recv,
                     k_box, v_box, q_box, o_box, r_send, r_recv, f_send):
    me, x, y, z = place()
    core = lax.axis_index("kvh")
    half = NZ // 2

    def dev(x_, y_, z_):
        return (index_of(x_, y_, z_), core)

    y_peers = [lax.rem(y + d, NY) for d in range(1, NY)]
    z_next, z_prev = lax.rem(z + 1, NZ), lax.rem(z + NZ - 1, NZ)
    x_next, x_prev = lax.rem(x + 1, NX), lax.rem(x + NX - 1, NX)
    barrier = pltpu.get_barrier_semaphore()
    friends = ([dev(x, p, z) for p in y_peers] + [(index_of(x, p, z), 1 - core) for p in [y] + y_peers]
               + [dev(x, y, z_next), dev(x, y, z_prev)])
    for friend in friends:
        pl.semaphore_signal(barrier, inc=1, device_id=friend, device_id_type=pl.DeviceIdType.MESH)

    @pl.when(x < NX - 1)
    def _():
        pl.semaphore_signal(barrier, inc=1, device_id=dev(x_next, y, z), device_id_type=pl.DeviceIdType.MESH)
    load_v = pltpu.make_async_copy(v_ref, v_buf, load_sem.at[0])
    load_q = pltpu.make_async_copy(q_ref, q_buf, load_sem.at[1])
    load_ids = pltpu.make_async_copy(seg_ref, seg_in, load_sem.at[2])
    load_ids.start()
    load_v.start()
    load_q.start()

    load_ids.wait()
    ids = seg_in[...].astype(jnp.float32)
    line = lax.broadcasted_iota(jnp.int32, (16, 128), 0)
    ids = jnp.where(line == 0, ids[0:1], jnp.where(line == 1, ids[1:2], FAR_ID))
    seg_buf[...] = ids.astype(jnp.bfloat16)
    def slot(row, shift):
        return (BACK + row) * NZ + lax.rem(z + shift + NZ, NZ)

    def head_cols(p):
        return pl.ds(pl.multiple_of(p * DIM, DIM), DIM)

    mine = (BACK + y) * NZ + z
    pltpu.make_async_copy(k_ref.at[:, head_cols(y)], kv.at[mine, pl.ds(0, TOK)], y_recv.at[y]).start()
    pltpu.make_async_copy(seg_buf, kv.at[mine, pl.ds(2 * TOK, 16)], y_recv.at[y]).start()
    load_v.wait()
    for p in range(NY):
        turned = v_buf[:, p * DIM:(p + 1) * DIM].T
        vt_buf[p, :DIM, :] = turned[:, :DIM]
        vt_buf[p, DIM:, :] = turned[:, DIM:]
    pltpu.make_async_copy(vt_buf.at[y], kv.at[mine, pl.ds(TOK, TOK)], y_recv.at[y]).start()
    pl.semaphore_wait(barrier, len(friends) + jnp.where(x > 0, 1, 0))

    @pl.when(x > 0)
    def _():
        pl.semaphore_signal(ready, inc=1, device_id=dev(x_prev, y, z), device_id_type=pl.DeviceIdType.MESH)

    up, across, down = y_peers
    sent = []

    def through(part, src, box):
        return remote(src, box, r_send.at[part], r_recv.at[part], dev(x, down if part % 2 else up, z))

    def direct(i, src, lo, rows, n):
        copy = remote(src, kv.at[mine, pl.ds(lo, rows)], y_send.at[n, i], y_recv.at[y], dev(x, y_peers[n], z))
        copy.start()
        sent.append(copy)

    def send(copy):
        copy.start()
        sent.append(copy)

    send(through(0, k_ref.at[:, head_cols(across)], k_box))
    send(through(1, vt_buf.at[across], v_box))
    for n in (0, 2):
        direct(0, k_ref.at[:, head_cols(y_peers[n])], 0, TOK, n)
        direct(1, vt_buf.at[y_peers[n]], TOK, TOK, n)
        direct(2, seg_buf, 2 * TOK, 16, n)
    direct(2, seg_buf, 2 * TOK, 16, 1)

    def shift_of(way, step):
        return step * (2 * way - 1)

    def z_copy(way, row, step):
        at = kv.at[slot(row, shift_of(way, step - 1))]
        neighbour = jnp.where(way == 0, z_next, z_prev)
        return remote(at, at, z_send.at[way, row, step - 1], z_recv.at[way, row, step - 1], dev(x, y, neighbour))

    def x_copy(row, way, step):
        shift = shift_of(way, step)
        return remote(kv.at[slot(row, shift)], kv.at[slot(row - NY, shift)], x_send.at[row - NY + BACK, way, step],
                      x_recv.at[row - NY + BACK, way, step], dev(x_next, y, z))

    def last_way(row):
        return lax.rem(row + 1, 2)

    def row2_over_x(way, step):
        return (lax.rem(z + shift_of(way, step) + NZ, NZ) >= z) & (step != 1)

    def over_x(way, row, step):
        return (row == NY - 1) | ((row == NY - 2) & row2_over_x(way, step))

    def forward(way, row, step):
        @pl.when(over_x(way, row, step) & (x < NX - 1))
        def _():
            x_copy(row, way, step).start()

    def pass_on(way, row, step):
        @pl.when((step < half - 1) | ((step == half - 1) & (way == last_way(row))))
        def _():
            z_copy(way, row, step + 1).start()
        forward(way, row, step)

    def side_copy(way):
        at = kv.at[slot(-BACK, 0)]
        return remote(at, at, side_send.at[way], side_recv.at[way], dev(x, y, z_prev if way else z_next))

    def side_goes(way):
        return (x > 0) & ((z >= 1) if way else (z == NZ - 1))

    def side_comes(way):
        return (x > 0) & ((z < NZ - 1) if way else (z == 0))

    def row_of(i):
        return lax.rem(y + jnp.where(i == 0, 0, jnp.where(i == 1, 1, jnp.where(i == 2, NY - 1, 2))), NY)

    def first_sends(i, _):
        row = row_of(i)
        at = kv.at[slot(row, 0)]
        pltpu.make_async_copy(at, at, y_recv.at[row]).wait()
        z_copy(0, row, 1).start()
        z_copy(1, row, 1).start()
        return 0

    lax.fori_loop(0, 1, first_sends, 0)

    def pass_through(part, box, dst, recv, device):
        pltpu.make_async_copy(box, box, r_recv.at[part]).wait()
        send(remote(box, dst, f_send.at[part], recv, device))

    up_dev, down_dev = dev(x, up, z), dev(x, down, z)
    pass_through(0, k_box, kv.at[slot(down, 0), pl.ds(0, TOK)], y_recv.at[down], up_dev)
    pass_through(1, v_box, kv.at[slot(up, 0), pl.ds(TOK, TOK)], y_recv.at[up], down_dev)
    lax.fori_loop(1, NY, first_sends, 0)

    @pl.when(x < NX - 1)
    def _():
        pl.semaphore_wait(ready, 1)
    forward(0, NY - 1, 0)
    forward(0, NY - 2, 0)
    load_q.wait()
    for p in range(NY):
        for g in range(GROUP):
            h = p * GROUP + g
            qt_buf[p, :, g * TOK:(g + 1) * TOK] = q_buf[:, h * DIM:(h + 1) * DIM].T
    part_rows = DIM // 2
    send(through(2, qt_buf.at[across, pl.ds(0, part_rows)], q_box.at[0]))
    send(through(3, qt_buf.at[across, pl.ds(part_rows, part_rows)], q_box.at[1]))
    asked = []
    for n in (0, 2):
        copy = remote(qt_buf.at[y_peers[n]], qe.at[y, pl.ds(0, DIM)], q_send.at[n], q_recv.at[n], dev(x, y_peers[n], z))
        copy.start()
        asked.append(copy)
    own_q = pltpu.make_async_copy(qt_buf.at[y], qe.at[y, pl.ds(0, DIM)], q_send.at[NY - 1])
    own_q.start()

    @pl.when(x == 0)
    def _():
        def blank(at, _):
            kv[at, :2 * TOK, :] = jnp.zeros((2 * TOK, DIM), jnp.bfloat16)
            kv[at, 2 * TOK:, :] = jnp.full((16, DIM), -1.0, jnp.bfloat16)
            return 0

        lax.fori_loop(0, BACK * NZ, blank, 0)

    def arrive(i, step):
        row = row_of(i)
        for way in range(2):
            @pl.when((step < half) | (way == last_way(row)))
            def _():
                z_copy(way, row, step).wait_recv()
                pass_on(way, row, step)

    def first_step(i, _):
        arrive(i, 1)
        return 0

    lax.fori_loop(0, 2, first_step, 0)
    pass_through(2, q_box.at[0], qe.at[down, pl.ds(0, part_rows)], q_recv.at[1], up_dev)
    pass_through(3, q_box.at[1], qe.at[up, pl.ds(part_rows, part_rows)], q_recv.at[1], down_dev)
    lax.fori_loop(2, NY, first_step, 0)

    def wait_x(row, way, step):
        @pl.when(over_x(way, row, step) & (x > 0))
        def _():
            x_copy(row, way, step).wait_recv()

    for row in (NY - 1, NY - 2):
        wait_x(row, 0, 0)
    for way in range(2):
        @pl.when(side_goes(way))
        def _():
            side_copy(way).start()
    for copy in asked:
        copy.wait_recv()
    far_q = qe.at[across, pl.ds(0, DIM)]
    pltpu.make_async_copy(far_q, far_q, q_recv.at[1]).wait()
    own_q.wait()

    key = lax.broadcasted_iota(jnp.int32, (TOK, TOK), 0)
    token = lax.broadcasted_iota(jnp.int32, (TOK, TOK), 1)

    lane = lax.broadcasted_iota(jnp.int32, (TOK, DIM), 1)
    line = lax.broadcasted_iota(jnp.int32, (TOK, DIM), 0)
    plain = jnp.where(lane == 1, 1.0, 0.0)

    def early_keys(at, b):
        there = kv[at, 2 * TOK:, :].astype(jnp.float32)
        less = jnp.where(there < first[b, 0:1, :], 1.0, 0.0)
        count = jnp.sum(jnp.sum(less, axis=0, keepdims=True), axis=1, keepdims=True).astype(jnp.int32)
        extra = jnp.where((lane == 0) & (line < count), NEG, plain).astype(jnp.bfloat16)
        return jnp.concatenate([kv[at, :TOK, :], extra], axis=1)

    def own_keys(at):
        return jnp.concatenate([kv[at, :TOK, :], jnp.zeros((TOK, DIM), jnp.bfloat16)], axis=1)

    def turned_values(slots):
        vt = jnp.concatenate([kv[at, lo:lo + DIM, :] for at in slots for lo in (TOK, TOK + DIM)], axis=1)
        return jnp.concatenate([vt, jnp.ones((16, vt.shape[1]), jnp.bfloat16)], axis=0)

    def chains(jobs):
        todo = [(b, slice(g * WIDE, (g + 1) * WIDE), keys, vt, bias, going)
                for b, keys, vt, bias, going in jobs for g in range(LANES // WIDE)]
        count = len(todo)

        def scores_of(i, n):
            b, cols, keys, _, bias, _ = todo[i]
            size = keys.shape[0] // PIECES
            s = jnp.dot(keys[n * size:(n + 1) * size], qe[b, :, cols], preferred_element_type=jnp.float32)
            if bias is not None and n == 0:
                s = jnp.concatenate([s[:TOK] + bias, s[TOK:]], axis=0)
            return s, jnp.max(s, axis=0, keepdims=True)

        def weigh(i, n, s, shift):
            power = s * SCALE - shift
            high = power.astype(jnp.bfloat16)
            low = ((power - high.astype(jnp.float32)) * LN2).astype(jnp.bfloat16)
            w = jnp.exp2(high)
            return w + w * low

        def values_of(i, n, w, o):
            vt = todo[i][3]
            size = vt.shape[1] // PIECES
            more = jnp.dot(vt[:, n * size:(n + 1) * size], w, preferred_element_type=jnp.float32)
            return more if o is None else o + more

        ahead = [scores_of(0, n) for n in range(PIECES)]
        late = None
        for i, (b, cols, keys, vt, bias, going) in enumerate(todo):
            held, ahead = ahead, []
            new = held[0][1]
            for _, top in held[1:]:
                new = jnp.maximum(new, top)
            fade = None
            if going:
                old = peak[b, 0:1, cols]
                new = jnp.maximum(old, new)
                fade = jnp.exp2((old - new) * SCALE)
            peak[b, 0:1, cols] = new
            shift = new * SCALE
            o = None
            for n in range(PIECES):
                if i + 1 < count:
                    ahead.append(scores_of(i + 1, n))
                w = weigh(i, n, held[n][0], shift)
                if late is not None:
                    late()
                    late = None
                if n + 1 < PIECES:
                    o = values_of(i, n, w, o)

            def late(i=i, w=w, o=o, b=b, cols=cols, fade=fade):
                total = values_of(i, PIECES - 1, w, o)
                acc[b, :, cols] = total if fade is None else acc[b, :, cols] * fade + total
        late()

    def own_work(j, _):
        jobs = []
        for i in (1, 0):
            b = NY - 2 - 2 * j + i
            at = slot(b, 0)
            own = kv[at, 2 * TOK:, :].astype(jnp.float32)
            row = jnp.concatenate([own[0:1], own[1:2]], axis=1)
            rows = jnp.broadcast_to(row, (TOK, TOK))
            begin = row[:, 0:1]
            first[b] = jnp.broadcast_to(begin, (8, 128))
            rest = jnp.concatenate([jnp.where(row == begin, 0.0, NEG)] * GROUP, axis=1)
            which = lax.broadcasted_iota(jnp.int32, (DIM, LANES), 0)
            qe[b, DIM:, :] = jnp.where(which == 0, 1.0, jnp.where(which == 1, rest, 0.0)).astype(jnp.bfloat16)
            bias = jnp.concatenate([jnp.where((rows == rows.T) & (key <= token), 0.0, NEG)] * (WIDE // TOK), axis=1)
            early = [slot(b - 1, 0), slot(b - 2, 0)]
            keys = jnp.concatenate([own_keys(at)] + [early_keys(one, b) for one in early], axis=0)
            jobs.append((b, keys, turned_values([at] + early), bias, False))
        chains(jobs)
        arrive(2 * j, 2)
        arrive(2 * j + 1, 2)
        return 0

    lax.fori_loop(0, NY // 2, own_work, 0)

    def pair_work(pair, ways, step):
        jobs = []
        for i in (1, 0):
            b = 2 * pair + i
            slots = []
            for way in ways:
                shift = shift_of(way, step)
                there = lax.rem(z + shift + NZ, NZ)
                slots += [slot(b - 1, shift), slot(jnp.where(there < z, b, b - 2), shift)]
            keys = jnp.concatenate([early_keys(at, b) for at in slots], axis=0)
            jobs.append((b, keys, turned_values(slots), None, True))
        chains(jobs)

    def wait_for_x(step):
        for way in range(2):
            for row in (NY - 1, NY - 2):
                wait_x(row, way, step)

            @pl.when((step == 1) & side_comes(way))
            def _():
                side_copy(way).wait_recv()

    def later_step(step, _):
        def catch_up(j, _):
            @pl.when(j == 1)
            def _():
                wait_for_x(step)
            pair_work(1 - j, (0, 1), step)

            @pl.when(step < half - 1)
            def _():
                arrive(2 * j, step + 2)
                arrive(2 * j + 1, step + 2)
            return 0

        lax.fori_loop(0, 2 - step // (half - 1), catch_up, 0)
        return 0

    lax.fori_loop(1, half, later_step, 0)

    rows = TOK // 2
    wide = GROUP * DIM
    cols = out_ref.at[:, pl.ds(pl.multiple_of((core * NY + y) * wide, wide), wide)]

    def part(b, c):
        return o_buf.at[b, pl.ds(pl.multiple_of(c * rows, rows), rows)]

    def over(b):
        return remote(part(b, 1 - core), cols, o_send.at[b, 1], o_recv.at[y, 1], (index_of(x, b, z), 1 - core))

    def along(b):
        return remote(part(b, core), cols, o_send.at[b, 0], o_recv.at[y, 0], (index_of(x, b, z), core))

    def stay(b):
        return pltpu.make_async_copy(part(b, core), cols, o_recv.at[y, 0])

    def send_back(b):
        mixed = (acc[b, :DIM, :] * (1.0 / acc[b, DIM:DIM + 1, :])).astype(jnp.bfloat16)
        for g in range(GROUP):
            o_buf[b, :, g * DIM:(g + 1) * DIM] = mixed[:, g * TOK:(g + 1) * TOK].T

        @pl.when(b == across)
        def _():
            through(4, part(b, core), o_box.at[0]).start()
            through(5, part(b, 1 - core), o_box.at[1]).start()

        @pl.when(b != across)
        def _():
            over(b).start()

        @pl.when((b != across) & (b != y))
        def _():
            along(b).start()

        @pl.when(b == y)
        def _():
            stay(b).start()

    def cols_of(source):
        return out_ref.at[:, pl.ds(pl.multiple_of((core * NY + source) * wide, wide), wide)]

    def output_through(part):
        pltpu.make_async_copy(o_box.at[part - 4], o_box.at[part - 4], r_recv.at[part]).wait()
        output_on(part).start()

    def output_on(part):
        if part == 4:
            return remote(o_box.at[0], cols_of(down), f_send.at[4], o_recv.at[down, 0], up_dev)
        return remote(o_box.at[1], cols_of(up), f_send.at[5], o_recv.at[up, 1], (index_of(x, down, z), 1 - core))

    early = (y == 1) | (y == 2)

    def finish(j, _):
        @pl.when(j == 1)
        def _():
            wait_for_x(half - 1)
            pair_work(0, (0, 1), half - 1)

            @pl.when(early)
            def _():
                output_through(4)

            @pl.when(jnp.logical_not(early))
            def _():
                output_through(5)
            for row in (NY - 1, NY - 2):
                wait_x(row, last_way(row), half)
        pair_work(1 - j, (0,), half)
        for i in (1, 0):
            send_back(2 * (1 - j) + i)
        return 0

    lax.fori_loop(0, 2, finish, 0)

    @pl.when(early)
    def _():
        output_through(5)

    @pl.when(jnp.logical_not(early))
    def _():
        output_through(4)

    for copy in sent + asked:
        copy.wait_send()

    def z_drain(j, _):
        row, way, step = j // (2 * half), (j // half) % 2, 1 + j % half

        @pl.when((step < half) | (way == last_way(row)))
        def _():
            z_copy(way, row, step).wait_send()
        return 0

    lax.fori_loop(0, 2 * NY * half, z_drain, 0)

    def x_drain(j, _):
        row, way, step = NY - 1 - j // (2 * (half + 1)), (j // (half + 1)) % 2, j % (half + 1)
        there_is = jnp.where(step == 0, way == 0, (step < half) | (way == last_way(row)))

        @pl.when(there_is & over_x(way, row, step) & (x < NX - 1))
        def _():
            x_copy(row, way, step).wait_send()
        return 0

    lax.fori_loop(0, 2 * BACK * (half + 1), x_drain, 0)
    for way in range(2):
        @pl.when(side_goes(way))
        def _():
            side_copy(way).wait_send()
    through(4, part(across, core), o_box.at[0]).wait_send()
    through(5, part(across, 1 - core), o_box.at[1]).wait_send()
    output_on(4).wait_send()
    output_on(5).wait_send()
    for b in range(NY):
        @pl.when(b != across)
        def _():
            over(b).wait_send()

        @pl.when((b != y) & (b != across))
        def _():
            along(b).wait_send()
        for e in range(2):
            pltpu.make_async_copy(part(b, core), cols, o_recv.at[b, e]).wait()


def per_device(queries, keys, values, segment_ids):
    any_spec = pl.BlockSpec(memory_space=pl.ANY)
    hbm_spec = pl.BlockSpec(memory_space=pltpu.HBM)
    dma = pltpu.SemaphoreType.DMA
    bf16, f32 = jnp.bfloat16, jnp.float32
    half = NZ // 2
    return pl.pallas_call(
        attention_kernel,
        out_shape=jax.ShapeDtypeStruct((TOK // 2, 2 * NY * GROUP * DIM), bf16),
        in_specs=[hbm_spec] * 4,
        out_specs=any_spec,
        scratch_shapes=[
            pltpu.VMEM(queries.shape, bf16), pltpu.VMEM(values.shape, bf16), pltpu.VMEM((2, 128), jnp.int32), pltpu.VMEM((16, 128), bf16),
            pltpu.VMEM((NY, 2 * DIM, TOK // 2), bf16), pltpu.VMEM((NY, DIM, LANES), bf16),
            pltpu.VMEM((SLOTS, SLOT_ROWS, DIM), bf16),
            pltpu.VMEM((NY, 2 * DIM, LANES), bf16), pltpu.VMEM((NY, DIM + 16, LANES), f32), pltpu.VMEM((NY, 8, LANES), f32),
            pltpu.VMEM((NY, 8, 128), f32), pltpu.VMEM((NY, TOK, GROUP * DIM), bf16),
            dma((3,)), dma((NY - 1, 3)), dma((NY,)), dma((NY,)), dma((NY - 1,)),
            dma((2, NY, half)), dma((2, NY, half)), dma((BACK, 2, half + 1)), dma((BACK, 2, half + 1)),
            dma((2,)), dma((2,)), pltpu.SemaphoreType.REGULAR, dma((NY, 2)), dma((NY, 2)),
            pltpu.VMEM((TOK, DIM), bf16), pltpu.VMEM((TOK, DIM), bf16), pltpu.VMEM((2, DIM // 2, LANES), bf16),
            pltpu.VMEM((2, TOK // 2, GROUP * DIM), bf16), dma((6,)), dma((6,)), dma((6,))],
        compiler_params=pltpu.CompilerParams(collective_id=0, has_side_effects=True,
                                             vmem_limit_bytes=40 * 1024 * 1024),
        name="attention",
    )(*(pltpu.with_memory_space_constraint(one, pltpu.HBM) for one in
        (queries, keys, values, segment_ids.reshape(2, 128))))


def solution(mesh):
    return jax.shard_map(
        per_device,
        mesh=mesh,
        in_specs=(P("ctx", "kvh"), P("ctx", "kvh"), P("ctx", "kvh"), P("ctx")),
        out_specs=P(("ctx", "kvh"), None),
        check_vma=False,
    )
```

```python
import jax
import jax.numpy as jnp
from jax import lax
from jax.experimental import pallas as pl
from jax.experimental.pallas import tpu as pltpu
from jax.sharding import PartitionSpec as P

NX, NY, NZ = 4, 4, 8
TOK = 256
DIM = 128
GROUP = 4
BACK = 2
ROWS = NY + BACK
SLOTS = ROWS * NZ
SLOT_ROWS = 2 * TOK + 16
LANES = GROUP * TOK
WIDE = TOK
PIECES = 2
NEG = -1e30
FAR_ID = 512.0
SCALE = 1.4426950408889634 * DIM ** -0.5


def place():
    me = lax.axis_index("ctx")
    return me, me // (NY * NZ), (me // NZ) % NY, me % NZ


def index_of(x, y, z):
    return (x * NY + y) * NZ + z


def remote(src, dst, send, recv, device):
    return pltpu.make_async_remote_copy(src_ref=src, dst_ref=dst, send_sem=send, recv_sem=recv,
                                        device_id=device, device_id_type=pl.DeviceIdType.MESH)


def attention_kernel(q_ref, k_ref, v_ref, seg_ref, out_ref, q_buf, v_buf, seg_in, seg_buf, vt_buf, qt_buf,
                     kv, qe, acc, peak, first, o_buf, load_sem,
                     y_send, y_recv, q_send, q_recv, z_send, z_recv, x_send, x_recv,
                     side_send, side_recv, ready, o_send, o_recv,
                     k_box, v_box, q_box, o_box, r_send, r_recv, f_send):
    me, x, y, z = place()
    core = lax.axis_index("kvh")
    half = NZ // 2

    def dev(x_, y_, z_):
        return (index_of(x_, y_, z_), core)

    y_peers = [lax.rem(y + d, NY) for d in range(1, NY)]
    z_next, z_prev = lax.rem(z + 1, NZ), lax.rem(z + NZ - 1, NZ)
    x_next, x_prev = lax.rem(x + 1, NX), lax.rem(x + NX - 1, NX)
    barrier = pltpu.get_barrier_semaphore()
    friends = ([dev(x, p, z) for p in y_peers] + [(index_of(x, p, z), 1 - core) for p in [y] + y_peers]
               + [dev(x, y, z_next), dev(x, y, z_prev)])
    for friend in friends:
        pl.semaphore_signal(barrier, inc=1, device_id=friend, device_id_type=pl.DeviceIdType.MESH)

    @pl.when(x < NX - 1)
    def _():
        pl.semaphore_signal(barrier, inc=1, device_id=dev(x_next, y, z), device_id_type=pl.DeviceIdType.MESH)
    load_v = pltpu.make_async_copy(v_ref, v_buf, load_sem.at[0])
    load_q = pltpu.make_async_copy(q_ref, q_buf, load_sem.at[1])
    load_ids = pltpu.make_async_copy(seg_ref, seg_in, load_sem.at[2])
    load_ids.start()
    load_v.start()
    load_q.start()

    load_ids.wait()
    ids = seg_in[...].astype(jnp.float32)
    line = lax.broadcasted_iota(jnp.int32, (16, 128), 0)
    ids = jnp.where(line == 0, ids[0:1], jnp.where(line == 1, ids[1:2], FAR_ID))
    seg_buf[...] = ids.astype(jnp.bfloat16)
    def slot(row, shift):
        return (BACK + row) * NZ + lax.rem(z + shift + NZ, NZ)

    def head_cols(p):
        return pl.ds(pl.multiple_of(p * DIM, DIM), DIM)

    mine = (BACK + y) * NZ + z
    pltpu.make_async_copy(k_ref.at[:, head_cols(y)], kv.at[mine, pl.ds(0, TOK)], y_recv.at[y]).start()
    pltpu.make_async_copy(seg_buf, kv.at[mine, pl.ds(2 * TOK, 16)], y_recv.at[y]).start()
    load_v.wait()
    for p in range(NY):
        turned = v_buf[:, p * DIM:(p + 1) * DIM].T
        vt_buf[p, :DIM, :] = turned[:, :DIM]
        vt_buf[p, DIM:, :] = turned[:, DIM:]
    pltpu.make_async_copy(vt_buf.at[y], kv.at[mine, pl.ds(TOK, TOK)], y_recv.at[y]).start()
    pl.semaphore_wait(barrier, len(friends) + jnp.where(x > 0, 1, 0))

    @pl.when(x > 0)
    def _():
        pl.semaphore_signal(ready, inc=1, device_id=dev(x_prev, y, z), device_id_type=pl.DeviceIdType.MESH)

    up, across, down = y_peers
    sent = []

    def through(part, src, box):
        return remote(src, box, r_send.at[part], r_recv.at[part], dev(x, down if part % 2 else up, z))

    def direct(i, src, lo, rows, n):
        copy = remote(src, kv.at[mine, pl.ds(lo, rows)], y_send.at[n, i], y_recv.at[y], dev(x, y_peers[n], z))
        copy.start()
        sent.append(copy)

    def send(copy):
        copy.start()
        sent.append(copy)

    send(through(0, k_ref.at[:, head_cols(across)], k_box))
    send(through(1, vt_buf.at[across], v_box))
    for n in (0, 2):
        direct(0, k_ref.at[:, head_cols(y_peers[n])], 0, TOK, n)
        direct(1, vt_buf.at[y_peers[n]], TOK, TOK, n)
        direct(2, seg_buf, 2 * TOK, 16, n)
    direct(2, seg_buf, 2 * TOK, 16, 1)

    def shift_of(way, step):
        return step * (2 * way - 1)

    def z_copy(way, row, step):
        at = kv.at[slot(row, shift_of(way, step - 1))]
        neighbour = jnp.where(way == 0, z_next, z_prev)
        return remote(at, at, z_send.at[way, row, step - 1], z_recv.at[way, row, step - 1], dev(x, y, neighbour))

    def x_copy(row, way, step):
        shift = shift_of(way, step)
        return remote(kv.at[slot(row, shift)], kv.at[slot(row - NY, shift)], x_send.at[row - NY + BACK, way, step],
                      x_recv.at[row - NY + BACK, way, step], dev(x_next, y, z))

    def last_way(row):
        return lax.rem(row + 1, 2)

    def row2_over_x(way, step):
        return (lax.rem(z + shift_of(way, step) + NZ, NZ) >= z) & (step != 1)

    def over_x(way, row, step):
        return (row == NY - 1) | ((row == NY - 2) & row2_over_x(way, step))

    def forward(way, row, step):
        @pl.when(over_x(way, row, step) & (x < NX - 1))
        def _():
            x_copy(row, way, step).start()

    def pass_on(way, row, step):
        @pl.when((step < half - 1) | ((step == half - 1) & (way == last_way(row))))
        def _():
            z_copy(way, row, step + 1).start()
        forward(way, row, step)

    def side_copy(way):
        at = kv.at[slot(-BACK, 0)]
        return remote(at, at, side_send.at[way], side_recv.at[way], dev(x, y, z_prev if way else z_next))

    def side_goes(way):
        return (x > 0) & ((z >= 1) if way else (z == NZ - 1))

    def side_comes(way):
        return (x > 0) & ((z < NZ - 1) if way else (z == 0))

    def row_of(i):
        return lax.rem(y + jnp.where(i == 0, 0, jnp.where(i == 1, 1, jnp.where(i == 2, NY - 1, 2))), NY)

    def first_sends(i, _):
        row = row_of(i)
        at = kv.at[slot(row, 0)]
        pltpu.make_async_copy(at, at, y_recv.at[row]).wait()
        z_copy(0, row, 1).start()
        z_copy(1, row, 1).start()
        return 0

    lax.fori_loop(0, 1, first_sends, 0)

    def pass_through(part, box, dst, recv, device):
        pltpu.make_async_copy(box, box, r_recv.at[part]).wait()
        send(remote(box, dst, f_send.at[part], recv, device))

    up_dev, down_dev = dev(x, up, z), dev(x, down, z)
    pass_through(0, k_box, kv.at[slot(down, 0), pl.ds(0, TOK)], y_recv.at[down], up_dev)
    pass_through(1, v_box, kv.at[slot(up, 0), pl.ds(TOK, TOK)], y_recv.at[up], down_dev)
    lax.fori_loop(1, NY, first_sends, 0)

    @pl.when(x < NX - 1)
    def _():
        pl.semaphore_wait(ready, 1)
    forward(0, NY - 1, 0)
    forward(0, NY - 2, 0)
    load_q.wait()
    for p in range(NY):
        for g in range(GROUP):
            h = p * GROUP + g
            qt_buf[p, :, g * TOK:(g + 1) * TOK] = q_buf[:, h * DIM:(h + 1) * DIM].T
    part_rows = DIM // 2
    send(through(2, qt_buf.at[across, pl.ds(0, part_rows)], q_box.at[0]))
    send(through(3, qt_buf.at[across, pl.ds(part_rows, part_rows)], q_box.at[1]))
    asked = []
    for n in (0, 2):
        copy = remote(qt_buf.at[y_peers[n]], qe.at[y, pl.ds(0, DIM)], q_send.at[n], q_recv.at[n], dev(x, y_peers[n], z))
        copy.start()
        asked.append(copy)
    own_q = pltpu.make_async_copy(qt_buf.at[y], qe.at[y, pl.ds(0, DIM)], q_send.at[NY - 1])
    own_q.start()

    @pl.when(x == 0)
    def _():
        def blank(at, _):
            kv[at, :2 * TOK, :] = jnp.zeros((2 * TOK, DIM), jnp.bfloat16)
            kv[at, 2 * TOK:, :] = jnp.full((16, DIM), -1.0, jnp.bfloat16)
            return 0

        lax.fori_loop(0, BACK * NZ, blank, 0)

    def arrive(i, step):
        row = row_of(i)
        for way in range(2):
            @pl.when((step < half) | (way == last_way(row)))
            def _():
                z_copy(way, row, step).wait_recv()
                pass_on(way, row, step)

    def first_step(i, _):
        arrive(i, 1)
        return 0

    lax.fori_loop(0, 2, first_step, 0)
    pass_through(2, q_box.at[0], qe.at[down, pl.ds(0, part_rows)], q_recv.at[1], up_dev)
    pass_through(3, q_box.at[1], qe.at[up, pl.ds(part_rows, part_rows)], q_recv.at[1], down_dev)
    lax.fori_loop(2, NY, first_step, 0)

    def wait_x(row, way, step):
        @pl.when(over_x(way, row, step) & (x > 0))
        def _():
            x_copy(row, way, step).wait_recv()

    for row in (NY - 1, NY - 2):
        wait_x(row, 0, 0)
    for way in range(2):
        @pl.when(side_goes(way))
        def _():
            side_copy(way).start()
    arrive(0, 2)
    arrive(1, 2)
    for copy in asked:
        copy.wait_recv()
    far_q = qe.at[across, pl.ds(0, DIM)]
    pltpu.make_async_copy(far_q, far_q, q_recv.at[1]).wait()
    own_q.wait()

    key = lax.broadcasted_iota(jnp.int32, (TOK, TOK), 0)
    token = lax.broadcasted_iota(jnp.int32, (TOK, TOK), 1)

    lane = lax.broadcasted_iota(jnp.int32, (TOK, DIM), 1)
    line = lax.broadcasted_iota(jnp.int32, (TOK, DIM), 0)
    plain = jnp.where(lane == 1, 1.0, 0.0)

    def early_keys(at, b):
        there = kv[at, 2 * TOK:, :].astype(jnp.float32)
        less = jnp.where(there < first[b, 0:1, :], 1.0, 0.0)
        count = jnp.sum(jnp.sum(less, axis=0, keepdims=True), axis=1, keepdims=True).astype(jnp.int32)
        extra = jnp.where((lane == 0) & (line < count), NEG, plain).astype(jnp.bfloat16)
        return jnp.concatenate([kv[at, :TOK, :], extra], axis=1)

    def own_keys(at):
        return jnp.concatenate([kv[at, :TOK, :], jnp.zeros((TOK, DIM), jnp.bfloat16)], axis=1)

    def turned_values(slots):
        vt = jnp.concatenate([kv[at, lo:lo + DIM, :] for at in slots for lo in (TOK, TOK + DIM)], axis=1)
        return jnp.concatenate([vt, jnp.ones((16, vt.shape[1]), jnp.bfloat16)], axis=0)

    def chains(jobs):
        todo = [(b, slice(g * WIDE, (g + 1) * WIDE), keys, vt, bias, going)
                for b, keys, vt, bias, going in jobs for g in range(LANES // WIDE)]
        count = len(todo)

        def scores_of(i, n):
            b, cols, keys, _, bias, _ = todo[i]
            size = keys.shape[0] // PIECES
            s = jnp.dot(keys[n * size:(n + 1) * size], qe[b, :, cols], preferred_element_type=jnp.float32)
            if bias is not None and n == 0:
                s = jnp.concatenate([s[:TOK] + bias, s[TOK:]], axis=0)
            return s, jnp.max(s, axis=0, keepdims=True)

        def weigh(i, n, s, shift):
            return jnp.exp2(s * SCALE - shift).astype(jnp.bfloat16)

        def values_of(i, n, w, o):
            vt = todo[i][3]
            size = vt.shape[1] // PIECES
            more = jnp.dot(vt[:, n * size:(n + 1) * size], w, preferred_element_type=jnp.float32)
            return more if o is None else o + more

        ahead = [scores_of(0, n) for n in range(PIECES)]
        late = None
        for i, (b, cols, keys, vt, bias, going) in enumerate(todo):
            held, ahead = ahead, []
            new = held[0][1]
            for _, top in held[1:]:
                new = jnp.maximum(new, top)
            fade = None
            if going:
                old = peak[b, 0:1, cols]
                new = jnp.maximum(old, new)
                fade = jnp.exp2((old - new) * SCALE)
            peak[b, 0:1, cols] = new
            shift = new * SCALE
            o = None
            for n in range(PIECES):
                if i + 1 < count:
                    ahead.append(scores_of(i + 1, n))
                w = weigh(i, n, held[n][0], shift)
                if late is not None:
                    late()
                    late = None
                if n + 1 < PIECES:
                    o = values_of(i, n, w, o)

            def late(i=i, w=w, o=o, b=b, cols=cols, fade=fade):
                total = values_of(i, PIECES - 1, w, o)
                acc[b, :, cols] = total if fade is None else acc[b, :, cols] * fade + total
        late()

    def own_work(j, _):
        b = NY - 1 - j
        at = slot(b, 0)
        own = kv[at, 2 * TOK:, :].astype(jnp.float32)
        row = jnp.concatenate([own[0:1], own[1:2]], axis=1)
        rows = jnp.broadcast_to(row, (TOK, TOK))
        begin = row[:, 0:1]
        first[b] = jnp.broadcast_to(begin, (8, 128))
        rest = jnp.concatenate([jnp.where(row == begin, 0.0, NEG)] * GROUP, axis=1)
        which = lax.broadcasted_iota(jnp.int32, (DIM, LANES), 0)
        qe[b, DIM:, :] = jnp.where(which == 0, 1.0, jnp.where(which == 1, rest, 0.0)).astype(jnp.bfloat16)
        bias = jnp.concatenate([jnp.where((rows == rows.T) & (key <= token), 0.0, NEG)] * (WIDE // TOK), axis=1)
        early = [slot(b - 1, 0), slot(b - 2, 0)]
        keys = jnp.concatenate([own_keys(at)] + [early_keys(one, b) for one in early], axis=0)
        chains([(b, keys, turned_values([at] + early), bias, False)])

        @pl.when(j < 2)
        def _():
            arrive(2 + j, 2)
        return 0

    lax.fori_loop(0, NY, own_work, 0)

    def block_work(b, ways, step):
        slots = []
        for way in ways:
            shift = shift_of(way, step)
            there = lax.rem(z + shift + NZ, NZ)
            slots += [slot(b - 1, shift), slot(jnp.where(there < z, b, b - 2), shift)]
        keys = jnp.concatenate([early_keys(at, b) for at in slots], axis=0)
        chains([(b, keys, turned_values(slots), None, True)])

    def wait_for_x(step):
        for way in range(2):
            for row in (NY - 1, NY - 2):
                wait_x(row, way, step)

            @pl.when((step == 1) & side_comes(way))
            def _():
                side_copy(way).wait_recv()

    def later_step(step, _):
        def catch_up(j, _):
            @pl.when(step < half - 1)
            def _():
                arrive(j, step + 2)

            @pl.when(j == 2)
            def _():
                wait_for_x(step)
            block_work(NY - 1 - j, (0, 1), step)
            return 0

        lax.fori_loop(0, NY - 2 * (step // (half - 1)), catch_up, 0)
        return 0

    lax.fori_loop(1, half, later_step, 0)

    rows = TOK // 2
    wide = GROUP * DIM
    cols = out_ref.at[:, pl.ds(pl.multiple_of((core * NY + y) * wide, wide), wide)]

    def part(b, c):
        return o_buf.at[b, pl.ds(pl.multiple_of(c * rows, rows), rows)]

    def over(b):
        return remote(part(b, 1 - core), cols, o_send.at[b, 1], o_recv.at[y, 1], (index_of(x, b, z), 1 - core))

    def along(b):
        return remote(part(b, core), cols, o_send.at[b, 0], o_recv.at[y, 0], (index_of(x, b, z), core))

    def stay(b):
        return pltpu.make_async_copy(part(b, core), cols, o_recv.at[y, 0])

    def send_back(b):
        mixed = (acc[b, :DIM, :] * (1.0 / acc[b, DIM:DIM + 1, :])).astype(jnp.bfloat16)
        for g in range(GROUP):
            o_buf[b, :, g * DIM:(g + 1) * DIM] = mixed[:, g * TOK:(g + 1) * TOK].T

        @pl.when(b == across)
        def _():
            through(4, part(b, core), o_box.at[0]).start()
            through(5, part(b, 1 - core), o_box.at[1]).start()

        @pl.when(b != across)
        def _():
            over(b).start()

        @pl.when((b != across) & (b != y))
        def _():
            along(b).start()

        @pl.when(b == y)
        def _():
            stay(b).start()

    def cols_of(source):
        return out_ref.at[:, pl.ds(pl.multiple_of((core * NY + source) * wide, wide), wide)]

    def output_through(part):
        pltpu.make_async_copy(o_box.at[part - 4], o_box.at[part - 4], r_recv.at[part]).wait()
        output_on(part).start()

    def output_on(part):
        if part == 4:
            return remote(o_box.at[0], cols_of(down), f_send.at[4], o_recv.at[down, 0], up_dev)
        return remote(o_box.at[1], cols_of(up), f_send.at[5], o_recv.at[up, 1], (index_of(x, down, z), 1 - core))

    early = (y == 1) | (y == 2)

    def finish(j, _):
        @pl.when(j == 2)
        def _():
            wait_for_x(half - 1)

        @pl.when(j >= 2)
        def _():
            block_work(NY - 1 - j, (0, 1), half - 1)

        @pl.when(j == 2)
        def _():
            for row in (NY - 1, NY - 2):
                wait_x(row, last_way(row), half)

        @pl.when((j == 3) & early)
        def _():
            output_through(4)

        @pl.when((j == 3) & jnp.logical_not(early))
        def _():
            output_through(5)
        block_work(NY - 1 - j, (0,), half)
        send_back(NY - 1 - j)
        return 0

    lax.fori_loop(0, NY, finish, 0)

    @pl.when(early)
    def _():
        output_through(5)

    @pl.when(jnp.logical_not(early))
    def _():
        output_through(4)

    for copy in sent + asked:
        copy.wait_send()

    def z_drain(j, _):
        row, way, step = j // (2 * half), (j // half) % 2, 1 + j % half

        @pl.when((step < half) | (way == last_way(row)))
        def _():
            z_copy(way, row, step).wait_send()
        return 0

    lax.fori_loop(0, 2 * NY * half, z_drain, 0)

    def x_drain(j, _):
        row, way, step = NY - 1 - j // (2 * (half + 1)), (j // (half + 1)) % 2, j % (half + 1)
        there_is = jnp.where(step == 0, way == 0, (step < half) | (way == last_way(row)))

        @pl.when(there_is & over_x(way, row, step) & (x < NX - 1))
        def _():
            x_copy(row, way, step).wait_send()
        return 0

    lax.fori_loop(0, 2 * BACK * (half + 1), x_drain, 0)
    for way in range(2):
        @pl.when(side_goes(way))
        def _():
            side_copy(way).wait_send()
    through(4, part(across, core), o_box.at[0]).wait_send()
    through(5, part(across, 1 - core), o_box.at[1]).wait_send()
    output_on(4).wait_send()
    output_on(5).wait_send()
    for b in range(NY):
        @pl.when(b != across)
        def _():
            over(b).wait_send()

        @pl.when((b != y) & (b != across))
        def _():
            along(b).wait_send()
        for e in range(2):
            pltpu.make_async_copy(part(b, core), cols, o_recv.at[b, e]).wait()


def per_device(queries, keys, values, segment_ids):
    any_spec = pl.BlockSpec(memory_space=pl.ANY)
    hbm_spec = pl.BlockSpec(memory_space=pltpu.HBM)
    dma = pltpu.SemaphoreType.DMA
    bf16, f32 = jnp.bfloat16, jnp.float32
    half = NZ // 2
    return pl.pallas_call(
        attention_kernel,
        out_shape=jax.ShapeDtypeStruct((TOK // 2, 2 * NY * GROUP * DIM), bf16),
        in_specs=[hbm_spec] * 4,
        out_specs=any_spec,
        scratch_shapes=[
            pltpu.VMEM(queries.shape, bf16), pltpu.VMEM(values.shape, bf16), pltpu.VMEM((2, 128), jnp.int32), pltpu.VMEM((16, 128), bf16),
            pltpu.VMEM((NY, 2 * DIM, TOK // 2), bf16), pltpu.VMEM((NY, DIM, LANES), bf16),
            pltpu.VMEM((SLOTS, SLOT_ROWS, DIM), bf16),
            pltpu.VMEM((NY, 2 * DIM, LANES), bf16), pltpu.VMEM((NY, DIM + 16, LANES), f32), pltpu.VMEM((NY, 8, LANES), f32),
            pltpu.VMEM((NY, 8, 128), f32), pltpu.VMEM((NY, TOK, GROUP * DIM), bf16),
            dma((3,)), dma((NY - 1, 3)), dma((NY,)), dma((NY,)), dma((NY - 1,)),
            dma((2, NY, half)), dma((2, NY, half)), dma((BACK, 2, half + 1)), dma((BACK, 2, half + 1)),
            dma((2,)), dma((2,)), pltpu.SemaphoreType.REGULAR, dma((NY, 2)), dma((NY, 2)),
            pltpu.VMEM((TOK, DIM), bf16), pltpu.VMEM((TOK, DIM), bf16), pltpu.VMEM((2, DIM // 2, LANES), bf16),
            pltpu.VMEM((2, TOK // 2, GROUP * DIM), bf16), dma((6,)), dma((6,)), dma((6,))],
        compiler_params=pltpu.CompilerParams(collective_id=0, has_side_effects=True,
                                             vmem_limit_bytes=40 * 1024 * 1024),
        name="attention",
    )(*(pltpu.with_memory_space_constraint(one, pltpu.HBM) for one in
        (queries, keys, values, segment_ids.reshape(2, 128))))


def solution(mesh):
    return jax.shard_map(
        per_device,
        mesh=mesh,
        in_specs=(P("ctx", "kvh"), P("ctx", "kvh"), P("ctx", "kvh"), P("ctx")),
        out_specs=P(("ctx", "kvh"), None),
        check_vma=False,
    )
```

```python
import jax
import jax.numpy as jnp
from jax import lax
from jax.experimental import pallas as pl
from jax.experimental.pallas import tpu as pltpu
from jax.sharding import PartitionSpec as P

NX, NY, NZ = 4, 4, 8
TOK = 256
DIM = 128
GROUP = 4
BACK = 2
ROWS = NY + BACK
SLOTS = ROWS * NZ
SLOT_ROWS = 2 * TOK + 16
LANES = GROUP * TOK
NEG = -1e30
FAR_ID = 512.0
SCALE = 1.4426950408889634 * DIM ** -0.5


def place():
    me = lax.axis_index("ctx")
    return me, me // (NY * NZ), (me // NZ) % NY, me % NZ


def index_of(x, y, z):
    return (x * NY + y) * NZ + z


def remote(src, dst, send, recv, device):
    return pltpu.make_async_remote_copy(src_ref=src, dst_ref=dst, send_sem=send, recv_sem=recv,
                                        device_id=device, device_id_type=pl.DeviceIdType.MESH)


def attention_kernel(q_ref, k_ref, v_ref, seg_ref, out_ref, q_buf, v_buf, seg_in, seg_buf, vt_buf, qt_buf,
                     kv, qe, acc, peak, first, o_buf, load_sem,
                     y_send, y_recv, q_send, q_recv, z_send, z_recv, x_send, x_recv,
                     side_send, side_recv, ready, o_send, o_recv,
                     q_box, o_box, r_send, r_recv, f_send):
    me, x, y, z = place()
    core = lax.axis_index("kvh")
    half = NZ // 2

    def dev(x_, y_, z_):
        return (index_of(x_, y_, z_), core)

    y_peers = [lax.rem(y + d, NY) for d in range(1, NY)]
    z_next, z_prev = lax.rem(z + 1, NZ), lax.rem(z + NZ - 1, NZ)
    x_next, x_prev = lax.rem(x + 1, NX), lax.rem(x + NX - 1, NX)
    barrier = pltpu.get_barrier_semaphore()
    friends = ([dev(x, p, z) for p in y_peers] + [(index_of(x, p, z), 1 - core) for p in [y] + y_peers]
               + [dev(x, y, z_next), dev(x, y, z_prev)])
    for friend in friends:
        pl.semaphore_signal(barrier, inc=1, device_id=friend, device_id_type=pl.DeviceIdType.MESH)

    @pl.when(x < NX - 1)
    def _():
        pl.semaphore_signal(barrier, inc=1, device_id=dev(x_next, y, z), device_id_type=pl.DeviceIdType.MESH)
    load_v = pltpu.make_async_copy(v_ref, v_buf, load_sem.at[0])
    load_q = pltpu.make_async_copy(q_ref, q_buf, load_sem.at[1])
    load_ids = pltpu.make_async_copy(seg_ref, seg_in, load_sem.at[2])
    load_ids.start()
    load_v.start()
    load_q.start()

    load_ids.wait()
    ids = seg_in[...].astype(jnp.float32)
    line = lax.broadcasted_iota(jnp.int32, (16, 128), 0)
    ids = jnp.where(line == 0, ids[0:1], jnp.where(line == 1, ids[1:2], FAR_ID))
    seg_buf[...] = ids.astype(jnp.bfloat16)
    def slot(row, shift):
        return (BACK + row) * NZ + lax.rem(z + shift + NZ, NZ)

    def head_cols(p):
        return pl.ds(pl.multiple_of(p * DIM, DIM), DIM)

    mine = (BACK + y) * NZ + z
    pltpu.make_async_copy(k_ref.at[:, head_cols(y)], kv.at[mine, pl.ds(0, TOK)], y_recv.at[y]).start()
    pltpu.make_async_copy(seg_buf, kv.at[mine, pl.ds(2 * TOK, 16)], y_recv.at[y]).start()
    load_v.wait()
    for p in range(NY):
        turned = v_buf[:, p * DIM:(p + 1) * DIM].T
        vt_buf[p, :DIM, :] = turned[:, :DIM]
        vt_buf[p, DIM:, :] = turned[:, DIM:]
    pltpu.make_async_copy(vt_buf.at[y], kv.at[mine, pl.ds(TOK, TOK)], y_recv.at[y]).start()
    pl.semaphore_wait(barrier, len(friends) + jnp.where(x > 0, 1, 0))

    @pl.when(x > 0)
    def _():
        pl.semaphore_signal(ready, inc=1, device_id=dev(x_prev, y, z), device_id_type=pl.DeviceIdType.MESH)

    sent = []
    for n, p in enumerate(y_peers):
        for i, (src, lo, rows) in enumerate(((k_ref.at[:, head_cols(p)], 0, TOK), (vt_buf.at[p], TOK, TOK),
                                             (seg_buf, 2 * TOK, 16))):
            copy = remote(src, kv.at[mine, pl.ds(lo, rows)], y_send.at[n, i], y_recv.at[y], dev(x, p, z))
            copy.start()
            sent.append(copy)

    up, across, down = y_peers
    up_dev, down_dev = dev(x, up, z), dev(x, down, z)

    def through(part, src, box):
        return remote(src, box, r_send.at[part - 2], r_recv.at[part - 2], down_dev if part % 2 else up_dev)

    def send(copy):
        copy.start()
        sent.append(copy)

    def pass_through(part, box, dst, recv, device):
        pltpu.make_async_copy(box, box, r_recv.at[part - 2]).wait()
        send(remote(box, dst, f_send.at[part - 2], recv, device))

    def shift_of(way, step):
        return step * (2 * way - 1)

    def z_copy(way, row, step):
        at = kv.at[slot(row, shift_of(way, step - 1))]
        neighbour = jnp.where(way == 0, z_next, z_prev)
        return remote(at, at, z_send.at[way, row, step - 1], z_recv.at[way, row, step - 1], dev(x, y, neighbour))

    def x_copy(row, way, step):
        shift = shift_of(way, step)
        return remote(kv.at[slot(row, shift)], kv.at[slot(row - NY, shift)], x_send.at[row - NY + BACK, way, step],
                      x_recv.at[row - NY + BACK, way, step], dev(x_next, y, z))

    def last_way(row):
        return lax.rem(row + 1, 2)

    def row2_over_x(way, step):
        return (lax.rem(z + shift_of(way, step) + NZ, NZ) >= z) & (step != 1)

    def over_x(way, row, step):
        return (row == NY - 1) | ((row == NY - 2) & row2_over_x(way, step))

    def forward(way, row, step):
        @pl.when(over_x(way, row, step) & (x < NX - 1))
        def _():
            x_copy(row, way, step).start()

    def pass_on(way, row, step):
        @pl.when((step < half - 1) | ((step == half - 1) & (way == last_way(row))))
        def _():
            z_copy(way, row, step + 1).start()
        forward(way, row, step)

    def side_copy(way):
        at = kv.at[slot(-BACK, 0)]
        return remote(at, at, side_send.at[way], side_recv.at[way], dev(x, y, z_prev if way else z_next))

    def side_goes(way):
        return (x > 0) & ((z >= 1) if way else (z == NZ - 1))

    def side_comes(way):
        return (x > 0) & ((z < NZ - 1) if way else (z == 0))

    def row_of(i):
        return lax.rem(y + jnp.where(i == 0, 0, jnp.where(i == 1, 1, jnp.where(i == 2, NY - 1, 2))), NY)

    def first_sends(i, _):
        row = row_of(i)
        at = kv.at[slot(row, 0)]
        pltpu.make_async_copy(at, at, y_recv.at[row]).wait()
        z_copy(0, row, 1).start()
        z_copy(1, row, 1).start()
        return 0

    lax.fori_loop(0, NY, first_sends, 0)

    @pl.when(x < NX - 1)
    def _():
        pl.semaphore_wait(ready, 1)
    forward(0, NY - 1, 0)
    forward(0, NY - 2, 0)
    load_q.wait()
    for p in range(NY):
        for g in range(GROUP):
            h = p * GROUP + g
            qt_buf[p, :, g * TOK:(g + 1) * TOK] = q_buf[:, h * DIM:(h + 1) * DIM].T
    part_rows = DIM // 2
    send(through(2, qt_buf.at[across, pl.ds(0, part_rows)], q_box.at[0]))
    send(through(3, qt_buf.at[across, pl.ds(part_rows, part_rows)], q_box.at[1]))
    asked = []
    for n in (0, 2):
        copy = remote(qt_buf.at[y_peers[n]], qe.at[y, pl.ds(0, DIM)], q_send.at[n], q_recv.at[n], dev(x, y_peers[n], z))
        copy.start()
        asked.append(copy)
    own_q = pltpu.make_async_copy(qt_buf.at[y], qe.at[y, pl.ds(0, DIM)], q_send.at[NY - 1])
    own_q.start()

    @pl.when(x == 0)
    def _():
        def blank(at, _):
            kv[at, :2 * TOK, :] = jnp.zeros((2 * TOK, DIM), jnp.bfloat16)
            kv[at, 2 * TOK:, :] = jnp.full((16, DIM), -1.0, jnp.bfloat16)
            return 0

        lax.fori_loop(0, BACK * NZ, blank, 0)

    def arrive(i, step):
        row = row_of(i)
        for way in range(2):
            @pl.when((step < half) | (way == last_way(row)))
            def _():
                z_copy(way, row, step).wait_recv()
                pass_on(way, row, step)

    def first_step(i, _):
        arrive(i, 1)
        return 0

    lax.fori_loop(0, 2, first_step, 0)
    pass_through(2, q_box.at[0], qe.at[down, pl.ds(0, part_rows)], q_recv.at[1], up_dev)
    pass_through(3, q_box.at[1], qe.at[up, pl.ds(part_rows, part_rows)], q_recv.at[1], down_dev)
    lax.fori_loop(2, NY, first_step, 0)

    def wait_x(row, way, step):
        @pl.when(over_x(way, row, step) & (x > 0))
        def _():
            x_copy(row, way, step).wait_recv()

    for row in (NY - 1, NY - 2):
        wait_x(row, 0, 0)
    for way in range(2):
        @pl.when(side_goes(way))
        def _():
            side_copy(way).start()
    for copy in asked:
        copy.wait_recv()
    far_q = qe.at[across, pl.ds(0, DIM)]
    pltpu.make_async_copy(far_q, far_q, q_recv.at[1]).wait()
    own_q.wait()

    key = lax.broadcasted_iota(jnp.int32, (TOK, TOK), 0)
    token = lax.broadcasted_iota(jnp.int32, (TOK, TOK), 1)

    lane = lax.broadcasted_iota(jnp.int32, (TOK, DIM), 1)
    line = lax.broadcasted_iota(jnp.int32, (TOK, DIM), 0)
    plain = jnp.where(lane == 1, 1.0, 0.0)

    def early_keys(at, b):
        there = kv[at, 2 * TOK:, :].astype(jnp.float32)
        less = jnp.where(there < first[b, 0:1, :], 1.0, 0.0)
        count = jnp.sum(jnp.sum(less, axis=0, keepdims=True), axis=1, keepdims=True).astype(jnp.int32)
        extra = jnp.where((lane == 0) & (line < count), NEG, plain).astype(jnp.bfloat16)
        return jnp.concatenate([kv[at, :TOK, :], extra], axis=1)

    def own_keys(at):
        return jnp.concatenate([kv[at, :TOK, :], jnp.zeros((TOK, DIM), jnp.bfloat16)], axis=1)

    def turned_values(slots):
        vt = jnp.concatenate([kv[at, lo:lo + DIM, :] for at in slots for lo in (TOK, TOK + DIM)], axis=1)
        return jnp.concatenate([vt, jnp.ones((16, vt.shape[1]), jnp.bfloat16)], axis=0)

    def chains(jobs):
        todo = [(b, slice(g * TOK, (g + 1) * TOK), keys, vt, bias, going)
                for b, keys, vt, bias, going in jobs for g in range(GROUP)]
        count = len(todo)
        scores, weights, done = [None] * count, [None] * count, []
        for i in range(count + 2):
            if i < count:
                b, cols, keys, _, _, _ = todo[i]
                scores[i] = jnp.dot(keys, qe[b, :, cols], preferred_element_type=jnp.float32)
            if 0 <= i - 1 < count:
                b, cols, _, _, bias, going = todo[i - 1]
                s = scores[i - 1]
                if bias is not None:
                    s = jnp.concatenate([s[:TOK] + bias, s[TOK:]], axis=0)
                new = jnp.max(s, axis=0, keepdims=True)
                fade = None
                if going:
                    old = peak[b, 0:1, cols]
                    new = jnp.maximum(old, new)
                    fade = jnp.exp2((old - new) * SCALE)
                weights[i - 1] = (jnp.exp2((s - new) * SCALE).astype(jnp.bfloat16), new, fade)
                scores[i - 1] = None
            if i >= 2:
                b, cols, _, vt, _, going = todo[i - 2]
                w, new, fade = weights[i - 2]
                done.append((b, cols, new, fade, jnp.dot(vt, w, preferred_element_type=jnp.float32)))
                weights[i - 2] = None
        for b, cols, new, fade, o in done:
            peak[b, 0:1, cols] = new
            acc[b, :, cols] = o if fade is None else acc[b, :, cols] * fade + o

    def own_work(j, _):
        jobs = []
        for i in (1, 0):
            b = NY - 2 - 2 * j + i
            at = slot(b, 0)
            own = kv[at, 2 * TOK:, :].astype(jnp.float32)
            row = jnp.concatenate([own[0:1], own[1:2]], axis=1)
            rows = jnp.broadcast_to(row, (TOK, TOK))
            begin = row[:, 0:1]
            first[b] = jnp.broadcast_to(begin, (8, 128))
            rest = jnp.concatenate([jnp.where(row == begin, 0.0, NEG)] * GROUP, axis=1)
            which = lax.broadcasted_iota(jnp.int32, (DIM, LANES), 0)
            qe[b, DIM:, :] = jnp.where(which == 0, 1.0, jnp.where(which == 1, rest, 0.0)).astype(jnp.bfloat16)
            bias = jnp.where((rows == rows.T) & (key <= token), 0.0, NEG)
            early = [slot(b - 1, 0), slot(b - 2, 0)]
            keys = jnp.concatenate([own_keys(at)] + [early_keys(one, b) for one in early], axis=0)
            jobs.append((b, keys, turned_values([at] + early), bias, False))
        chains(jobs)
        return 0

    lax.fori_loop(0, NY // 2, own_work, 0)

    def pair_work(pair, way, step):
        shift = shift_of(way, step)
        there = lax.rem(z + shift + NZ, NZ)
        jobs = []
        for i in (1, 0):
            b = 2 * pair + i
            slots = [slot(b - 1, shift), slot(jnp.where(there < z, b, b - 2), shift)]
            keys = jnp.concatenate([early_keys(at, b) for at in slots], axis=0)
            jobs.append((b, keys, turned_values(slots), None, True))
        chains(jobs)

    def later_step(step, _):
        def catch_up(j, _):
            @pl.when(step < half - 1)
            def _():
                arrive(j, step + 1)

            @pl.when(j == 2)
            def _():
                for way in range(2):
                    for row in (NY - 1, NY - 2):
                        wait_x(row, way, step)

                    @pl.when((step == 1) & side_comes(way))
                    def _():
                        side_copy(way).wait_recv()
            pair_work(1 - j // 2, j % 2, step)
            return 0

        lax.fori_loop(0, 4, catch_up, 0)
        return 0

    lax.fori_loop(1, half, later_step, 0)

    def last_step(i, _):
        arrive(i, half)
        return 0

    lax.fori_loop(0, NY, last_step, 0)

    rows = TOK // 2
    wide = GROUP * DIM
    cols = out_ref.at[:, pl.ds(pl.multiple_of((core * NY + y) * wide, wide), wide)]

    def part(b, c):
        return o_buf.at[b, pl.ds(pl.multiple_of(c * rows, rows), rows)]

    def over(b):
        return remote(part(b, 1 - core), cols, o_send.at[b, 1], o_recv.at[y, 1], (index_of(x, b, z), 1 - core))

    def along(b):
        return remote(part(b, core), cols, o_send.at[b, 0], o_recv.at[y, 0], (index_of(x, b, z), core))

    def stay(b):
        return pltpu.make_async_copy(part(b, core), cols, o_recv.at[y, 0])

    def send_back(b):
        mixed = (acc[b, :DIM, :] * (1.0 / acc[b, DIM:DIM + 1, :])).astype(jnp.bfloat16)
        for g in range(GROUP):
            o_buf[b, :, g * DIM:(g + 1) * DIM] = mixed[:, g * TOK:(g + 1) * TOK].T

        @pl.when(b == across)
        def _():
            through(4, part(b, core), o_box.at[0]).start()
            through(5, part(b, 1 - core), o_box.at[1]).start()

        @pl.when(b != across)
        def _():
            over(b).start()

        @pl.when((b != across) & (b != y))
        def _():
            along(b).start()

        @pl.when(b == y)
        def _():
            stay(b).start()

    def cols_of(source):
        return out_ref.at[:, pl.ds(pl.multiple_of((core * NY + source) * wide, wide), wide)]

    def output_through(part):
        pltpu.make_async_copy(o_box.at[part - 4], o_box.at[part - 4], r_recv.at[part - 2]).wait()
        output_on(part).start()

    def output_on(part):
        if part == 4:
            return remote(o_box.at[0], cols_of(down), f_send.at[2], o_recv.at[down, 0], up_dev)
        return remote(o_box.at[1], cols_of(up), f_send.at[3], o_recv.at[up, 1], (index_of(x, down, z), 1 - core))

    early = (y == 1) | (y == 2)

    def finish(j, _):
        @pl.when(j == 1)
        def _():
            for row in (NY - 1, NY - 2):
                wait_x(row, last_way(row), half)
        pair_work(1 - j, 0, half)
        for i in (1, 0):
            send_back(2 * (1 - j) + i)
        return 0

    lax.fori_loop(0, 2, finish, 0)

    @pl.when(early)
    def _():
        output_through(4)
        output_through(5)

    @pl.when(jnp.logical_not(early))
    def _():
        output_through(5)
        output_through(4)

    for copy in sent + asked:
        copy.wait_send()

    def z_drain(j, _):
        row, way, step = j // (2 * half), (j // half) % 2, 1 + j % half

        @pl.when((step < half) | (way == last_way(row)))
        def _():
            z_copy(way, row, step).wait_send()
        return 0

    lax.fori_loop(0, 2 * NY * half, z_drain, 0)

    def x_drain(j, _):
        row, way, step = NY - 1 - j // (2 * (half + 1)), (j // (half + 1)) % 2, j % (half + 1)
        there_is = jnp.where(step == 0, way == 0, (step < half) | (way == last_way(row)))

        @pl.when(there_is & over_x(way, row, step) & (x < NX - 1))
        def _():
            x_copy(row, way, step).wait_send()
        return 0

    lax.fori_loop(0, 2 * BACK * (half + 1), x_drain, 0)
    for way in range(2):
        @pl.when(side_goes(way))
        def _():
            side_copy(way).wait_send()
    through(4, part(across, core), o_box.at[0]).wait_send()
    through(5, part(across, 1 - core), o_box.at[1]).wait_send()
    output_on(4).wait_send()
    output_on(5).wait_send()
    for b in range(NY):
        @pl.when(b != across)
        def _():
            over(b).wait_send()

        @pl.when((b != y) & (b != across))
        def _():
            along(b).wait_send()
        for e in range(2):
            pltpu.make_async_copy(part(b, core), cols, o_recv.at[b, e]).wait()


def per_device(queries, keys, values, segment_ids):
    any_spec = pl.BlockSpec(memory_space=pl.ANY)
    hbm_spec = pl.BlockSpec(memory_space=pltpu.HBM)
    dma = pltpu.SemaphoreType.DMA
    bf16, f32 = jnp.bfloat16, jnp.float32
    half = NZ // 2
    return pl.pallas_call(
        attention_kernel,
        out_shape=jax.ShapeDtypeStruct((TOK // 2, 2 * NY * GROUP * DIM), bf16),
        in_specs=[hbm_spec] * 4,
        out_specs=any_spec,
        scratch_shapes=[
            pltpu.VMEM(queries.shape, bf16), pltpu.VMEM(values.shape, bf16), pltpu.VMEM((2, 128), jnp.int32), pltpu.VMEM((16, 128), bf16),
            pltpu.VMEM((NY, 2 * DIM, TOK // 2), bf16), pltpu.VMEM((NY, DIM, LANES), bf16),
            pltpu.VMEM((SLOTS, SLOT_ROWS, DIM), bf16),
            pltpu.VMEM((NY, 2 * DIM, LANES), bf16), pltpu.VMEM((NY, DIM + 16, LANES), f32), pltpu.VMEM((NY, 8, LANES), f32),
            pltpu.VMEM((NY, 8, 128), f32), pltpu.VMEM((NY, TOK, GROUP * DIM), bf16),
            dma((3,)), dma((NY - 1, 3)), dma((NY,)), dma((NY,)), dma((NY - 1,)),
            dma((2, NY, half)), dma((2, NY, half)), dma((BACK, 2, half + 1)), dma((BACK, 2, half + 1)),
            dma((2,)), dma((2,)), pltpu.SemaphoreType.REGULAR, dma((NY, 2)), dma((NY, 2)),
            pltpu.VMEM((2, DIM // 2, LANES), bf16), pltpu.VMEM((2, TOK // 2, GROUP * DIM), bf16),
            dma((4,)), dma((4,)), dma((4,))],
        compiler_params=pltpu.CompilerParams(collective_id=0, has_side_effects=True,
                                             vmem_limit_bytes=40 * 1024 * 1024),
        name="attention",
    )(*(pltpu.with_memory_space_constraint(one, pltpu.HBM) for one in
        (queries, keys, values, segment_ids.reshape(2, 128))))


def solution(mesh):
    return jax.shard_map(
        per_device,
        mesh=mesh,
        in_specs=(P("ctx", "kvh"), P("ctx", "kvh"), P("ctx", "kvh"), P("ctx")),
        out_specs=P(("ctx", "kvh"), None),
        check_vma=False,
    )
```

```python
import jax
import jax.numpy as jnp
from jax import lax
from jax.experimental import pallas as pl
from jax.experimental.pallas import tpu as pltpu
from jax.sharding import PartitionSpec as P

NX, NY, NZ = 4, 4, 8
TOK = 256
DIM = 128
GROUP = 4
BACK = 2
ROWS = NY + BACK
SLOTS = ROWS * NZ
SLOT_ROWS = 2 * TOK + 16
LANES = GROUP * TOK
NEG = -1e30
FAR_ID = 512.0
SCALE = 1.4426950408889634 * DIM ** -0.5


def place():
    me = lax.axis_index("ctx")
    return me, me // (NY * NZ), (me // NZ) % NY, me % NZ


def index_of(x, y, z):
    return (x * NY + y) * NZ + z


def remote(src, dst, send, recv, device):
    return pltpu.make_async_remote_copy(src_ref=src, dst_ref=dst, send_sem=send, recv_sem=recv,
                                        device_id=device, device_id_type=pl.DeviceIdType.MESH)


def attention_kernel(q_ref, k_ref, v_ref, seg_ref, out_ref, q_buf, v_buf, seg_in, seg_buf, vt_buf, qt_buf,
                     kv, qe, acc, peak, first, o_buf, load_sem,
                     y_send, y_recv, q_send, q_recv, z_send, z_recv, x_send, x_recv,
                     side_send, side_recv, ready, o_send, o_recv):
    me, x, y, z = place()
    core = lax.axis_index("kvh")
    half = NZ // 2

    def dev(x_, y_, z_):
        return (index_of(x_, y_, z_), core)

    y_peers = [lax.rem(y + d, NY) for d in range(1, NY)]
    z_next, z_prev = lax.rem(z + 1, NZ), lax.rem(z + NZ - 1, NZ)
    x_next, x_prev = lax.rem(x + 1, NX), lax.rem(x + NX - 1, NX)
    barrier = pltpu.get_barrier_semaphore()
    friends = ([dev(x, p, z) for p in y_peers] + [(index_of(x, p, z), 1 - core) for p in [y] + y_peers]
               + [dev(x, y, z_next), dev(x, y, z_prev)])
    for friend in friends:
        pl.semaphore_signal(barrier, inc=1, device_id=friend, device_id_type=pl.DeviceIdType.MESH)

    @pl.when(x < NX - 1)
    def _():
        pl.semaphore_signal(barrier, inc=1, device_id=dev(x_next, y, z), device_id_type=pl.DeviceIdType.MESH)
    load_v = pltpu.make_async_copy(v_ref, v_buf, load_sem.at[0])
    load_q = pltpu.make_async_copy(q_ref, q_buf, load_sem.at[1])
    load_ids = pltpu.make_async_copy(seg_ref, seg_in, load_sem.at[2])
    load_ids.start()
    load_v.start()
    load_q.start()

    load_ids.wait()
    ids = seg_in[...].astype(jnp.float32)
    line = lax.broadcasted_iota(jnp.int32, (16, 128), 0)
    ids = jnp.where(line == 0, ids[0:1], jnp.where(line == 1, ids[1:2], FAR_ID))
    seg_buf[...] = ids.astype(jnp.bfloat16)
    def slot(row, shift):
        return (BACK + row) * NZ + lax.rem(z + shift + NZ, NZ)

    def head_cols(p):
        return pl.ds(pl.multiple_of(p * DIM, DIM), DIM)

    mine = (BACK + y) * NZ + z
    pltpu.make_async_copy(k_ref.at[:, head_cols(y)], kv.at[mine, pl.ds(0, TOK)], y_recv.at[y]).start()
    pltpu.make_async_copy(seg_buf, kv.at[mine, pl.ds(2 * TOK, 16)], y_recv.at[y]).start()
    load_v.wait()
    for p in range(NY):
        turned = v_buf[:, p * DIM:(p + 1) * DIM].T
        vt_buf[p, :DIM, :] = turned[:, :DIM]
        vt_buf[p, DIM:, :] = turned[:, DIM:]
    pltpu.make_async_copy(vt_buf.at[y], kv.at[mine, pl.ds(TOK, TOK)], y_recv.at[y]).start()
    pl.semaphore_wait(barrier, len(friends) + jnp.where(x > 0, 1, 0))

    @pl.when(x > 0)
    def _():
        pl.semaphore_signal(ready, inc=1, device_id=dev(x_prev, y, z), device_id_type=pl.DeviceIdType.MESH)

    sent = []
    for n, p in enumerate(y_peers):
        for i, (src, lo, rows) in enumerate(((k_ref.at[:, head_cols(p)], 0, TOK), (vt_buf.at[p], TOK, TOK),
                                             (seg_buf, 2 * TOK, 16))):
            copy = remote(src, kv.at[mine, pl.ds(lo, rows)], y_send.at[n, i], y_recv.at[y], dev(x, p, z))
            copy.start()
            sent.append(copy)

    def shift_of(way, step):
        return step * (2 * way - 1)

    def z_copy(way, row, step):
        at = kv.at[slot(row, shift_of(way, step - 1))]
        neighbour = jnp.where(way == 0, z_next, z_prev)
        return remote(at, at, z_send.at[way, row, step - 1], z_recv.at[way, row, step - 1], dev(x, y, neighbour))

    def x_copy(row, way, step):
        shift = shift_of(way, step)
        return remote(kv.at[slot(row, shift)], kv.at[slot(row - NY, shift)], x_send.at[row - NY + BACK, way, step],
                      x_recv.at[row - NY + BACK, way, step], dev(x_next, y, z))

    def last_way(row):
        return lax.rem(row + 1, 2)

    def row2_over_x(way, step):
        return (lax.rem(z + shift_of(way, step) + NZ, NZ) >= z) & (step != 1)

    def over_x(way, row, step):
        return (row == NY - 1) | ((row == NY - 2) & row2_over_x(way, step))

    def forward(way, row, step):
        @pl.when(over_x(way, row, step) & (x < NX - 1))
        def _():
            x_copy(row, way, step).start()

    def pass_on(way, row, step):
        @pl.when((step < half - 1) | ((step == half - 1) & (way == last_way(row))))
        def _():
            z_copy(way, row, step + 1).start()
        forward(way, row, step)

    def side_copy(way):
        at = kv.at[slot(-BACK, 0)]
        return remote(at, at, side_send.at[way], side_recv.at[way], dev(x, y, z_prev if way else z_next))

    def side_goes(way):
        return (x > 0) & ((z >= 1) if way else (z == NZ - 1))

    def side_comes(way):
        return (x > 0) & ((z < NZ - 1) if way else (z == 0))

    def row_of(i):
        return lax.rem(y + jnp.where(i == 0, 0, jnp.where(i == 1, 1, jnp.where(i == 2, NY - 1, 2))), NY)

    def first_sends(i, _):
        row = row_of(i)
        at = kv.at[slot(row, 0)]
        pltpu.make_async_copy(at, at, y_recv.at[row]).wait()
        z_copy(0, row, 1).start()
        z_copy(1, row, 1).start()
        return 0

    lax.fori_loop(0, NY, first_sends, 0)

    @pl.when(x < NX - 1)
    def _():
        pl.semaphore_wait(ready, 1)
    forward(0, NY - 1, 0)
    forward(0, NY - 2, 0)
    load_q.wait()
    for p in range(NY):
        for g in range(GROUP):
            h = p * GROUP + g
            qt_buf[p, :, g * TOK:(g + 1) * TOK] = q_buf[:, h * DIM:(h + 1) * DIM].T
    asked = []
    for n, p in enumerate(y_peers):
        copy = remote(qt_buf.at[p], qe.at[y, pl.ds(0, DIM)], q_send.at[n], q_recv.at[n], dev(x, p, z))
        copy.start()
        asked.append(copy)
    own_q = pltpu.make_async_copy(qt_buf.at[y], qe.at[y, pl.ds(0, DIM)], q_send.at[NY - 1])
    own_q.start()

    @pl.when(x == 0)
    def _():
        def blank(at, _):
            kv[at, :2 * TOK, :] = jnp.zeros((2 * TOK, DIM), jnp.bfloat16)
            kv[at, 2 * TOK:, :] = jnp.full((16, DIM), -1.0, jnp.bfloat16)
            return 0

        lax.fori_loop(0, BACK * NZ, blank, 0)

    def arrive(i, step):
        row = NY - 1 - i
        for way in range(2):
            @pl.when((step < half) | (way == last_way(row)))
            def _():
                z_copy(way, row, step).wait_recv()
                pass_on(way, row, step)

    def first_step(i, _):
        arrive(i, 1)
        return 0

    lax.fori_loop(0, NY, first_step, 0)

    def wait_x(row, way, step):
        @pl.when(over_x(way, row, step) & (x > 0))
        def _():
            x_copy(row, way, step).wait_recv()

    for row in (NY - 1, NY - 2):
        wait_x(row, 0, 0)
    for way in range(2):
        @pl.when(side_goes(way))
        def _():
            side_copy(way).start()
    for copy in asked:
        copy.wait_recv()
    own_q.wait()

    key = lax.broadcasted_iota(jnp.int32, (TOK, TOK), 0)
    token = lax.broadcasted_iota(jnp.int32, (TOK, TOK), 1)

    lane = lax.broadcasted_iota(jnp.int32, (TOK, DIM), 1)
    line = lax.broadcasted_iota(jnp.int32, (TOK, DIM), 0)
    plain = jnp.where(lane == 1, 1.0, 0.0)

    def early_keys(at, b):
        there = kv[at, 2 * TOK:, :].astype(jnp.float32)
        less = jnp.where(there < first[b, 0:1, :], 1.0, 0.0)
        count = jnp.sum(jnp.sum(less, axis=0, keepdims=True), axis=1, keepdims=True).astype(jnp.int32)
        extra = jnp.where((lane == 0) & (line < count), NEG, plain).astype(jnp.bfloat16)
        return jnp.concatenate([kv[at, :TOK, :], extra], axis=1)

    def own_keys(at):
        return jnp.concatenate([kv[at, :TOK, :], jnp.zeros((TOK, DIM), jnp.bfloat16)], axis=1)

    def turned_values(slots):
        vt = jnp.concatenate([kv[at, lo:lo + DIM, :] for at in slots for lo in (TOK, TOK + DIM)], axis=1)
        return jnp.concatenate([vt, jnp.ones((16, vt.shape[1]), jnp.bfloat16)], axis=0)

    def chains(jobs):
        todo = [(b, slice(g * TOK, (g + 1) * TOK), keys, vt, bias, going)
                for b, keys, vt, bias, going in jobs for g in range(GROUP)]
        count = len(todo)
        scores, weights, done = [None] * count, [None] * count, []
        for i in range(count + 2):
            if i < count:
                b, cols, keys, _, _, _ = todo[i]
                scores[i] = jnp.dot(keys, qe[b, :, cols], preferred_element_type=jnp.float32)
            if 0 <= i - 1 < count:
                b, cols, _, _, bias, going = todo[i - 1]
                s = scores[i - 1]
                if bias is not None:
                    s = jnp.concatenate([s[:TOK] + bias, s[TOK:]], axis=0)
                new = jnp.max(s, axis=0, keepdims=True)
                fade = None
                if going:
                    old = peak[b, 0:1, cols]
                    new = jnp.maximum(old, new)
                    fade = jnp.exp2((old - new) * SCALE)
                weights[i - 1] = (jnp.exp2((s - new) * SCALE).astype(jnp.bfloat16), new, fade)
                scores[i - 1] = None
            if i >= 2:
                b, cols, _, vt, _, going = todo[i - 2]
                w, new, fade = weights[i - 2]
                done.append((b, cols, new, fade, jnp.dot(vt, w, preferred_element_type=jnp.float32)))
                weights[i - 2] = None
        for b, cols, new, fade, o in done:
            peak[b, 0:1, cols] = new
            acc[b, :, cols] = o if fade is None else acc[b, :, cols] * fade + o

    def own_work(j, _):
        jobs = []
        for i in (1, 0):
            b = NY - 2 - 2 * j + i
            at = slot(b, 0)
            own = kv[at, 2 * TOK:, :].astype(jnp.float32)
            row = jnp.concatenate([own[0:1], own[1:2]], axis=1)
            rows = jnp.broadcast_to(row, (TOK, TOK))
            begin = row[:, 0:1]
            first[b] = jnp.broadcast_to(begin, (8, 128))
            rest = jnp.concatenate([jnp.where(row == begin, 0.0, NEG)] * GROUP, axis=1)
            which = lax.broadcasted_iota(jnp.int32, (DIM, LANES), 0)
            qe[b, DIM:, :] = jnp.where(which == 0, 1.0, jnp.where(which == 1, rest, 0.0)).astype(jnp.bfloat16)
            bias = jnp.where((rows == rows.T) & (key <= token), 0.0, NEG)
            early = [slot(b - 1, 0), slot(b - 2, 0)]
            keys = jnp.concatenate([own_keys(at)] + [early_keys(one, b) for one in early], axis=0)
            jobs.append((b, keys, turned_values([at] + early), bias, False))
        chains(jobs)
        return 0

    lax.fori_loop(0, NY // 2, own_work, 0)

    def pair_work(pair, way, step):
        shift = shift_of(way, step)
        there = lax.rem(z + shift + NZ, NZ)
        jobs = []
        for i in (1, 0):
            b = 2 * pair + i
            slots = [slot(b - 1, shift), slot(jnp.where(there < z, b, b - 2), shift)]
            keys = jnp.concatenate([early_keys(at, b) for at in slots], axis=0)
            jobs.append((b, keys, turned_values(slots), None, True))
        chains(jobs)

    def later_step(step, _):
        def catch_up(j, _):
            @pl.when(step < half - 1)
            def _():
                arrive(j, step + 1)

            @pl.when(j == 2)
            def _():
                for way in range(2):
                    for row in (NY - 1, NY - 2):
                        wait_x(row, way, step)

                    @pl.when((step == 1) & side_comes(way))
                    def _():
                        side_copy(way).wait_recv()
            pair_work(1 - j // 2, j % 2, step)
            return 0

        lax.fori_loop(0, 4, catch_up, 0)
        return 0

    lax.fori_loop(1, half, later_step, 0)

    def last_step(i, _):
        arrive(i, half)
        return 0

    lax.fori_loop(0, NY, last_step, 0)

    rows = TOK // 2
    wide = GROUP * DIM
    cols = out_ref.at[:, pl.ds(pl.multiple_of((core * NY + y) * wide, wide), wide)]

    def part(b, c):
        return o_buf.at[b, pl.ds(pl.multiple_of(c * rows, rows), rows)]

    def over(b):
        return remote(part(b, 1 - core), cols, o_send.at[b, 1], o_recv.at[y, 1], (index_of(x, b, z), 1 - core))

    def along(b):
        return remote(part(b, core), cols, o_send.at[b, 0], o_recv.at[y, 0], (index_of(x, b, z), core))

    def stay(b):
        return pltpu.make_async_copy(part(b, core), cols, o_recv.at[y, 0])

    def send_back(b):
        mixed = (acc[b, :DIM, :] * (1.0 / acc[b, DIM:DIM + 1, :])).astype(jnp.bfloat16)
        for g in range(GROUP):
            o_buf[b, :, g * DIM:(g + 1) * DIM] = mixed[:, g * TOK:(g + 1) * TOK].T
        over(b).start()

        @pl.when(b != y)
        def _():
            along(b).start()

        @pl.when(b == y)
        def _():
            stay(b).start()

    def finish(j, _):
        @pl.when(j == 1)
        def _():
            for row in (NY - 1, NY - 2):
                wait_x(row, last_way(row), half)
        pair_work(1 - j, 0, half)
        for i in (1, 0):
            send_back(2 * (1 - j) + i)
        return 0

    lax.fori_loop(0, 2, finish, 0)

    for copy in sent + asked:
        copy.wait_send()

    def z_drain(j, _):
        row, way, step = j // (2 * half), (j // half) % 2, 1 + j % half

        @pl.when((step < half) | (way == last_way(row)))
        def _():
            z_copy(way, row, step).wait_send()
        return 0

    lax.fori_loop(0, 2 * NY * half, z_drain, 0)

    def x_drain(j, _):
        row, way, step = NY - 1 - j // (2 * (half + 1)), (j // (half + 1)) % 2, j % (half + 1)
        there_is = jnp.where(step == 0, way == 0, (step < half) | (way == last_way(row)))

        @pl.when(there_is & over_x(way, row, step) & (x < NX - 1))
        def _():
            x_copy(row, way, step).wait_send()
        return 0

    lax.fori_loop(0, 2 * BACK * (half + 1), x_drain, 0)
    for way in range(2):
        @pl.when(side_goes(way))
        def _():
            side_copy(way).wait_send()
    for b in range(NY):
        over(b).wait_send()

        @pl.when(b != y)
        def _():
            along(b).wait_send()
        for e in range(2):
            pltpu.make_async_copy(part(b, core), cols, o_recv.at[b, e]).wait()


def per_device(queries, keys, values, segment_ids):
    any_spec = pl.BlockSpec(memory_space=pl.ANY)
    hbm_spec = pl.BlockSpec(memory_space=pltpu.HBM)
    dma = pltpu.SemaphoreType.DMA
    bf16, f32 = jnp.bfloat16, jnp.float32
    half = NZ // 2
    return pl.pallas_call(
        attention_kernel,
        out_shape=jax.ShapeDtypeStruct((TOK // 2, 2 * NY * GROUP * DIM), bf16),
        in_specs=[hbm_spec] * 4,
        out_specs=any_spec,
        scratch_shapes=[
            pltpu.VMEM(queries.shape, bf16), pltpu.VMEM(values.shape, bf16), pltpu.VMEM((2, 128), jnp.int32), pltpu.VMEM((16, 128), bf16),
            pltpu.VMEM((NY, 2 * DIM, TOK // 2), bf16), pltpu.VMEM((NY, DIM, LANES), bf16),
            pltpu.VMEM((SLOTS, SLOT_ROWS, DIM), bf16),
            pltpu.VMEM((NY, 2 * DIM, LANES), bf16), pltpu.VMEM((NY, DIM + 16, LANES), f32), pltpu.VMEM((NY, 8, LANES), f32),
            pltpu.VMEM((NY, 8, 128), f32), pltpu.VMEM((NY, TOK, GROUP * DIM), bf16),
            dma((3,)), dma((NY - 1, 3)), dma((NY,)), dma((NY,)), dma((NY - 1,)),
            dma((2, NY, half)), dma((2, NY, half)), dma((BACK, 2, half + 1)), dma((BACK, 2, half + 1)),
            dma((2,)), dma((2,)), pltpu.SemaphoreType.REGULAR, dma((NY, 2)), dma((NY, 2))],
        compiler_params=pltpu.CompilerParams(collective_id=0, has_side_effects=True,
                                             vmem_limit_bytes=40 * 1024 * 1024),
        name="attention",
    )(*(pltpu.with_memory_space_constraint(one, pltpu.HBM) for one in
        (queries, keys, values, segment_ids.reshape(2, 128))))


def solution(mesh):
    return jax.shard_map(
        per_device,
        mesh=mesh,
        in_specs=(P("ctx", "kvh"), P("ctx", "kvh"), P("ctx", "kvh"), P("ctx")),
        out_specs=P(("ctx", "kvh"), None),
        check_vma=False,
    )
```

```python
import jax
import jax.numpy as jnp
from jax import lax
from jax.experimental import pallas as pl
from jax.experimental.pallas import tpu as pltpu
from jax.sharding import PartitionSpec as P

NX, NY, NZ = 4, 4, 8
TOK = 256
DIM = 128
GROUP = 4
BACK = 2
ROWS = NY + BACK
SLOTS = ROWS * NZ
SLOT_ROWS = 2 * TOK + 16
LANES = GROUP * TOK
NEG = -1e30
FAR_ID = 512.0
SCALE = 1.4426950408889634 * DIM ** -0.5


def place():
    me = lax.axis_index("ctx")
    return me, me // (NY * NZ), (me // NZ) % NY, me % NZ


def index_of(x, y, z):
    return (x * NY + y) * NZ + z


def remote(src, dst, send, recv, device):
    return pltpu.make_async_remote_copy(src_ref=src, dst_ref=dst, send_sem=send, recv_sem=recv,
                                        device_id=device, device_id_type=pl.DeviceIdType.MESH)


def attention_kernel(q_ref, k_ref, v_ref, seg_ref, out_ref, q_buf, v_buf, seg_in, seg_buf, vt_buf,
                     kv, qe, acc, peak, first, o_buf, load_sem,
                     y_send, y_recv, q_send, q_recv, z_send, z_recv, x_send, x_recv,
                     side_send, side_recv, ready, o_send, o_recv):
    me, x, y, z = place()
    core = lax.axis_index("kvh")
    half = NZ // 2

    def dev(x_, y_, z_):
        return (index_of(x_, y_, z_), core)

    y_peers = [lax.rem(y + d, NY) for d in range(1, NY)]
    z_next, z_prev = lax.rem(z + 1, NZ), lax.rem(z + NZ - 1, NZ)
    x_next, x_prev = lax.rem(x + 1, NX), lax.rem(x + NX - 1, NX)
    barrier = pltpu.get_barrier_semaphore()
    friends = ([dev(x, p, z) for p in y_peers] + [(index_of(x, p, z), 1 - core) for p in [y] + y_peers]
               + [dev(x, y, z_next), dev(x, y, z_prev)])
    for friend in friends:
        pl.semaphore_signal(barrier, inc=1, device_id=friend, device_id_type=pl.DeviceIdType.MESH)

    @pl.when(x < NX - 1)
    def _():
        pl.semaphore_signal(barrier, inc=1, device_id=dev(x_next, y, z), device_id_type=pl.DeviceIdType.MESH)
    load_v = pltpu.make_async_copy(v_ref, v_buf, load_sem.at[0])
    load_ids = pltpu.make_async_copy(seg_ref, seg_in, load_sem.at[2])
    load_ids.start()
    load_v.start()

    load_ids.wait()
    ids = seg_in[...].astype(jnp.float32)
    line = lax.broadcasted_iota(jnp.int32, (16, 128), 0)
    ids = jnp.where(line == 0, ids[0:1], jnp.where(line == 1, ids[1:2], FAR_ID))
    seg_buf[...] = ids.astype(jnp.bfloat16)
    def slot(row, shift):
        return (BACK + row) * NZ + lax.rem(z + shift + NZ, NZ)

    def head_cols(p):
        return pl.ds(pl.multiple_of(p * DIM, DIM), DIM)

    def query_cols(p):
        return pl.ds(pl.multiple_of(p * GROUP * DIM, GROUP * DIM), GROUP * DIM)

    mine = (BACK + y) * NZ + z
    pltpu.make_async_copy(k_ref.at[:, head_cols(y)], kv.at[mine, pl.ds(0, TOK)], y_recv.at[y]).start()
    pltpu.make_async_copy(seg_buf, kv.at[mine, pl.ds(2 * TOK, 16)], y_recv.at[y]).start()
    load_v.wait()
    for p in range(NY):
        turned = v_buf[:, p * DIM:(p + 1) * DIM].T
        vt_buf[p, :DIM, :] = turned[:, :DIM]
        vt_buf[p, DIM:, :] = turned[:, DIM:]
    pltpu.make_async_copy(vt_buf.at[y], kv.at[mine, pl.ds(TOK, TOK)], y_recv.at[y]).start()
    pl.semaphore_wait(barrier, len(friends) + jnp.where(x > 0, 1, 0))

    @pl.when(x > 0)
    def _():
        pl.semaphore_signal(ready, inc=1, device_id=dev(x_prev, y, z), device_id_type=pl.DeviceIdType.MESH)

    sent = []
    for n, p in enumerate(y_peers):
        for i, (src, lo, rows) in enumerate(((k_ref.at[:, head_cols(p)], 0, TOK), (vt_buf.at[p], TOK, TOK),
                                             (seg_buf, 2 * TOK, 16))):
            copy = remote(src, kv.at[mine, pl.ds(lo, rows)], y_send.at[n, i], y_recv.at[y], dev(x, p, z))
            copy.start()
            sent.append(copy)

    def shift_of(way, step):
        return step * (2 * way - 1)

    def z_copy(way, row, step):
        at = kv.at[slot(row, shift_of(way, step - 1))]
        neighbour = jnp.where(way == 0, z_next, z_prev)
        return remote(at, at, z_send.at[way, row, step - 1], z_recv.at[way, row, step - 1], dev(x, y, neighbour))

    def x_copy(row, way, step):
        shift = shift_of(way, step)
        return remote(kv.at[slot(row, shift)], kv.at[slot(row - NY, shift)], x_send.at[row - NY + BACK, way, step],
                      x_recv.at[row - NY + BACK, way, step], dev(x_next, y, z))

    def last_way(row):
        return lax.rem(row + 1, 2)

    def row2_over_x(way, step):
        return (lax.rem(z + shift_of(way, step) + NZ, NZ) >= z) & (step != 1)

    def over_x(way, row, step):
        return (row == NY - 1) | ((row == NY - 2) & row2_over_x(way, step))

    def forward(way, row, step):
        @pl.when(over_x(way, row, step) & (x < NX - 1))
        def _():
            x_copy(row, way, step).start()

    def pass_on(way, row, step):
        @pl.when((step < half - 1) | ((step == half - 1) & (way == last_way(row))))
        def _():
            z_copy(way, row, step + 1).start()
        forward(way, row, step)

    def side_copy(way):
        at = kv.at[slot(-BACK, 0)]
        return remote(at, at, side_send.at[way], side_recv.at[way], dev(x, y, z_prev if way else z_next))

    def side_goes(way):
        return (x > 0) & ((z >= 1) if way else (z == NZ - 1))

    def side_comes(way):
        return (x > 0) & ((z < NZ - 1) if way else (z == 0))

    def row_of(i):
        return lax.rem(y + jnp.where(i == 0, 0, jnp.where(i == 1, 1, jnp.where(i == 2, NY - 1, 2))), NY)

    def first_sends(i, _):
        row = row_of(i)
        at = kv.at[slot(row, 0)]
        pltpu.make_async_copy(at, at, y_recv.at[row]).wait()
        z_copy(0, row, 1).start()
        z_copy(1, row, 1).start()
        return 0

    lax.fori_loop(0, NY, first_sends, 0)

    @pl.when(x < NX - 1)
    def _():
        pl.semaphore_wait(ready, 1)
    forward(0, NY - 1, 0)
    forward(0, NY - 2, 0)
    asked = []
    for n, p in enumerate(y_peers):
        copy = remote(q_ref.at[:, query_cols(p)], q_buf.at[y], q_send.at[n], q_recv.at[n], dev(x, p, z))
        copy.start()
        asked.append(copy)
    own_q = pltpu.make_async_copy(q_ref.at[:, query_cols(y)], q_buf.at[y], q_send.at[NY - 1])
    own_q.start()

    @pl.when(x == 0)
    def _():
        def blank(at, _):
            kv[at, :2 * TOK, :] = jnp.zeros((2 * TOK, DIM), jnp.bfloat16)
            kv[at, 2 * TOK:, :] = jnp.full((16, DIM), -1.0, jnp.bfloat16)
            return 0

        lax.fori_loop(0, BACK * NZ, blank, 0)

    def arrive(i, step):
        row = NY - 1 - i
        for way in range(2):
            @pl.when((step < half) | (way == last_way(row)))
            def _():
                z_copy(way, row, step).wait_recv()
                pass_on(way, row, step)

    def first_step(i, _):
        arrive(i, 1)
        return 0

    lax.fori_loop(0, NY, first_step, 0)

    def wait_x(row, way, step):
        @pl.when(over_x(way, row, step) & (x > 0))
        def _():
            x_copy(row, way, step).wait_recv()

    for row in (NY - 1, NY - 2):
        wait_x(row, 0, 0)
    for way in range(2):
        @pl.when(side_goes(way))
        def _():
            side_copy(way).start()
    for copy in asked:
        copy.wait_recv()
    own_q.wait()

    key = lax.broadcasted_iota(jnp.int32, (TOK, TOK), 0)
    token = lax.broadcasted_iota(jnp.int32, (TOK, TOK), 1)

    lane = lax.broadcasted_iota(jnp.int32, (TOK, DIM), 1)
    line = lax.broadcasted_iota(jnp.int32, (TOK, DIM), 0)
    plain = jnp.where(lane == 1, 1.0, 0.0)

    def early_keys(at, b):
        there = kv[at, 2 * TOK:, :].astype(jnp.float32)
        less = jnp.where(there < first[b, 0:1, :], 1.0, 0.0)
        count = jnp.sum(jnp.sum(less, axis=0, keepdims=True), axis=1, keepdims=True).astype(jnp.int32)
        extra = jnp.where((lane == 0) & (line < count), NEG, plain).astype(jnp.bfloat16)
        return jnp.concatenate([kv[at, :TOK, :], extra], axis=1)

    def own_keys(at):
        return jnp.concatenate([kv[at, :TOK, :], jnp.zeros((TOK, DIM), jnp.bfloat16)], axis=1)

    def turned_values(slots):
        vt = jnp.concatenate([kv[at, lo:lo + DIM, :] for at in slots for lo in (TOK, TOK + DIM)], axis=1)
        return jnp.concatenate([vt, jnp.ones((16, vt.shape[1]), jnp.bfloat16)], axis=0)

    def chains(jobs):
        todo = [(b, slice(g * TOK, (g + 1) * TOK), keys, vt, bias, going)
                for b, keys, vt, bias, going in jobs for g in range(GROUP)]
        count = len(todo)
        scores, weights, done = [None] * count, [None] * count, []
        for i in range(count + 2):
            if i < count:
                b, cols, keys, _, _, _ = todo[i]
                scores[i] = lax.dot_general(keys, qe[b, cols, :], (((1,), (1,)), ((), ())), preferred_element_type=jnp.float32)
            if 0 <= i - 1 < count:
                b, cols, _, _, bias, going = todo[i - 1]
                s = scores[i - 1]
                if bias is not None:
                    s = jnp.concatenate([s[:TOK] + bias, s[TOK:]], axis=0)
                new = jnp.max(s, axis=0, keepdims=True)
                fade = None
                if going:
                    old = peak[b, 0:1, cols]
                    new = jnp.maximum(old, new)
                    fade = jnp.exp2((old - new) * SCALE)
                weights[i - 1] = (jnp.exp2((s - new) * SCALE).astype(jnp.bfloat16), new, fade)
                scores[i - 1] = None
            if i >= 2:
                b, cols, _, vt, _, going = todo[i - 2]
                w, new, fade = weights[i - 2]
                done.append((b, cols, new, fade, jnp.dot(vt, w, preferred_element_type=jnp.float32)))
                weights[i - 2] = None
        for b, cols, new, fade, o in done:
            peak[b, 0:1, cols] = new
            acc[b, :, cols] = o if fade is None else acc[b, :, cols] * fade + o

    def own_work(j, _):
        jobs = []
        for i in (1, 0):
            b = NY - 2 - 2 * j + i
            at = slot(b, 0)
            own = kv[at, 2 * TOK:, :].astype(jnp.float32)
            row = jnp.concatenate([own[0:1], own[1:2]], axis=1)
            rows = jnp.broadcast_to(row, (TOK, TOK))
            begin = row[:, 0:1]
            first[b] = jnp.broadcast_to(begin, (8, 128))
            columns = rows.T
            rest = jnp.where(columns[:, :DIM] == begin, 0.0, NEG)
            extra = jnp.where(lane == 0, 1.0, jnp.where(lane == 1, rest, 0.0)).astype(jnp.bfloat16)
            for g in range(GROUP):
                qe[b, g * TOK:(g + 1) * TOK, :DIM] = q_buf[b, :, g * DIM:(g + 1) * DIM]
                qe[b, g * TOK:(g + 1) * TOK, DIM:] = extra
            bias = jnp.where((rows == columns) & (key <= token), 0.0, NEG)
            early = [slot(b - 1, 0), slot(b - 2, 0)]
            keys = jnp.concatenate([own_keys(at)] + [early_keys(one, b) for one in early], axis=0)
            jobs.append((b, keys, turned_values([at] + early), bias, False))
        chains(jobs)
        return 0

    lax.fori_loop(0, NY // 2, own_work, 0)

    def pair_work(pair, way, step):
        shift = shift_of(way, step)
        there = lax.rem(z + shift + NZ, NZ)
        jobs = []
        for i in (1, 0):
            b = 2 * pair + i
            slots = [slot(b - 1, shift), slot(jnp.where(there < z, b, b - 2), shift)]
            keys = jnp.concatenate([early_keys(at, b) for at in slots], axis=0)
            jobs.append((b, keys, turned_values(slots), None, True))
        chains(jobs)

    def later_step(step, _):
        def catch_up(j, _):
            @pl.when(step < half - 1)
            def _():
                arrive(j, step + 1)

            @pl.when(j == 2)
            def _():
                for way in range(2):
                    for row in (NY - 1, NY - 2):
                        wait_x(row, way, step)

                    @pl.when((step == 1) & side_comes(way))
                    def _():
                        side_copy(way).wait_recv()
            pair_work(1 - j // 2, j % 2, step)
            return 0

        lax.fori_loop(0, 4, catch_up, 0)
        return 0

    lax.fori_loop(1, half, later_step, 0)

    def last_step(i, _):
        arrive(i, half)
        return 0

    lax.fori_loop(0, NY, last_step, 0)

    rows = TOK // 2
    wide = GROUP * DIM
    cols = out_ref.at[:, pl.ds(pl.multiple_of((core * NY + y) * wide, wide), wide)]

    def part(b, c):
        return o_buf.at[b, pl.ds(pl.multiple_of(c * rows, rows), rows)]

    def over(b):
        return remote(part(b, 1 - core), cols, o_send.at[b, 1], o_recv.at[y, 1], (index_of(x, b, z), 1 - core))

    def along(b):
        return remote(part(b, core), cols, o_send.at[b, 0], o_recv.at[y, 0], (index_of(x, b, z), core))

    def stay(b):
        return pltpu.make_async_copy(part(b, core), cols, o_recv.at[y, 0])

    def send_back(b):
        mixed = (acc[b, :DIM, :] * (1.0 / acc[b, DIM:DIM + 1, :])).astype(jnp.bfloat16)
        for g in range(GROUP):
            o_buf[b, :, g * DIM:(g + 1) * DIM] = mixed[:, g * TOK:(g + 1) * TOK].T
        over(b).start()

        @pl.when(b != y)
        def _():
            along(b).start()

        @pl.when(b == y)
        def _():
            stay(b).start()

    def finish(j, _):
        @pl.when(j == 1)
        def _():
            for row in (NY - 1, NY - 2):
                wait_x(row, last_way(row), half)
        pair_work(1 - j, 0, half)
        for i in (1, 0):
            send_back(2 * (1 - j) + i)
        return 0

    lax.fori_loop(0, 2, finish, 0)

    for copy in sent + asked:
        copy.wait_send()

    def z_drain(j, _):
        row, way, step = j // (2 * half), (j // half) % 2, 1 + j % half

        @pl.when((step < half) | (way == last_way(row)))
        def _():
            z_copy(way, row, step).wait_send()
        return 0

    lax.fori_loop(0, 2 * NY * half, z_drain, 0)

    def x_drain(j, _):
        row, way, step = NY - 1 - j // (2 * (half + 1)), (j // (half + 1)) % 2, j % (half + 1)
        there_is = jnp.where(step == 0, way == 0, (step < half) | (way == last_way(row)))

        @pl.when(there_is & over_x(way, row, step) & (x < NX - 1))
        def _():
            x_copy(row, way, step).wait_send()
        return 0

    lax.fori_loop(0, 2 * BACK * (half + 1), x_drain, 0)
    for way in range(2):
        @pl.when(side_goes(way))
        def _():
            side_copy(way).wait_send()
    for b in range(NY):
        over(b).wait_send()

        @pl.when(b != y)
        def _():
            along(b).wait_send()
        for e in range(2):
            pltpu.make_async_copy(part(b, core), cols, o_recv.at[b, e]).wait()


def per_device(queries, keys, values, segment_ids):
    any_spec = pl.BlockSpec(memory_space=pl.ANY)
    hbm_spec = pl.BlockSpec(memory_space=pltpu.HBM)
    dma = pltpu.SemaphoreType.DMA
    bf16, f32 = jnp.bfloat16, jnp.float32
    half = NZ // 2
    return pl.pallas_call(
        attention_kernel,
        out_shape=jax.ShapeDtypeStruct((TOK // 2, 2 * NY * GROUP * DIM), bf16),
        in_specs=[hbm_spec] * 4,
        out_specs=any_spec,
        scratch_shapes=[
            pltpu.VMEM((NY, TOK, GROUP * DIM), bf16), pltpu.VMEM(values.shape, bf16), pltpu.VMEM((2, 128), jnp.int32), pltpu.VMEM((16, 128), bf16),
            pltpu.VMEM((NY, 2 * DIM, TOK // 2), bf16),
            pltpu.VMEM((SLOTS, SLOT_ROWS, DIM), bf16),
            pltpu.VMEM((NY, LANES, 2 * DIM), bf16), pltpu.VMEM((NY, DIM + 16, LANES), f32), pltpu.VMEM((NY, 8, LANES), f32),
            pltpu.VMEM((NY, 8, 128), f32), pltpu.VMEM((NY, TOK, GROUP * DIM), bf16),
            dma((3,)), dma((NY - 1, 3)), dma((NY,)), dma((NY,)), dma((NY - 1,)),
            dma((2, NY, half)), dma((2, NY, half)), dma((BACK, 2, half + 1)), dma((BACK, 2, half + 1)),
            dma((2,)), dma((2,)), pltpu.SemaphoreType.REGULAR, dma((NY, 2)), dma((NY, 2))],
        compiler_params=pltpu.CompilerParams(collective_id=0, has_side_effects=True,
                                             vmem_limit_bytes=40 * 1024 * 1024),
        name="attention",
    )(*(pltpu.with_memory_space_constraint(one, pltpu.HBM) for one in
        (queries, keys, values, segment_ids.reshape(2, 128))))


def solution(mesh):
    return jax.shard_map(
        per_device,
        mesh=mesh,
        in_specs=(P("ctx", "kvh"), P("ctx", "kvh"), P("ctx", "kvh"), P("ctx")),
        out_specs=P(("ctx", "kvh"), None),
        check_vma=False,
    )
```

```python
import jax
import jax.numpy as jnp
from jax import lax
from jax.experimental import pallas as pl
from jax.experimental.pallas import tpu as pltpu
from jax.sharding import PartitionSpec as P

NX, NY, NZ = 4, 4, 8
TOK = 256
DIM = 128
GROUP = 4
BACK = 2
ROWS = NY + BACK
SLOTS = ROWS * NZ
SLOT_ROWS = 2 * TOK + 16
LANES = GROUP * TOK
WIDE = LANES
PIECES = 2
NEG = -1e30
FAR_ID = 512.0
SCALE = 1.4426950408889634 * DIM ** -0.5


def place():
    me = lax.axis_index("ctx")
    return me, me // (NY * NZ), (me // NZ) % NY, me % NZ


def index_of(x, y, z):
    return (x * NY + y) * NZ + z


def remote(src, dst, send, recv, device):
    return pltpu.make_async_remote_copy(src_ref=src, dst_ref=dst, send_sem=send, recv_sem=recv,
                                        device_id=device, device_id_type=pl.DeviceIdType.MESH)


def attention_kernel(q_ref, k_ref, v_ref, seg_ref, out_ref, q_buf, v_buf, seg_in, seg_buf, vt_buf, qt_buf,
                     kv, qe, acc, peak, first, o_buf, load_sem,
                     y_send, y_recv, q_send, q_recv, z_send, z_recv, x_send, x_recv,
                     side_send, side_recv, ready, o_send, o_recv):
    me, x, y, z = place()
    core = lax.axis_index("kvh")
    half = NZ // 2

    def dev(x_, y_, z_):
        return (index_of(x_, y_, z_), core)

    y_peers = [lax.rem(y + d, NY) for d in range(1, NY)]
    z_next, z_prev = lax.rem(z + 1, NZ), lax.rem(z + NZ - 1, NZ)
    x_next, x_prev = lax.rem(x + 1, NX), lax.rem(x + NX - 1, NX)
    barrier = pltpu.get_barrier_semaphore()
    friends = ([dev(x, p, z) for p in y_peers] + [(index_of(x, p, z), 1 - core) for p in [y] + y_peers]
               + [dev(x, y, z_next), dev(x, y, z_prev)])
    for friend in friends:
        pl.semaphore_signal(barrier, inc=1, device_id=friend, device_id_type=pl.DeviceIdType.MESH)

    @pl.when(x < NX - 1)
    def _():
        pl.semaphore_signal(barrier, inc=1, device_id=dev(x_next, y, z), device_id_type=pl.DeviceIdType.MESH)
    load_v = pltpu.make_async_copy(v_ref, v_buf, load_sem.at[0])
    load_q = pltpu.make_async_copy(q_ref, q_buf, load_sem.at[1])
    load_ids = pltpu.make_async_copy(seg_ref, seg_in, load_sem.at[2])
    load_ids.start()
    load_v.start()
    load_q.start()

    load_ids.wait()
    ids = seg_in[...].astype(jnp.float32)
    line = lax.broadcasted_iota(jnp.int32, (16, 128), 0)
    ids = jnp.where(line == 0, ids[0:1], jnp.where(line == 1, ids[1:2], FAR_ID))
    seg_buf[...] = ids.astype(jnp.bfloat16)
    def slot(row, shift):
        return (BACK + row) * NZ + lax.rem(z + shift + NZ, NZ)

    def head_cols(p):
        return pl.ds(pl.multiple_of(p * DIM, DIM), DIM)

    mine = (BACK + y) * NZ + z
    pltpu.make_async_copy(k_ref.at[:, head_cols(y)], kv.at[mine, pl.ds(0, TOK)], y_recv.at[y]).start()
    pltpu.make_async_copy(seg_buf, kv.at[mine, pl.ds(2 * TOK, 16)], y_recv.at[y]).start()
    load_v.wait()
    for p in range(NY):
        turned = v_buf[:, p * DIM:(p + 1) * DIM].T
        vt_buf[p, :DIM, :] = turned[:, :DIM]
        vt_buf[p, DIM:, :] = turned[:, DIM:]
    pltpu.make_async_copy(vt_buf.at[y], kv.at[mine, pl.ds(TOK, TOK)], y_recv.at[y]).start()
    pl.semaphore_wait(barrier, len(friends) + jnp.where(x > 0, 1, 0))

    @pl.when(x > 0)
    def _():
        pl.semaphore_signal(ready, inc=1, device_id=dev(x_prev, y, z), device_id_type=pl.DeviceIdType.MESH)

    sent = []
    for n, p in enumerate(y_peers):
        for i, (src, lo, rows) in enumerate(((k_ref.at[:, head_cols(p)], 0, TOK), (vt_buf.at[p], TOK, TOK),
                                             (seg_buf, 2 * TOK, 16))):
            copy = remote(src, kv.at[mine, pl.ds(lo, rows)], y_send.at[n, i], y_recv.at[y], dev(x, p, z))
            copy.start()
            sent.append(copy)

    def shift_of(way, step):
        return step * (2 * way - 1)

    def z_copy(way, row, step):
        at = kv.at[slot(row, shift_of(way, step - 1))]
        neighbour = jnp.where(way == 0, z_next, z_prev)
        return remote(at, at, z_send.at[way, row, step - 1], z_recv.at[way, row, step - 1], dev(x, y, neighbour))

    def x_copy(row, way, step):
        shift = shift_of(way, step)
        return remote(kv.at[slot(row, shift)], kv.at[slot(row - NY, shift)], x_send.at[row - NY + BACK, way, step],
                      x_recv.at[row - NY + BACK, way, step], dev(x_next, y, z))

    def last_way(row):
        return lax.rem(row + 1, 2)

    def row2_over_x(way, step):
        return (lax.rem(z + shift_of(way, step) + NZ, NZ) >= z) & (step != 1)

    def over_x(way, row, step):
        return (row == NY - 1) | ((row == NY - 2) & row2_over_x(way, step))

    def forward(way, row, step):
        @pl.when(over_x(way, row, step) & (x < NX - 1))
        def _():
            x_copy(row, way, step).start()

    def pass_on(way, row, step):
        @pl.when((step < half - 1) | ((step == half - 1) & (way == last_way(row))))
        def _():
            z_copy(way, row, step + 1).start()
        forward(way, row, step)

    def side_copy(way):
        at = kv.at[slot(-BACK, 0)]
        return remote(at, at, side_send.at[way], side_recv.at[way], dev(x, y, z_prev if way else z_next))

    def side_goes(way):
        return (x > 0) & ((z >= 1) if way else (z == NZ - 1))

    def side_comes(way):
        return (x > 0) & ((z < NZ - 1) if way else (z == 0))

    def row_of(i):
        return lax.rem(y + jnp.where(i == 0, 0, jnp.where(i == 1, 1, jnp.where(i == 2, NY - 1, 2))), NY)

    def first_sends(i, _):
        row = row_of(i)
        at = kv.at[slot(row, 0)]
        pltpu.make_async_copy(at, at, y_recv.at[row]).wait()
        z_copy(0, row, 1).start()
        z_copy(1, row, 1).start()
        return 0

    lax.fori_loop(0, NY, first_sends, 0)

    @pl.when(x < NX - 1)
    def _():
        pl.semaphore_wait(ready, 1)
    forward(0, NY - 1, 0)
    forward(0, NY - 2, 0)
    load_q.wait()
    for p in range(NY):
        for g in range(GROUP):
            h = p * GROUP + g
            qt_buf[p, :, g * TOK:(g + 1) * TOK] = q_buf[:, h * DIM:(h + 1) * DIM].T
    asked = []
    for n, p in enumerate(y_peers):
        copy = remote(qt_buf.at[p], qe.at[y, pl.ds(0, DIM)], q_send.at[n], q_recv.at[n], dev(x, p, z))
        copy.start()
        asked.append(copy)
    own_q = pltpu.make_async_copy(qt_buf.at[y], qe.at[y, pl.ds(0, DIM)], q_send.at[NY - 1])
    own_q.start()

    @pl.when(x == 0)
    def _():
        def blank(at, _):
            kv[at, :2 * TOK, :] = jnp.zeros((2 * TOK, DIM), jnp.bfloat16)
            kv[at, 2 * TOK:, :] = jnp.full((16, DIM), -1.0, jnp.bfloat16)
            return 0

        lax.fori_loop(0, BACK * NZ, blank, 0)

    def arrive(i, step):
        row = NY - 1 - i
        for way in range(2):
            @pl.when((step < half) | (way == last_way(row)))
            def _():
                z_copy(way, row, step).wait_recv()
                pass_on(way, row, step)

    def first_step(i, _):
        arrive(i, 1)
        return 0

    lax.fori_loop(0, NY, first_step, 0)

    def wait_x(row, way, step):
        @pl.when(over_x(way, row, step) & (x > 0))
        def _():
            x_copy(row, way, step).wait_recv()

    for row in (NY - 1, NY - 2):
        wait_x(row, 0, 0)
    for way in range(2):
        @pl.when(side_goes(way))
        def _():
            side_copy(way).start()
    for copy in asked:
        copy.wait_recv()
    own_q.wait()

    key = lax.broadcasted_iota(jnp.int32, (TOK, TOK), 0)
    token = lax.broadcasted_iota(jnp.int32, (TOK, TOK), 1)

    lane = lax.broadcasted_iota(jnp.int32, (TOK, DIM), 1)
    line = lax.broadcasted_iota(jnp.int32, (TOK, DIM), 0)
    plain = jnp.where(lane == 1, 1.0, 0.0)

    def early_keys(at, b):
        there = kv[at, 2 * TOK:, :].astype(jnp.float32)
        less = jnp.where(there < first[b, 0:1, :], 1.0, 0.0)
        count = jnp.sum(jnp.sum(less, axis=0, keepdims=True), axis=1, keepdims=True).astype(jnp.int32)
        extra = jnp.where((lane == 0) & (line < count), NEG, plain).astype(jnp.bfloat16)
        return jnp.concatenate([kv[at, :TOK, :], extra], axis=1)

    def own_keys(at):
        return jnp.concatenate([kv[at, :TOK, :], jnp.zeros((TOK, DIM), jnp.bfloat16)], axis=1)

    def turned_values(slots):
        vt = jnp.concatenate([kv[at, lo:lo + DIM, :] for at in slots for lo in (TOK, TOK + DIM)], axis=1)
        return jnp.concatenate([vt, jnp.ones((16, vt.shape[1]), jnp.bfloat16)], axis=0)

    def chains(jobs):
        todo = [(b, slice(g * WIDE, (g + 1) * WIDE), keys, vt, bias, going)
                for b, keys, vt, bias, going in jobs for g in range(LANES // WIDE)]
        count = len(todo)

        def scores_of(i, n):
            b, cols, keys, _, bias, _ = todo[i]
            size = keys.shape[0] // PIECES
            s = jnp.dot(keys[n * size:(n + 1) * size], qe[b, :, cols], preferred_element_type=jnp.float32)
            if bias is not None and n == 0:
                s = jnp.concatenate([s[:TOK] + bias, s[TOK:]], axis=0)
            return s, jnp.max(s, axis=0, keepdims=True)

        def weigh(i, n, s, shift):
            return jnp.exp2(s * SCALE - shift).astype(jnp.bfloat16)

        def values_of(i, n, w, o):
            vt = todo[i][3]
            size = vt.shape[1] // PIECES
            more = jnp.dot(vt[:, n * size:(n + 1) * size], w, preferred_element_type=jnp.float32)
            return more if o is None else o + more

        ahead = [scores_of(0, n) for n in range(PIECES)]
        late = None
        for i, (b, cols, keys, vt, bias, going) in enumerate(todo):
            held, ahead = ahead, []
            new = held[0][1]
            for _, top in held[1:]:
                new = jnp.maximum(new, top)
            fade = None
            if going:
                old = peak[b, 0:1, cols]
                new = jnp.maximum(old, new)
                fade = jnp.exp2((old - new) * SCALE)
            peak[b, 0:1, cols] = new
            shift = new * SCALE
            o = None
            for n in range(PIECES):
                if i + 1 < count:
                    ahead.append(scores_of(i + 1, n))
                w = weigh(i, n, held[n][0], shift)
                if late is not None:
                    late()
                    late = None
                if n + 1 < PIECES:
                    o = values_of(i, n, w, o)

            def late(i=i, w=w, o=o, b=b, cols=cols, fade=fade):
                total = values_of(i, PIECES - 1, w, o)
                acc[b, :, cols] = total if fade is None else acc[b, :, cols] * fade + total
        late()

    def own_work(j, _):
        jobs = []
        for i in (1, 0):
            b = NY - 2 - 2 * j + i
            at = slot(b, 0)
            own = kv[at, 2 * TOK:, :].astype(jnp.float32)
            row = jnp.concatenate([own[0:1], own[1:2]], axis=1)
            rows = jnp.broadcast_to(row, (TOK, TOK))
            begin = row[:, 0:1]
            first[b] = jnp.broadcast_to(begin, (8, 128))
            rest = jnp.concatenate([jnp.where(row == begin, 0.0, NEG)] * GROUP, axis=1)
            which = lax.broadcasted_iota(jnp.int32, (DIM, LANES), 0)
            qe[b, DIM:, :] = jnp.where(which == 0, 1.0, jnp.where(which == 1, rest, 0.0)).astype(jnp.bfloat16)
            bias = jnp.concatenate([jnp.where((rows == rows.T) & (key <= token), 0.0, NEG)] * (WIDE // TOK), axis=1)
            early = [slot(b - 1, 0), slot(b - 2, 0)]
            keys = jnp.concatenate([own_keys(at)] + [early_keys(one, b) for one in early], axis=0)
            jobs.append((b, keys, turned_values([at] + early), bias, False))
        chains(jobs)
        return 0

    lax.fori_loop(0, NY // 2, own_work, 0)

    def pair_work(pair, ways, step):
        jobs = []
        for i in (1, 0):
            b = 2 * pair + i
            slots = []
            for way in ways:
                shift = shift_of(way, step)
                there = lax.rem(z + shift + NZ, NZ)
                slots += [slot(b - 1, shift), slot(jnp.where(there < z, b, b - 2), shift)]
            keys = jnp.concatenate([early_keys(at, b) for at in slots], axis=0)
            jobs.append((b, keys, turned_values(slots), None, True))
        chains(jobs)

    def later_step(step, _):
        def catch_up(j, _):
            @pl.when(step < half - 1)
            def _():
                arrive(2 * j, step + 1)
                arrive(2 * j + 1, step + 1)

            @pl.when(j == 1)
            def _():
                for way in range(2):
                    for row in (NY - 1, NY - 2):
                        wait_x(row, way, step)

                    @pl.when((step == 1) & side_comes(way))
                    def _():
                        side_copy(way).wait_recv()
            pair_work(1 - j, (0, 1), step)
            return 0

        lax.fori_loop(0, 2, catch_up, 0)
        return 0

    lax.fori_loop(1, half, later_step, 0)

    def last_step(i, _):
        arrive(i, half)
        return 0

    lax.fori_loop(0, NY, last_step, 0)

    rows = TOK // 2
    wide = GROUP * DIM
    cols = out_ref.at[:, pl.ds(pl.multiple_of((core * NY + y) * wide, wide), wide)]

    def part(b, c):
        return o_buf.at[b, pl.ds(pl.multiple_of(c * rows, rows), rows)]

    def over(b):
        return remote(part(b, 1 - core), cols, o_send.at[b, 1], o_recv.at[y, 1], (index_of(x, b, z), 1 - core))

    def along(b):
        return remote(part(b, core), cols, o_send.at[b, 0], o_recv.at[y, 0], (index_of(x, b, z), core))

    def stay(b):
        return pltpu.make_async_copy(part(b, core), cols, o_recv.at[y, 0])

    def send_back(b):
        mixed = (acc[b, :DIM, :] * (1.0 / acc[b, DIM:DIM + 1, :])).astype(jnp.bfloat16)
        for g in range(GROUP):
            o_buf[b, :, g * DIM:(g + 1) * DIM] = mixed[:, g * TOK:(g + 1) * TOK].T
        over(b).start()

        @pl.when(b != y)
        def _():
            along(b).start()

        @pl.when(b == y)
        def _():
            stay(b).start()

    def finish(j, _):
        @pl.when(j == 1)
        def _():
            for row in (NY - 1, NY - 2):
                wait_x(row, last_way(row), half)
        pair_work(1 - j, (0,), half)
        for i in (1, 0):
            send_back(2 * (1 - j) + i)
        return 0

    lax.fori_loop(0, 2, finish, 0)

    for copy in sent + asked:
        copy.wait_send()

    def z_drain(j, _):
        row, way, step = j // (2 * half), (j // half) % 2, 1 + j % half

        @pl.when((step < half) | (way == last_way(row)))
        def _():
            z_copy(way, row, step).wait_send()
        return 0

    lax.fori_loop(0, 2 * NY * half, z_drain, 0)

    def x_drain(j, _):
        row, way, step = NY - 1 - j // (2 * (half + 1)), (j // (half + 1)) % 2, j % (half + 1)
        there_is = jnp.where(step == 0, way == 0, (step < half) | (way == last_way(row)))

        @pl.when(there_is & over_x(way, row, step) & (x < NX - 1))
        def _():
            x_copy(row, way, step).wait_send()
        return 0

    lax.fori_loop(0, 2 * BACK * (half + 1), x_drain, 0)
    for way in range(2):
        @pl.when(side_goes(way))
        def _():
            side_copy(way).wait_send()
    for b in range(NY):
        over(b).wait_send()

        @pl.when(b != y)
        def _():
            along(b).wait_send()
        for e in range(2):
            pltpu.make_async_copy(part(b, core), cols, o_recv.at[b, e]).wait()


def per_device(queries, keys, values, segment_ids):
    any_spec = pl.BlockSpec(memory_space=pl.ANY)
    hbm_spec = pl.BlockSpec(memory_space=pltpu.HBM)
    dma = pltpu.SemaphoreType.DMA
    bf16, f32 = jnp.bfloat16, jnp.float32
    half = NZ // 2
    return pl.pallas_call(
        attention_kernel,
        out_shape=jax.ShapeDtypeStruct((TOK // 2, 2 * NY * GROUP * DIM), bf16),
        in_specs=[hbm_spec] * 4,
        out_specs=any_spec,
        scratch_shapes=[
            pltpu.VMEM(queries.shape, bf16), pltpu.VMEM(values.shape, bf16), pltpu.VMEM((2, 128), jnp.int32), pltpu.VMEM((16, 128), bf16),
            pltpu.VMEM((NY, 2 * DIM, TOK // 2), bf16), pltpu.VMEM((NY, DIM, LANES), bf16),
            pltpu.VMEM((SLOTS, SLOT_ROWS, DIM), bf16),
            pltpu.VMEM((NY, 2 * DIM, LANES), bf16), pltpu.VMEM((NY, DIM + 16, LANES), f32), pltpu.VMEM((NY, 8, LANES), f32),
            pltpu.VMEM((NY, 8, 128), f32), pltpu.VMEM((NY, TOK, GROUP * DIM), bf16),
            dma((3,)), dma((NY - 1, 3)), dma((NY,)), dma((NY,)), dma((NY - 1,)),
            dma((2, NY, half)), dma((2, NY, half)), dma((BACK, 2, half + 1)), dma((BACK, 2, half + 1)),
            dma((2,)), dma((2,)), pltpu.SemaphoreType.REGULAR, dma((NY, 2)), dma((NY, 2))],
        compiler_params=pltpu.CompilerParams(collective_id=0, has_side_effects=True,
                                             vmem_limit_bytes=40 * 1024 * 1024),
        name="attention",
    )(*(pltpu.with_memory_space_constraint(one, pltpu.HBM) for one in
        (queries, keys, values, segment_ids.reshape(2, 128))))


def solution(mesh):
    return jax.shard_map(
        per_device,
        mesh=mesh,
        in_specs=(P("ctx", "kvh"), P("ctx", "kvh"), P("ctx", "kvh"), P("ctx")),
        out_specs=P(("ctx", "kvh"), None),
        check_vma=False,
    )
```

```python
import jax
import jax.numpy as jnp
from jax import lax
from jax.experimental import pallas as pl
from jax.experimental.pallas import tpu as pltpu
from jax.sharding import PartitionSpec as P

NX, NY, NZ = 4, 4, 8
TOK = 256
DIM = 128
GROUP = 4
BACK = 2
ROWS = NY + BACK
SLOTS = ROWS * NZ
SLOT_ROWS = 2 * TOK + 16
LANES = GROUP * TOK
WIDE = LANES
PIECES = 2
NEG = -1e30
FAR_ID = 512.0
SCALE = 1.4426950408889634 * DIM ** -0.5


def place():
    me = lax.axis_index("ctx")
    return me, me // (NY * NZ), (me // NZ) % NY, me % NZ


def index_of(x, y, z):
    return (x * NY + y) * NZ + z


def remote(src, dst, send, recv, device):
    return pltpu.make_async_remote_copy(src_ref=src, dst_ref=dst, send_sem=send, recv_sem=recv,
                                        device_id=device, device_id_type=pl.DeviceIdType.MESH)


def attention_kernel(q_ref, k_ref, v_ref, seg_ref, out_ref, q_buf, v_buf, seg_in, seg_buf, vt_buf, qt_buf,
                     kv, qe, acc, peak, first, o_buf, load_sem,
                     y_send, y_recv, q_send, q_recv, z_send, z_recv, x_send, x_recv,
                     side_send, side_recv, ready, o_send, o_recv,
                     o_box, r_send, r_recv, f_send):
    me, x, y, z = place()
    core = lax.axis_index("kvh")
    half = NZ // 2

    def dev(x_, y_, z_):
        return (index_of(x_, y_, z_), core)

    y_peers = [lax.rem(y + d, NY) for d in range(1, NY)]
    z_next, z_prev = lax.rem(z + 1, NZ), lax.rem(z + NZ - 1, NZ)
    x_next, x_prev = lax.rem(x + 1, NX), lax.rem(x + NX - 1, NX)
    barrier = pltpu.get_barrier_semaphore()
    friends = ([dev(x, p, z) for p in y_peers] + [(index_of(x, p, z), 1 - core) for p in [y] + y_peers]
               + [dev(x, y, z_next), dev(x, y, z_prev)])
    for friend in friends:
        pl.semaphore_signal(barrier, inc=1, device_id=friend, device_id_type=pl.DeviceIdType.MESH)

    @pl.when(x < NX - 1)
    def _():
        pl.semaphore_signal(barrier, inc=1, device_id=dev(x_next, y, z), device_id_type=pl.DeviceIdType.MESH)
    load_v = pltpu.make_async_copy(v_ref, v_buf, load_sem.at[0])
    load_q = pltpu.make_async_copy(q_ref, q_buf, load_sem.at[1])
    load_ids = pltpu.make_async_copy(seg_ref, seg_in, load_sem.at[2])
    load_ids.start()
    load_v.start()
    load_q.start()

    load_ids.wait()
    ids = seg_in[...].astype(jnp.float32)
    line = lax.broadcasted_iota(jnp.int32, (16, 128), 0)
    ids = jnp.where(line == 0, ids[0:1], jnp.where(line == 1, ids[1:2], FAR_ID))
    seg_buf[...] = ids.astype(jnp.bfloat16)
    def slot(row, shift):
        return (BACK + row) * NZ + lax.rem(z + shift + NZ, NZ)

    def head_cols(p):
        return pl.ds(pl.multiple_of(p * DIM, DIM), DIM)

    mine = (BACK + y) * NZ + z
    pltpu.make_async_copy(k_ref.at[:, head_cols(y)], kv.at[mine, pl.ds(0, TOK)], y_recv.at[y]).start()
    pltpu.make_async_copy(seg_buf, kv.at[mine, pl.ds(2 * TOK, 16)], y_recv.at[y]).start()
    load_v.wait()
    for p in range(NY):
        turned = v_buf[:, p * DIM:(p + 1) * DIM].T
        vt_buf[p, :DIM, :] = turned[:, :DIM]
        vt_buf[p, DIM:, :] = turned[:, DIM:]
    pltpu.make_async_copy(vt_buf.at[y], kv.at[mine, pl.ds(TOK, TOK)], y_recv.at[y]).start()
    pl.semaphore_wait(barrier, len(friends) + jnp.where(x > 0, 1, 0))

    @pl.when(x > 0)
    def _():
        pl.semaphore_signal(ready, inc=1, device_id=dev(x_prev, y, z), device_id_type=pl.DeviceIdType.MESH)

    sent = []
    for n, p in enumerate(y_peers):
        for i, (src, lo, rows) in enumerate(((k_ref.at[:, head_cols(p)], 0, TOK), (vt_buf.at[p], TOK, TOK),
                                             (seg_buf, 2 * TOK, 16))):
            copy = remote(src, kv.at[mine, pl.ds(lo, rows)], y_send.at[n, i], y_recv.at[y], dev(x, p, z))
            copy.start()
            sent.append(copy)

    up, across, down = y_peers
    up_dev, down_dev = dev(x, up, z), dev(x, down, z)

    def through(part, src, box):
        return remote(src, box, r_send.at[part - 4], r_recv.at[part - 4], down_dev if part % 2 else up_dev)

    def shift_of(way, step):
        return step * (2 * way - 1)

    def z_copy(way, row, step):
        at = kv.at[slot(row, shift_of(way, step - 1))]
        neighbour = jnp.where(way == 0, z_next, z_prev)
        return remote(at, at, z_send.at[way, row, step - 1], z_recv.at[way, row, step - 1], dev(x, y, neighbour))

    def x_copy(row, way, step):
        shift = shift_of(way, step)
        return remote(kv.at[slot(row, shift)], kv.at[slot(row - NY, shift)], x_send.at[row - NY + BACK, way, step],
                      x_recv.at[row - NY + BACK, way, step], dev(x_next, y, z))

    def last_way(row):
        return lax.rem(row + 1, 2)

    def row2_over_x(way, step):
        return (lax.rem(z + shift_of(way, step) + NZ, NZ) >= z) & (step != 1)

    def over_x(way, row, step):
        return (row == NY - 1) | ((row == NY - 2) & row2_over_x(way, step))

    def forward(way, row, step):
        @pl.when(over_x(way, row, step) & (x < NX - 1))
        def _():
            x_copy(row, way, step).start()

    def pass_on(way, row, step):
        @pl.when((step < half - 1) | ((step == half - 1) & (way == last_way(row))))
        def _():
            z_copy(way, row, step + 1).start()
        forward(way, row, step)

    def side_copy(way):
        at = kv.at[slot(-BACK, 0)]
        return remote(at, at, side_send.at[way], side_recv.at[way], dev(x, y, z_prev if way else z_next))

    def side_goes(way):
        return (x > 0) & ((z >= 1) if way else (z == NZ - 1))

    def side_comes(way):
        return (x > 0) & ((z < NZ - 1) if way else (z == 0))

    def row_of(i):
        return lax.rem(y + jnp.where(i == 0, 0, jnp.where(i == 1, 1, jnp.where(i == 2, NY - 1, 2))), NY)

    def first_sends(i, _):
        row = row_of(i)
        at = kv.at[slot(row, 0)]
        pltpu.make_async_copy(at, at, y_recv.at[row]).wait()
        z_copy(0, row, 1).start()
        z_copy(1, row, 1).start()
        return 0

    lax.fori_loop(0, NY, first_sends, 0)

    @pl.when(x < NX - 1)
    def _():
        pl.semaphore_wait(ready, 1)
    forward(0, NY - 1, 0)
    forward(0, NY - 2, 0)
    load_q.wait()
    for p in range(NY):
        for g in range(GROUP):
            h = p * GROUP + g
            qt_buf[p, :, g * TOK:(g + 1) * TOK] = q_buf[:, h * DIM:(h + 1) * DIM].T
    asked = []
    for n, p in enumerate(y_peers):
        copy = remote(qt_buf.at[p], qe.at[y, pl.ds(0, DIM)], q_send.at[n], q_recv.at[n], dev(x, p, z))
        copy.start()
        asked.append(copy)
    own_q = pltpu.make_async_copy(qt_buf.at[y], qe.at[y, pl.ds(0, DIM)], q_send.at[NY - 1])
    own_q.start()

    @pl.when(x == 0)
    def _():
        def blank(at, _):
            kv[at, :2 * TOK, :] = jnp.zeros((2 * TOK, DIM), jnp.bfloat16)
            kv[at, 2 * TOK:, :] = jnp.full((16, DIM), -1.0, jnp.bfloat16)
            return 0

        lax.fori_loop(0, BACK * NZ, blank, 0)

    def arrive(i, step):
        row = NY - 1 - i
        for way in range(2):
            @pl.when((step < half) | (way == last_way(row)))
            def _():
                z_copy(way, row, step).wait_recv()
                pass_on(way, row, step)

    def first_step(i, _):
        arrive(i, 1)
        return 0

    lax.fori_loop(0, NY, first_step, 0)

    def wait_x(row, way, step):
        @pl.when(over_x(way, row, step) & (x > 0))
        def _():
            x_copy(row, way, step).wait_recv()

    for row in (NY - 1, NY - 2):
        wait_x(row, 0, 0)
    for way in range(2):
        @pl.when(side_goes(way))
        def _():
            side_copy(way).start()
    for copy in asked:
        copy.wait_recv()
    own_q.wait()

    key = lax.broadcasted_iota(jnp.int32, (TOK, TOK), 0)
    token = lax.broadcasted_iota(jnp.int32, (TOK, TOK), 1)

    lane = lax.broadcasted_iota(jnp.int32, (TOK, DIM), 1)
    line = lax.broadcasted_iota(jnp.int32, (TOK, DIM), 0)
    plain = jnp.where(lane == 1, 1.0, 0.0)

    def early_keys(at, b):
        there = kv[at, 2 * TOK:, :].astype(jnp.float32)
        less = jnp.where(there < first[b, 0:1, :], 1.0, 0.0)
        count = jnp.sum(jnp.sum(less, axis=0, keepdims=True), axis=1, keepdims=True).astype(jnp.int32)
        extra = jnp.where((lane == 0) & (line < count), NEG, plain).astype(jnp.bfloat16)
        return jnp.concatenate([kv[at, :TOK, :], extra], axis=1)

    def own_keys(at):
        return jnp.concatenate([kv[at, :TOK, :], jnp.zeros((TOK, DIM), jnp.bfloat16)], axis=1)

    def turned_values(slots):
        vt = jnp.concatenate([kv[at, lo:lo + DIM, :] for at in slots for lo in (TOK, TOK + DIM)], axis=1)
        return jnp.concatenate([vt, jnp.ones((16, vt.shape[1]), jnp.bfloat16)], axis=0)

    def chains(jobs):
        todo = [(b, slice(g * WIDE, (g + 1) * WIDE), keys, vt, bias, going)
                for b, keys, vt, bias, going in jobs for g in range(LANES // WIDE)]
        count = len(todo)

        def scores_of(i, n):
            b, cols, keys, _, bias, _ = todo[i]
            size = keys.shape[0] // PIECES
            s = jnp.dot(keys[n * size:(n + 1) * size], qe[b, :, cols], preferred_element_type=jnp.float32)
            if bias is not None and n == 0:
                s = jnp.concatenate([s[:TOK] + bias, s[TOK:]], axis=0)
            return s, jnp.max(s, axis=0, keepdims=True)

        def weigh(i, n, s, shift):
            return jnp.exp2(s * SCALE - shift).astype(jnp.bfloat16)

        def values_of(i, n, w, o):
            vt = todo[i][3]
            size = vt.shape[1] // PIECES
            more = jnp.dot(vt[:, n * size:(n + 1) * size], w, preferred_element_type=jnp.float32)
            return more if o is None else o + more

        ahead = [scores_of(0, n) for n in range(PIECES)]
        late = None
        for i, (b, cols, keys, vt, bias, going) in enumerate(todo):
            held, ahead = ahead, []
            new = held[0][1]
            for _, top in held[1:]:
                new = jnp.maximum(new, top)
            fade = None
            if going:
                old = peak[b, 0:1, cols]
                new = jnp.maximum(old, new)
                fade = jnp.exp2((old - new) * SCALE)
            peak[b, 0:1, cols] = new
            shift = new * SCALE
            o = None
            for n in range(PIECES):
                if i + 1 < count:
                    ahead.append(scores_of(i + 1, n))
                w = weigh(i, n, held[n][0], shift)
                if late is not None:
                    late()
                    late = None
                if n + 1 < PIECES:
                    o = values_of(i, n, w, o)

            def late(i=i, w=w, o=o, b=b, cols=cols, fade=fade):
                total = values_of(i, PIECES - 1, w, o)
                acc[b, :, cols] = total if fade is None else acc[b, :, cols] * fade + total
        late()

    def own_work(j, _):
        jobs = []
        for i in (1, 0):
            b = NY - 2 - 2 * j + i
            at = slot(b, 0)
            own = kv[at, 2 * TOK:, :].astype(jnp.float32)
            row = jnp.concatenate([own[0:1], own[1:2]], axis=1)
            rows = jnp.broadcast_to(row, (TOK, TOK))
            begin = row[:, 0:1]
            first[b] = jnp.broadcast_to(begin, (8, 128))
            rest = jnp.concatenate([jnp.where(row == begin, 0.0, NEG)] * GROUP, axis=1)
            which = lax.broadcasted_iota(jnp.int32, (DIM, LANES), 0)
            qe[b, DIM:, :] = jnp.where(which == 0, 1.0, jnp.where(which == 1, rest, 0.0)).astype(jnp.bfloat16)
            bias = jnp.concatenate([jnp.where((rows == rows.T) & (key <= token), 0.0, NEG)] * (WIDE // TOK), axis=1)
            early = [slot(b - 1, 0), slot(b - 2, 0)]
            keys = jnp.concatenate([own_keys(at)] + [early_keys(one, b) for one in early], axis=0)
            jobs.append((b, keys, turned_values([at] + early), bias, False))
        chains(jobs)
        return 0

    lax.fori_loop(0, NY // 2, own_work, 0)

    def pair_work(pair, ways, step):
        jobs = []
        for i in (1, 0):
            b = 2 * pair + i
            slots = []
            for way in ways:
                shift = shift_of(way, step)
                there = lax.rem(z + shift + NZ, NZ)
                slots += [slot(b - 1, shift), slot(jnp.where(there < z, b, b - 2), shift)]
            keys = jnp.concatenate([early_keys(at, b) for at in slots], axis=0)
            jobs.append((b, keys, turned_values(slots), None, True))
        chains(jobs)

    def later_step(step, _):
        def catch_up(j, _):
            @pl.when(step < half - 1)
            def _():
                arrive(2 * j, step + 1)
                arrive(2 * j + 1, step + 1)

            @pl.when(j == 1)
            def _():
                for way in range(2):
                    for row in (NY - 1, NY - 2):
                        wait_x(row, way, step)

                    @pl.when((step == 1) & side_comes(way))
                    def _():
                        side_copy(way).wait_recv()
            pair_work(1 - j, (0, 1), step)
            return 0

        lax.fori_loop(0, 2, catch_up, 0)
        return 0

    lax.fori_loop(1, half, later_step, 0)

    def last_step(i, _):
        arrive(i, half)
        return 0

    lax.fori_loop(0, NY, last_step, 0)

    rows = TOK // 2
    wide = GROUP * DIM
    cols = out_ref.at[:, pl.ds(pl.multiple_of((core * NY + y) * wide, wide), wide)]

    def part(b, c):
        return o_buf.at[b, pl.ds(pl.multiple_of(c * rows, rows), rows)]

    def over(b):
        return remote(part(b, 1 - core), cols, o_send.at[b, 1], o_recv.at[y, 1], (index_of(x, b, z), 1 - core))

    def along(b):
        return remote(part(b, core), cols, o_send.at[b, 0], o_recv.at[y, 0], (index_of(x, b, z), core))

    def stay(b):
        return pltpu.make_async_copy(part(b, core), cols, o_recv.at[y, 0])

    def send_back(b):
        mixed = (acc[b, :DIM, :] * (1.0 / acc[b, DIM:DIM + 1, :])).astype(jnp.bfloat16)
        for g in range(GROUP):
            o_buf[b, :, g * DIM:(g + 1) * DIM] = mixed[:, g * TOK:(g + 1) * TOK].T

        @pl.when(b == across)
        def _():
            through(4, part(b, core), o_box.at[0]).start()
            through(5, part(b, 1 - core), o_box.at[1]).start()

        @pl.when(b != across)
        def _():
            over(b).start()

        @pl.when((b != across) & (b != y))
        def _():
            along(b).start()

        @pl.when(b == y)
        def _():
            stay(b).start()

    def cols_of(source):
        return out_ref.at[:, pl.ds(pl.multiple_of((core * NY + source) * wide, wide), wide)]

    def output_through(part):
        pltpu.make_async_copy(o_box.at[part - 4], o_box.at[part - 4], r_recv.at[part - 4]).wait()
        output_on(part).start()

    def output_on(part):
        if part == 4:
            return remote(o_box.at[0], cols_of(down), f_send.at[0], o_recv.at[down, 0], up_dev)
        return remote(o_box.at[1], cols_of(up), f_send.at[1], o_recv.at[up, 1], (index_of(x, down, z), 1 - core))

    early = (y == 1) | (y == 2)

    def finish(j, _):
        @pl.when(j == 1)
        def _():
            for row in (NY - 1, NY - 2):
                wait_x(row, last_way(row), half)
        pair_work(1 - j, (0,), half)
        for i in (1, 0):
            send_back(2 * (1 - j) + i)
        return 0

    lax.fori_loop(0, 2, finish, 0)

    @pl.when(early)
    def _():
        output_through(4)
        output_through(5)

    @pl.when(jnp.logical_not(early))
    def _():
        output_through(5)
        output_through(4)

    for copy in sent + asked:
        copy.wait_send()

    def z_drain(j, _):
        row, way, step = j // (2 * half), (j // half) % 2, 1 + j % half

        @pl.when((step < half) | (way == last_way(row)))
        def _():
            z_copy(way, row, step).wait_send()
        return 0

    lax.fori_loop(0, 2 * NY * half, z_drain, 0)

    def x_drain(j, _):
        row, way, step = NY - 1 - j // (2 * (half + 1)), (j // (half + 1)) % 2, j % (half + 1)
        there_is = jnp.where(step == 0, way == 0, (step < half) | (way == last_way(row)))

        @pl.when(there_is & over_x(way, row, step) & (x < NX - 1))
        def _():
            x_copy(row, way, step).wait_send()
        return 0

    lax.fori_loop(0, 2 * BACK * (half + 1), x_drain, 0)
    for way in range(2):
        @pl.when(side_goes(way))
        def _():
            side_copy(way).wait_send()
    through(4, part(across, core), o_box.at[0]).wait_send()
    through(5, part(across, 1 - core), o_box.at[1]).wait_send()
    output_on(4).wait_send()
    output_on(5).wait_send()
    for b in range(NY):
        @pl.when(b != across)
        def _():
            over(b).wait_send()

        @pl.when((b != y) & (b != across))
        def _():
            along(b).wait_send()
        for e in range(2):
            pltpu.make_async_copy(part(b, core), cols, o_recv.at[b, e]).wait()


def per_device(queries, keys, values, segment_ids):
    any_spec = pl.BlockSpec(memory_space=pl.ANY)
    hbm_spec = pl.BlockSpec(memory_space=pltpu.HBM)
    dma = pltpu.SemaphoreType.DMA
    bf16, f32 = jnp.bfloat16, jnp.float32
    half = NZ // 2
    return pl.pallas_call(
        attention_kernel,
        out_shape=jax.ShapeDtypeStruct((TOK // 2, 2 * NY * GROUP * DIM), bf16),
        in_specs=[hbm_spec] * 4,
        out_specs=any_spec,
        scratch_shapes=[
            pltpu.VMEM(queries.shape, bf16), pltpu.VMEM(values.shape, bf16), pltpu.VMEM((2, 128), jnp.int32), pltpu.VMEM((16, 128), bf16),
            pltpu.VMEM((NY, 2 * DIM, TOK // 2), bf16), pltpu.VMEM((NY, DIM, LANES), bf16),
            pltpu.VMEM((SLOTS, SLOT_ROWS, DIM), bf16),
            pltpu.VMEM((NY, 2 * DIM, LANES), bf16), pltpu.VMEM((NY, DIM + 16, LANES), f32), pltpu.VMEM((NY, 8, LANES), f32),
            pltpu.VMEM((NY, 8, 128), f32), pltpu.VMEM((NY, TOK, GROUP * DIM), bf16),
            dma((3,)), dma((NY - 1, 3)), dma((NY,)), dma((NY,)), dma((NY - 1,)),
            dma((2, NY, half)), dma((2, NY, half)), dma((BACK, 2, half + 1)), dma((BACK, 2, half + 1)),
            dma((2,)), dma((2,)), pltpu.SemaphoreType.REGULAR, dma((NY, 2)), dma((NY, 2)),
            pltpu.VMEM((2, TOK // 2, GROUP * DIM), bf16), dma((2,)), dma((2,)), dma((2,))],
        compiler_params=pltpu.CompilerParams(collective_id=0, has_side_effects=True,
                                             vmem_limit_bytes=40 * 1024 * 1024),
        name="attention",
    )(*(pltpu.with_memory_space_constraint(one, pltpu.HBM) for one in
        (queries, keys, values, segment_ids.reshape(2, 128))))


def solution(mesh):
    return jax.shard_map(
        per_device,
        mesh=mesh,
        in_specs=(P("ctx", "kvh"), P("ctx", "kvh"), P("ctx", "kvh"), P("ctx")),
        out_specs=P(("ctx", "kvh"), None),
        check_vma=False,
    )
```
